128 devices in a mesh: dom: 8 (over y, core), cls: 16 (over x, z).
Axes of the slice: x: 4, y: 4, z: 4, core: 2. Of those that a mesh axis runs over, the one named last changes fastest.
Arguments:
- particles: bfloat16 [6144, 64, 288], P(('dom', 'cls')), may hold values from -6 to 6
- references: bfloat16 [400, 64, 288], P('cls'), may hold values from -6 to 6
- class_block: int32 [6144, 1], P(('dom', 'cls')), may hold values from 0 to 15; in each aligned block of 48 rows (0 to 47, 48 to 95, ...) at most 6 rows name the same one
- class_local: int32 [6144], P(('dom', 'cls')), may hold values from 0 to 24
- rotation: int32 [6144], P(('dom', 'cls')), may hold values from 0 to 35
- shifts: int32 [6144, 2], P(('dom', 'cls')), may hold values from -5 to 5
- defocus: int32 [6144], P(('dom', 'cls')), may hold values from 0 to 15
Outputs:
- best_score: float32 [6144], P(('dom', 'cls'))
- class_average: float32 [400, 64, 288], P('cls', 'dom')
The draws below stay inside these ranges and needn't reach their ends.
Inputs may be any that keep to these rules, and one draw needn't show every extreme that they name: `class_block`: in the rows of one device no class block is named more than 6 times, and some class block is named exactly 6 times by some device.
All inputs are finite; a program needn't handle non-finite values.
Results may differ from the reference program's by a relative error of at most 0.0045.
Values may be sent and summed in bfloat16 or wider, within the bound.
No kernel may reach another device: no remote copies, remote signals or barrier semaphores. Data moves between devices by JAX's collectives and lax.ppermute only.
A program may use at most 128 MiB of HBM per device.

```python
import math
import jax
import jax.numpy as jnp
import numpy as np
from jax import lax

CYCLES = 64
ANG = 144
ROT = 36
BOX = 128
NBINS = 16
SHIFT = 5
CLS_DEV = 25
P_DEV = 48
OWNERS = 16
CLASSES = 400
CAP = 6
PARTICLES = 6144


def touch_ends(drawn, rng, low, high):
    longest = drawn.shape.index(max(drawn.shape))
    spots = []
    for shift in (0, 1):
        where = [jax.random.randint(jax.random.fold_in(rng, axis), (), 0, length) for axis, length in enumerate(drawn.shape)]
        where[longest] = (where[longest] + shift) % drawn.shape[longest]
        spots.append(tuple(where))
    return drawn.at[spots[0]].set(low).at[spots[1]].set(high)


def steps_of(own_key, extent, cuts, low, top_value):
    gain, own = 1.0, jax.random.fold_in(own_key, 6)
    for dim, parts in cuts:
        heights = jnp.exp(jax.random.uniform(jax.random.fold_in(own, dim), (parts,), jnp.float32, low / len(cuts), top_value / len(cuts)))
        gain = gain * jnp.repeat(heights, extent[dim] // parts).reshape([-1 if axis == dim else 1 for axis in range(len(extent))])
    return gain


def shared_out(stream_key, own, number, rows, number_of, top, most, skew):
    order = jax.random.permutation(stream_key, number_of)
    crowded, usual = load_shares(number_of, rows * top, most, skew, True), load_shares(number_of, rows * top, most, skew, False)
    places = jnp.arange(number_of)

    def named(lengths, turn):
        used = int((lengths > 0).sum())
        fixed = max(1, used // 4)
        passed = fixed + (places - fixed + turn * (used - fixed)) % max(1, number_of - fixed)
        return jnp.zeros((number_of,), jnp.int32).at[order[jnp.where(places < fixed, places, passed)]].set(jnp.asarray(lengths, jnp.int32))

    lengths = jnp.where(number % 4 == 0, named(crowded, number // 4), named(usual, number - number // 4 - 1))
    mixed = jax.random.permutation(jax.random.fold_in(own, 3), number_of)
    donor, sink = mixed[0:number_of // 2 * 2:2], mixed[1:number_of // 2 * 2:2]
    margin = jnp.minimum(lengths[donor] - 1, most - lengths[sink]) // 2
    margin = jnp.where((donor == order[0]) | (sink == order[0]) | (lengths[sink] == 0), 0, jnp.maximum(margin, 0))
    passed = jax.random.randint(jax.random.fold_in(own, 4), (number_of // 2,), 0, 1 << 20) % (margin + 1)
    lengths = lengths.at[donor].add(-passed).at[sink].add(passed)
    members = jnp.searchsorted(jnp.cumsum(lengths), jnp.arange(rows * top), side="right").astype(jnp.int32)
    grid = members.reshape(top, rows).T
    grid = grid[jax.random.permutation(jax.random.fold_in(own, 1), rows)]
    turn = jax.random.randint(jax.random.fold_in(own, 2), (rows, 1), 0, top)
    return jnp.take_along_axis(grid, (jnp.arange(top)[None, :] + turn) % top, axis=1)


def load_shares(amount, total, most, skew, full):
    weights = [(1 << 20) // math.isqrt(rank ** skew) + 1 for rank in range(1, amount + 1)]
    largest = most if full else min(most, max(-(-total // amount), total * weights[0] // sum(weights)))
    least = 1 if total - largest >= amount - 1 else 0
    given, surplus = [largest] + [least] * (amount - 1), total - largest - least * (amount - 1)
    while surplus > 0:
        movable = [i for i in range(1, amount) if given[i] < largest] or [i for i in range(1, amount) if given[i] < most]
        pool, remaining = sum([weights[i] for i in movable]), surplus
        for i in movable:
            extra = min(most - given[i], max(1, remaining * weights[i] // pool), surplus)
            given[i] = given[i] + extra
            surplus = surplus - extra
    return np.array(given)


def normal_values(key, dims, scale, most, split=(), kind=jnp.bfloat16):
    entries = scale * jax.random.normal(key, dims, jnp.float32)
    if split:
        entries = entries * steps_of(key, dims, split, -0.22, 0.18)
    return jnp.clip(entries, -most, most).astype(kind)


def setup_inputs(seed: int = 0) -> dict:
    key_of = jax.random.split(jax.random.key(seed), 8)
    particles = normal_values(key_of[0], (PARTICLES, CYCLES, 2 * ANG), 1.0, 6.0, ((0, 128),))
    references = normal_values(key_of[1], (CLASSES, CYCLES, 2 * ANG), 1.0, 6.0, ((0, 16),))
    class_block_keys = jax.random.split(jax.random.fold_in(key_of[2], 1), PARTICLES // P_DEV)
    class_block_turns = jax.random.permutation(jax.random.fold_in(key_of[2], 3), PARTICLES // P_DEV)
    class_block = jax.vmap(lambda own, number: shared_out(jax.random.fold_in(key_of[2], 2), own, number, P_DEV, OWNERS, 1, CAP, 2))(class_block_keys, class_block_turns).reshape((PARTICLES, 1))
    class_local = touch_ends(jax.random.randint(key_of[3], (PARTICLES,), 0, CLS_DEV), jax.random.fold_in(key_of[3], 1), 0, CLS_DEV - 1).astype(jnp.int32)
    rotation = touch_ends(jax.random.randint(key_of[4], (PARTICLES,), 0, ROT), jax.random.fold_in(key_of[4], 1), 0, ROT - 1).astype(jnp.int32)
    shifts = touch_ends(jax.random.randint(key_of[5], (PARTICLES, 2), 0 - SHIFT, SHIFT + 1), jax.random.fold_in(key_of[5], 1), 0 - SHIFT, SHIFT).astype(jnp.int32)
    defocus = touch_ends(jax.random.randint(key_of[6], (PARTICLES,), 0, NBINS), jax.random.fold_in(key_of[6], 1), 0, NBINS - 1).astype(jnp.int32)
    return {"particles": particles, "references": references, "class_block": class_block, "class_local": class_local, "rotation": rotation, "shifts": shifts, "defocus": defocus}


EPSILON = 1e-06

def angle_table(angles):
    sample_index = jnp.arange(angles, dtype=jnp.int32)
    turn_count = sample_index[:, None] * sample_index[None, :] % angles
    angle_value = turn_count.astype(jnp.float32) * (2.0 * math.pi / angles)
    cosine = jnp.cos(angle_value)
    sine_part = jnp.sin(angle_value)
    upper_half = jnp.concatenate([cosine, -sine_part], axis=1)
    lower_half = jnp.concatenate([sine_part, cosine], axis=1)
    return jnp.concatenate([upper_half, lower_half], axis=0).astype(jnp.bfloat16)

def rotation_table(angles, rotations):
    rotate_step = angles // rotations
    harmonic = jnp.arange(angles, dtype=jnp.int32)
    rotate_index = jnp.arange(rotations, dtype=jnp.int32)
    turn_count = harmonic[:, None] * (rotate_step * rotate_index[None, :]) % angles
    angle_value = turn_count.astype(jnp.float32) * (2.0 * math.pi / angles)
    return jnp.stack([jnp.cos(angle_value), jnp.sin(angle_value)]) * (1.0 / angles)

def ctf_table(bins, cycle_count):
    radius = (jnp.arange(cycle_count, dtype=jnp.int32) + 1).astype(jnp.float32) / cycle_count
    defocus_level = jnp.arange(bins, dtype=jnp.int32).astype(jnp.float32) / bins
    phase = math.pi * (3.0 + 9.0 * defocus_level[:, None]) * (radius[None, :] * radius[None, :])
    return 0.995 * jnp.sin(phase) + 0.1 * jnp.cos(phase)

def ctf_rows(defocus, bins, cycle_count):
    defocus_hits = (defocus[:, None] == jnp.arange(bins, dtype=jnp.int32)[None, :]).astype(jnp.float32)
    return jnp.dot(defocus_hits, ctf_table(bins, cycle_count), precision=lax.Precision.HIGHEST)

def shift_phase(shifts, cycle_count, angles):
    angle_value = jnp.arange(angles, dtype=jnp.int32).astype(jnp.float32) * (2.0 * math.pi / angles)
    radius = jnp.arange(cycle_count, dtype=jnp.int32).astype(jnp.float32)
    shift_x = shifts[:, 0].astype(jnp.float32)
    shift_y = shifts[:, 1].astype(jnp.float32)
    along_beam = shift_x[:, None] * jnp.cos(angle_value)[None, :] + shift_y[:, None] * jnp.sin(angle_value)[None, :]
    return 2.0 * math.pi / BOX * radius[None, :, None] * along_beam[:, None, :]

def prepare(particles, rotation, shifts, defocus):
    particle_count, cycle_count, row_width = particles.shape
    angles = row_width // 2
    phase = shift_phase(shifts, cycle_count, angles)
    real_part = particles[:, :, :angles].astype(jnp.float32)
    imag_part = particles[:, :, angles:].astype(jnp.float32)
    cos_phase = jnp.cos(phase)
    sin_phase = jnp.sin(phase)
    shifted = jnp.concatenate([real_part * cos_phase - imag_part * sin_phase, real_part * sin_phase + imag_part * cos_phase], axis=2).astype(jnp.bfloat16)
    spectrum = jnp.dot(shifted.reshape(particle_count * cycle_count, row_width), angle_table(angles), preferred_element_type=jnp.float32).reshape(particle_count, cycle_count, row_width)
    contrast = ctf_rows(defocus, NBINS, cycle_count)
    weighted = (contrast[:, :, None] * spectrum).astype(jnp.bfloat16)
    rotate_step = angles // ROT
    harmonic = jnp.arange(angles, dtype=jnp.int32)
    turn_count = harmonic[None, :] * (rotate_step * rotation[:, None]) % angles
    angle_value = turn_count.astype(jnp.float32) * (2.0 * math.pi / angles)
    cos_rot = jnp.cos(angle_value)[:, None, :]
    sin_rot = jnp.sin(angle_value)[:, None, :]
    spec_real = spectrum[:, :, :angles]
    spec_imag = spectrum[:, :, angles:]
    turned = jnp.concatenate([spec_real * cos_rot - spec_imag * sin_rot, spec_real * sin_rot + spec_imag * cos_rot], axis=2)
    unrotated = (contrast[:, :, None] * turned).astype(jnp.bfloat16)
    return (contrast, weighted, unrotated)

def block_scores(weighted, contrast, harmonics, rotate_table):
    particle_count, cycle_count, row_width = weighted.shape
    angles = row_width // 2
    class_count = harmonics.shape[0]
    stacked = jnp.concatenate([weighted[:, :, :angles], weighted[:, :, angles:]], axis=1)
    harm_real = harmonics[:, :, :angles]
    harm_imag = harmonics[:, :, angles:]
    paired = jnp.concatenate([jnp.concatenate([harm_real, harm_imag], axis=1), jnp.concatenate([harm_imag, -harm_real], axis=1)], axis=0)
    folded = jnp.einsum('pjm,njm->pnm', stacked.astype(jnp.float32), paired.astype(jnp.float32), precision=lax.Precision.HIGHEST)
    correlation = jnp.einsum('pcnm,cmr->pnr', folded.reshape(particle_count, 2, class_count, angles), rotate_table, precision=lax.Precision.HIGHEST)
    real_wide = harm_real.astype(jnp.float32)
    imag_wide = harm_imag.astype(jnp.float32)
    energy = lax.optimization_barrier(jnp.sum(real_wide * real_wide + imag_wide * imag_wide, axis=2))
    ref_power = jnp.dot(contrast * contrast, energy.T, precision=lax.Precision.HIGHEST) / angles
    scores = correlation / jnp.sqrt(ref_power + EPSILON)[:, :, None]
    return lax.optimization_barrier(jnp.max(scores, axis=(1, 2)))

def reference(particles, references, class_block, class_local, rotation, shifts, defocus):
    particle_total, cycle_count, row_width = particles.shape
    angles = row_width // 2
    harmonics = jnp.dot(references.reshape(CLASSES * cycle_count, row_width), angle_table(angles), preferred_element_type=jnp.float32).reshape(CLASSES, cycle_count, row_width).astype(jnp.bfloat16)
    rotate_table = rotation_table(angles, ROT)
    class_ids = class_block[:, 0] * CLS_DEV + class_local
    blocks = particle_total // P_DEV

    def one_block(running, block_index):
        numerator, denominator = running
        first_row = block_index * P_DEV

        def take_rows(source):
            return lax.dynamic_slice_in_dim(source, first_row, P_DEV, 0)
        contrast, weighted, unrotated = prepare(take_rows(particles), take_rows(rotation), take_rows(shifts), take_rows(defocus))

        def per_class(best_score, class_index):
            harm_block = lax.dynamic_slice_in_dim(harmonics, class_index * CLS_DEV, CLS_DEV, 0)
            return (jnp.maximum(best_score, block_scores(weighted, contrast, harm_block, rotate_table)), None)
        best_score, ignored = lax.scan(per_class, jnp.full((P_DEV,), -1e+30, jnp.float32), jnp.arange(CLASSES // CLS_DEV, dtype=jnp.int32))
        block_ids = take_rows(class_ids)
        numerator = numerator + jax.ops.segment_sum(unrotated.astype(jnp.float32), block_ids, num_segments=CLASSES)
        denominator = denominator + jax.ops.segment_sum(contrast * contrast, block_ids, num_segments=CLASSES)
        return ((numerator, denominator), best_score)
    start_sums = (jnp.zeros((CLASSES, cycle_count, row_width), jnp.float32), jnp.zeros((CLASSES, cycle_count), jnp.float32))
    (numerator, denominator), best_score = lax.scan(one_block, start_sums, jnp.arange(blocks, dtype=jnp.int32))
    class_average = numerator / (denominator[:, :, None] + 1.0)
    return (best_score.reshape(particle_total), class_average)
```

```python
import math

import jax
import jax.numpy as jnp
import ml_dtypes
import numpy as np
from jax import lax
from jax.experimental import pallas as pl
from jax.experimental.pallas import tpu as pltpu
from jax.sharding import PartitionSpec as P

ROT = 36
BOX = 128
NBINS = 16
EPSILON = 1e-06
CYC = 64
ANG = 144
ROW = 2 * ANG
SHIFT = 5
PD = 48
KD = 25
OWN = 16
DOM = 8
BAND = CYC // DOM
UNITS = 18
HALF = UNITS // 2
MH = HALF * 8
HEAD = 192
NORM0 = 96
HROWS = HEAD + MH * 24
CHUNKS = 19
UROWS = CHUNKS * PD
SROWS = 480
KPAD = 512
F32 = jnp.float32
BF16 = jnp.bfloat16
VMEM_BYTES = 50 * 1024 * 1024
NT = (((1,), (1,)), ((), ()))


def unit_harmonics():
    rows = []
    for unit in range(UNITS):
        plus, minus = (0, 18) if unit == 0 else (unit, ROT - unit)
        rows.append([plus + ROT * q for q in range(4)] + [minus + ROT * q for q in range(4)])
    return np.array(rows).reshape(2, MH)


def dft_rows():
    turn = np.arange(ANG)[:, None] * np.arange(ANG)[None, :] % ANG
    angle = turn.astype(np.float32) * np.float32(2.0 * math.pi / ANG)
    cosine = np.cos(angle.astype(np.float64))
    sine = np.sin(angle.astype(np.float64))
    upper = np.concatenate([cosine, -sine], axis=1)
    lower = np.concatenate([sine, cosine], axis=1)
    full = np.concatenate([upper, lower], axis=0).astype(np.float32).astype(ml_dtypes.bfloat16)
    halves = unit_harmonics()
    split = []
    for core in range(2):
        mine, other = halves[core], halves[1 - core]
        columns = np.concatenate([mine, ANG + mine, other, ANG + other])
        split.append(full[:, columns].T)
    return full, np.stack(split)


def wide_columns(full):
    order = np.concatenate([np.arange(256)] + [np.arange(256, 288)] * 4)
    swapped = np.concatenate([-full[:, ANG:], full[:, :ANG]], axis=1)
    return np.concatenate([full[:, order], swapped[:, order]], axis=1), order


def turn_rows(order):
    harmonic = order % ANG
    turn = np.arange(ROT)[:, None] * 4 * harmonic[None, :] % ANG
    angle = turn * (2.0 * math.pi / ANG)
    angle = angle.reshape(ROT, 3, 128)
    return np.cos(angle).astype(np.float32), np.sin(angle).astype(np.float32)


def ctf_values():
    radius = (np.arange(CYC) + 1) / CYC
    level = np.arange(NBINS) / NBINS
    phase = math.pi * (3.0 + 9.0 * level[:, None]) * (radius * radius)[None, :]
    return 0.995 * np.sin(phase) + 0.1 * np.cos(phase)


def shift_rows():
    angle = np.arange(ANG) * (2.0 * math.pi / ANG)
    scale = 2.0 * math.pi / BOX * np.arange(CYC)
    size = np.arange(SHIFT + 1)
    out = []
    for beam in (np.cos(angle), np.sin(angle)):
        phase = size[:, None, None] * scale[None, :, None] * beam[None, None, :]
        phase = np.concatenate([phase, phase], axis=2)
        out += [np.cos(phase), np.sin(phase)]
    return np.stack(out).astype(np.float32)


def swap_matrix():
    swap = np.zeros((ROW, ROW), np.float32)
    index = np.arange(ANG)
    swap[ANG + index, index] = -1.0
    swap[index, ANG + index] = 1.0
    return swap.astype(ml_dtypes.bfloat16)


def pair_signs():
    signs = np.zeros((2, 3, MH, 128), np.float32)
    for core in range(2):
        for row in range(MH):
            unit, place = core * HALF + row // 8, row % 8
            if unit == 0:
                signs[core, 0 if place < 4 else 1, row] = 1.0
            else:
                signs[core, 0, row] = 1.0
                flip = 1.0 if place < 4 else -1.0
                signs[core, 2, row, :64] = -flip
                signs[core, 2, row, 64:] = flip
    return signs


def whole(shape):
    return pl.BlockSpec(shape, lambda *_: (0,) * len(shape))


def merge_halves(real, imag, low):
    first = jnp.where(low, real, pltpu.roll(imag, 64, 1))
    second = jnp.where(low, pltpu.roll(real, 64, 1), imag)
    return first, second


def harmonics_kernel(core, refs, table, squares, out, scratch, energy, norms):
    scratch[0:HEAD, :] = jnp.zeros((HEAD, 128), F32)
    energy[...] = jnp.zeros_like(energy)
    low = lax.broadcasted_iota(jnp.int32, (MH, 128), 1) < 64
    rows = table[0]

    def place(klass, value):
        if klass < 24:
            scratch[pl.ds(HEAD + klass, MH, stride=24), :] = value
        else:
            scratch[0:MH, :] = value

    for group in range(7):
        start, width = (group * 256, 256) if group < 6 else (KD * CYC - 128, 128)
        full = lax.dot_general(rows, refs[start : start + width, :], NT, preferred_element_type=F32)
        kept = full.astype(BF16).astype(F32)
        total = jnp.sum(kept * kept, axis=0, keepdims=True)
        if group < 6:
            energy[group : group + 1, :] = total
        else:
            energy[group : group + 1, 0:128] = jnp.where(low[0:1], pltpu.roll(total, 64, 1), 0.0)
        for pair in range(width // 128):
            lanes = slice(pair * 128, pair * 128 + 128)
            first, second = merge_halves(full[0:MH, lanes], full[MH : 2 * MH, lanes], low)
            if group < 6:
                place(group * 4 + pair * 2, first)
                place(group * 4 + pair * 2 + 1, second)
            else:
                place(24, second)
    for sub in range(4):
        power = jnp.dot(
            energy[...], squares[sub], precision=lax.Precision.HIGHEST, preferred_element_type=F32
        )
        norms[pl.ds(sub, 8, stride=4), :] = power
    scale = (1.0 / ANG) / jnp.sqrt(norms[...] * (1.0 / ANG) + EPSILON)
    scale = jnp.where(lax.broadcasted_iota(jnp.int32, (32, 128), 1) < NBINS, scale, 0.0)
    high = scale.astype(BF16).astype(F32)
    scratch[NORM0 : NORM0 + 32, :] = high + pltpu.roll(scale - high, NBINS, 1)
    out[...] = scratch[...].astype(BF16)


def own_harmonics(core, references, table):
    squares = np.zeros((4, 256, 128), np.float32)
    ctf = ctf_values()
    for sub in range(4):
        squares[sub, 64 * sub : 64 * sub + 64, :NBINS] = (ctf * ctf).T
    return pl.pallas_call(
        harmonics_kernel,
        grid_spec=pltpu.PrefetchScalarGridSpec(
            num_scalar_prefetch=1,
            grid=(1,),
            in_specs=[
                whole((KD * CYC, ROW)),
                pl.BlockSpec((1, ROW, ROW), lambda i, core: (core[0], 0, 0)),
                whole((4, 256, 128)),
            ],
            out_specs=whole((HROWS, 128)),
            scratch_shapes=[
                pltpu.VMEM((HROWS, 128), F32),
                pltpu.VMEM((8, 256), F32),
                pltpu.VMEM((32, 128), F32),
            ],
        ),
        out_shape=jax.ShapeDtypeStruct((HROWS, 128), BF16),
        compiler_params=pltpu.CompilerParams(vmem_limit_bytes=VMEM_BYTES),
        name="harmonics",
    )(core, references.reshape(KD * CYC, ROW), table, jnp.asarray(squares))


def prepare_kernel(
    scalars,
    parts,
    table,
    wide,
    swap,
    phases,
    turn_cos,
    turn_sin,
    ctf_lanes,
    ctf_rows,
    mine,
    other,
    spread,
    weighted,
    turned,
    tails,
):
    step = pl.program_id(0)
    data = parts[...]
    crossed = jnp.dot(data, swap[...], preferred_element_type=F32)
    lane = lax.broadcasted_iota(jnp.int32, (1, 128), 1)
    shifted = []
    for sub in range(4):
        index = step * 4 + sub
        move_x = scalars[0, index]
        move_y = scalars[1, index]
        sign_x = jnp.where(move_x < 0, -1.0, 1.0)
        sign_y = jnp.where(move_y < 0, -1.0, 1.0)
        size_x = jnp.abs(move_x)
        size_y = jnp.abs(move_y)
        cos_x = phases[0, size_x]
        sin_x = phases[1, size_x] * sign_x
        cos_y = phases[2, size_y]
        sin_y = phases[3, size_y] * sign_y
        cosine = cos_x * cos_y - sin_x * sin_y
        sine = sin_x * cos_y + cos_x * sin_y
        rows = slice(sub * CYC, sub * CYC + CYC)
        moved = data[rows].astype(F32) * cosine + crossed[rows] * sine
        shifted.append(moved.astype(BF16))
    shifted = jnp.concatenate(shifted, axis=0)
    full = lax.dot_general(table[0], shifted, NT, preferred_element_type=F32)
    low = lax.broadcasted_iota(jnp.int32, (MH, 128), 1) < 64
    for pair in range(2):
        lanes = slice(pair * 128, pair * 128 + 128)
        for side in range(2):
            base = side * 2 * MH
            both = merge_halves(
                full[base : base + MH, lanes], full[base + MH : base + 2 * MH, lanes], low
            )
            for which in range(2):
                index = step * 4 + pair * 2 + which
                contrast = ctf_rows[pl.ds(scalars[2, index], 1), :]
                weighted[pl.ds(side * MH * PD + index, MH, stride=PD), :] = both[which] * contrast
    natural = jnp.dot(shifted, wide[...], preferred_element_type=F32)
    group = lax.broadcasted_iota(jnp.int32, (16, 128), 1) // 32
    for sub in range(4):
        index = step * 4 + sub
        rows = slice(sub * CYC, sub * CYC + CYC)
        rotation = scalars[3, index]
        contrast = ctf_lanes[scalars[2, index]]
        for tile in range(3):
            lanes = slice(tile * 128, tile * 128 + 128)
            cos_rot = turn_cos[rotation, tile : tile + 1, :]
            sin_rot = turn_sin[rotation, tile : tile + 1, :]
            there = slice(384 + tile * 128, 384 + tile * 128 + 128)
            value = contrast * (natural[rows, lanes] * cos_rot + natural[rows, there] * sin_rot)
            if tile < 2:
                for band in range(DOM):
                    turned[pl.ds(band * UROWS + tile * PD + index, BAND, stride=2 * PD), :] = value[
                        band * BAND : band * BAND + BAND
                    ]
            else:
                tails[...] = value
                packed = tails[pl.ds(0, 16, stride=4), :]
                for place in range(1, 4):
                    packed = jnp.where(group == place, tails[pl.ds(place, 16, stride=4), :], packed)
                tails[0:16, :] = packed
                for piece in range(2):
                    turned[pl.ds((16 + piece) * PD + index, DOM, stride=UROWS), :] = tails[
                        pl.ds(piece, DOM, stride=2), :
                    ]
        label = jnp.where(lane == scalars[2, index], 1.0, 0.0)
        label = jnp.where(lane == 16, scalars[4, index].astype(F32), label)
        label = jnp.where(lane == 17, scalars[5, index].astype(F32), label)
        turned[pl.ds(18 * PD + index, DOM, stride=UROWS), :] = jnp.broadcast_to(label, (DOM, 128))

    @pl.when(step == PD // 4 - 1)
    def _():
        mine[...] = weighted[0 : MH * PD, :].astype(BF16)
        other[...] = weighted[MH * PD :, :].astype(BF16)
        spread[...] = turned[...].astype(BF16)


def prepare(core, particles, scalars, table, full_table):
    wide, order = wide_columns(full_table)
    turn_cos, turn_sin = turn_rows(order)
    ctf = ctf_values().astype(np.float32)
    ctf_lanes = np.repeat(ctf[:, :, None], 128, axis=2)
    ctf_both = np.concatenate([ctf, ctf], axis=1)
    half_shape = jax.ShapeDtypeStruct((MH * PD, 128), BF16)

    def kernel(core, *rest):
        prepare_kernel(*rest)

    return pl.pallas_call(
        kernel,
        grid_spec=pltpu.PrefetchScalarGridSpec(
            num_scalar_prefetch=2,
            grid=(PD // 4,),
            in_specs=[
                pl.BlockSpec((4 * CYC, ROW), lambda i, core, sc: (i, 0)),
                pl.BlockSpec((1, ROW, ROW), lambda i, core, sc: (core[0], 0, 0)),
                whole((ROW, 768)),
                whole((ROW, ROW)),
                whole((4, SHIFT + 1, CYC, ROW)),
                whole((ROT, 3, 128)),
                whole((ROT, 3, 128)),
                whole((NBINS, CYC, 128)),
                whole((NBINS, 128)),
            ],
            out_specs=[
                whole((MH * PD, 128)),
                whole((MH * PD, 128)),
                whole((DOM * UROWS, 128)),
            ],
            scratch_shapes=[
                pltpu.VMEM((2 * MH * PD, 128), F32),
                pltpu.VMEM((DOM * UROWS, 128), F32),
                pltpu.VMEM((CYC, 128), F32),
            ],
        ),
        out_shape=[half_shape, half_shape, jax.ShapeDtypeStruct((DOM * UROWS, 128), BF16)],
        compiler_params=pltpu.CompilerParams(vmem_limit_bytes=VMEM_BYTES),
        name="prepare",
    )(
        core,
        scalars,
        particles.reshape(PD * CYC, ROW),
        table,
        jnp.asarray(wide),
        jnp.asarray(swap_matrix()),
        jnp.asarray(shift_rows()),
        jnp.asarray(turn_cos),
        jnp.asarray(turn_sin),
        jnp.asarray(ctf_lanes),
        jnp.asarray(ctf_both),
    )


def fold_kernel(
    core, head, main, own, far, signs, bins, kept, sent, norm, held, last, wide_rows
):
    unit = pl.program_id(0)

    @pl.when(unit == 0)
    def _():
        held[...] = jnp.zeros_like(held)
        for owner in range(OWN):
            rows = head[owner, 0:80, :].astype(F32)
            last[pl.ds(owner, MH, stride=OWN), :] = rows[0:MH]
        scales = head[:, NORM0 : NORM0 + 32, :].astype(F32)
        wide_rows[...] = scales.reshape(OWN * 32, 128)
        final = wide_rows[pl.ds(24, OWN, stride=32), :]
        table = jnp.concatenate(
            [
                scales[:, 0:24, :].reshape(OWN * 24, 128),
                final,
                jnp.zeros((KPAD - OWN * KD, 128), F32),
            ],
            axis=0,
        ).astype(BF16)
        lane = lax.broadcasted_iota(jnp.int32, (PD, 128), 1)
        hits = jnp.where((lane == bins[...]) | (lane == bins[...] + NBINS), 1.0, 0.0).astype(BF16)
        norm[...] = lax.dot_general(hits, table, NT, preferred_element_type=F32)

    parts_a, parts_b = [], []
    for place in range(8):
        row = jnp.concatenate([own[place], far[place]], axis=0).astype(F32)
        factor = signs[0, :, place : place + 1, :]
        parts_a.append((row * factor[0]).astype(BF16))
        parts_b.append((row * factor[1] + pltpu.roll(row, 64, 1) * factor[2]).astype(BF16))
    left = jnp.concatenate(
        [jnp.concatenate(parts_a, axis=1), jnp.concatenate(parts_b, axis=1)], axis=0
    )
    for pair in range(4):
        slab = main[:, pair * 48 : pair * 48 + 48, :].astype(F32)
        for side in range(2):
            place = pair * 2 + side
            lanes = slice(place * 128, place * 128 + 128)
            rows = slab[:, side * 24 : side * 24 + 24, :].reshape(OWN * 24, 128)
            held[0 : OWN * 24, lanes] = rows.astype(BF16)
            start = pl.multiple_of((unit * 8 + place) * OWN, OWN)
            held[OWN * 24 : OWN * KD, lanes] = last[pl.ds(start, OWN), :].astype(BF16)
    folded = lax.dot_general(left, held[...], NT, preferred_element_type=F32)
    kept[0] = folded[0:PD]
    sent[0] = folded[PD : 2 * PD]
    kept[1] = folded[2 * PD : 3 * PD]
    sent[1] = folded[3 * PD : 4 * PD]


def fold(core, gathered, own, far, bins):
    piece = jax.ShapeDtypeStruct((UNITS, PD, KPAD), F32)
    return pl.pallas_call(
        fold_kernel,
        grid_spec=pltpu.PrefetchScalarGridSpec(
            num_scalar_prefetch=1,
            grid=(HALF,),
            in_specs=[
                pl.BlockSpec((OWN, HEAD, 128), lambda i, core: (0, 0, 0)),
                pl.BlockSpec((OWN, HEAD, 128), lambda i, core: (0, i + 1, 0)),
                pl.BlockSpec((8, PD, 128), lambda i, core: (i, 0, 0)),
                pl.BlockSpec((8, PD, 128), lambda i, core: (i, 0, 0)),
                pl.BlockSpec((1, 3, 8, 128), lambda i, core: (core[0], 0, i, 0)),
                whole((PD, 1)),
            ],
            out_specs=[
                pl.BlockSpec((2, PD, KPAD), lambda i, core: (i, 0, 0)),
                pl.BlockSpec((2, PD, KPAD), lambda i, core: (i, 0, 0)),
                whole((PD, KPAD)),
            ],
            scratch_shapes=[
                pltpu.VMEM((KPAD, 1024), BF16),
                pltpu.VMEM((MH * OWN, 128), F32),
                pltpu.VMEM((OWN * 32, 128), F32),
            ],
        ),
        out_shape=[piece, piece, jax.ShapeDtypeStruct((PD, KPAD), F32)],
        compiler_params=pltpu.CompilerParams(vmem_limit_bytes=VMEM_BYTES),
        name="fold",
    )(
        core,
        gathered,
        gathered,
        own.reshape(MH, PD, 128),
        far.reshape(MH, PD, 128),
        jnp.asarray(pair_signs()),
        bins,
    )


def weigh(total, coefficient, value):
    if abs(coefficient) < 1e-12:
        return total
    if abs(coefficient - 1.0) < 1e-12:
        return value if total is None else total + value
    if abs(coefficient + 1.0) < 1e-12:
        return -value if total is None else total - value
    term = value * coefficient
    return term if total is None else total + term


def best_rotation(cosines, sines):
    best = None
    for parity in range(2):
        sign = 1.0 if parity == 0 else -1.0
        even = {0: cosines[0] + sign * cosines[18]}
        odd = {}
        for unit in range(1, 9):
            even[unit] = cosines[unit] + sign * cosines[18 - unit]
            odd[unit] = sines[unit] - sign * sines[18 - unit]
        even[9] = cosines[9]
        odd[9] = sines[9]
        for rotation in range(parity, 10, 2):
            sums = {}
            for name, values, wave in (("e", even, math.cos), ("o", odd, math.sin)):
                for rest in range(2):
                    total = None
                    for unit, value in values.items():
                        if unit % 2 == rest:
                            angle = math.pi * ((unit * rotation) % 36) / 18.0
                            total = weigh(total, wave(angle), value)
                    sums[name, rest] = total

            def joined(first, second, flip):
                if first is None and second is None:
                    return None
                if second is None:
                    return first
                if first is None:
                    return second
                return first - second if flip else first + second

            for flip in (False, True) if rotation < 9 else (False,):
                value = joined(sums["e", 0], sums["e", 1], flip)
                swing = joined(sums["o", 1], sums["o", 0], flip)
                if swing is not None:
                    value = value + jnp.abs(swing)
                best = value if best is None else jnp.maximum(best, value)
    return best


def score_kernel(core, kept, came, norm, out):
    def score(low, high):
        for block in range(PD // 8):
            rows = slice(block * 8, block * 8 + 8)
            best = None
            for tile in range(KPAD // 128):
                lanes = slice(tile * 128, tile * 128 + 128)
                cosines, sines = {}, {}
                for unit in range(UNITS):
                    source = low if unit < HALF else high
                    place = unit % HALF * 2
                    cosines[unit] = source[place, rows, lanes]
                    sines[unit] = source[place + 1, rows, lanes]
                cosines[18] = sines[0]
                value = best_rotation(cosines, sines) * norm[rows, lanes]
                if tile == 3:
                    lane = lax.broadcasted_iota(jnp.int32, (8, 128), 1)
                    value = jnp.where(lane < OWN * KD - 384, value, -3e38)
                best = value if best is None else jnp.maximum(best, value)
            out[rows, :] = jnp.max(best, axis=1, keepdims=True)

    @pl.when(core[0] == 0)
    def _():
        score(kept, came)

    @pl.when(core[0] == 1)
    def _():
        score(came, kept)


def scores(core, kept, came, norm):
    return pl.pallas_call(
        score_kernel,
        grid_spec=pltpu.PrefetchScalarGridSpec(
            num_scalar_prefetch=1,
            grid=(1,),
            in_specs=[whole((UNITS, PD, KPAD)), whole((UNITS, PD, KPAD)), whole((PD, KPAD))],
            out_specs=whole((PD, 1)),
        ),
        out_shape=jax.ShapeDtypeStruct((PD, 1), F32),
        compiler_params=pltpu.CompilerParams(vmem_limit_bytes=VMEM_BYTES),
        name="scores",
    )(core, kept, came, norm)


def class_sum_kernel(arrived, out, last):
    labels = arrived[:, 18 * PD : 19 * PD, :].astype(F32).reshape(DOM * PD, 128)
    block = labels[:, 16:17]
    local = labels[:, 17:18]
    row = jnp.where(local < 23.5, block * 24.0 + local, block + 384.0)
    lane = lax.broadcasted_iota(jnp.int32, (DOM * PD, KPAD), 1).astype(F32)
    hits = jnp.where(lane == row, 1.0, 0.0).T[0 : OWN * KD].astype(BF16)
    last[...] = jnp.zeros_like(last)
    for pair in range(10):
        pieces = [2 * pair, 2 * pair + 1] if pair < 9 else [18]
        right = jnp.concatenate(
            [arrived[:, c * PD : c * PD + PD, :].reshape(DOM * PD, 128) for c in pieces], axis=1
        )
        total = jnp.dot(hits, right, preferred_element_type=F32)
        sums = [total[:, i * 128 : i * 128 + 128] for i in range(len(pieces))]
        for place, value in zip(pieces, sums):
            last[pl.ds(24 + place, OWN, stride=48), :] = value[OWN * 24 :]
        if pair < 9:
            both = jnp.concatenate(
                [value[0 : OWN * 24].reshape(OWN, 24, 128) for value in sums], axis=1
            )
            out[:, pair * 48 : pair * 48 + 48, :] = both.astype(BF16)
        else:
            for owner in range(OWN):
                last[owner * 48 : owner * 48 + 24, :] = sums[0][owner * 24 : owner * 24 + 24]
    out[:, 432:480, :] = last[...].reshape(OWN, 48, 128).astype(BF16)


def class_sums(arrived):
    return pl.pallas_call(
        class_sum_kernel,
        in_specs=[pl.BlockSpec(memory_space=pltpu.VMEM)],
        out_specs=pl.BlockSpec(memory_space=pltpu.VMEM),
        scratch_shapes=[pltpu.VMEM((OWN * 48, 128), F32)],
        out_shape=jax.ShapeDtypeStruct((OWN, SROWS, 128), BF16),
        compiler_params=pltpu.CompilerParams(vmem_limit_bytes=VMEM_BYTES),
        name="class_sums",
    )(arrived)


def average_kernel(dom, arrived, squares, out, left, middle, right):
    total = arrived[0].astype(F32)
    for source in range(1, OWN):
        total = total + arrived[source].astype(F32)
    counts = jnp.concatenate([total[432:456], total[472:480]], axis=0)
    below = jnp.dot(counts, squares[0], precision=lax.Precision.HIGHEST, preferred_element_type=F32)
    below = below + 1.0
    for cycle in range(BAND):
        usual = below[0:24, cycle : cycle + 1]
        final = below[26:27, cycle : cycle + 1]
        for tile, target in ((0, left), (1, middle), (2, right)):
            if tile < 2:
                piece, turn = cycle * 2 + tile, 0
            else:
                piece, turn = 16 + cycle // 4, (128 - cycle % 4 * 32) % 128
            value = total[piece * 24 : piece * 24 + 24] / usual
            end = total[456 + piece : 457 + piece] / final
            if turn:
                value = pltpu.roll(value, turn, 1)
                end = pltpu.roll(end, turn, 1)
            target[pl.ds(cycle, 24, stride=BAND), :] = value
            target[24 * BAND + cycle : 24 * BAND + cycle + 1, :] = end
    out[:, 0:128] = left[...]
    out[:, 128:256] = middle[...]
    out[:, 256:288] = right[:, 0:32]


def averages(dom, arrived):
    ctf = ctf_values()
    squares = np.zeros((DOM, 128, 128), np.float32)
    for band in range(DOM):
        squares[band, :NBINS, :BAND] = (ctf * ctf)[:, band * BAND : band * BAND + BAND]
    return pl.pallas_call(
        average_kernel,
        grid_spec=pltpu.PrefetchScalarGridSpec(
            num_scalar_prefetch=1,
            grid=(1,),
            in_specs=[
                whole((OWN, SROWS, 128)),
                pl.BlockSpec((1, 128, 128), lambda i, dom: (dom[0], 0, 0)),
            ],
            out_specs=whole((KD * BAND, ROW)),
            scratch_shapes=[pltpu.VMEM((KD * BAND, 128), F32)] * 3,
        ),
        out_shape=jax.ShapeDtypeStruct((KD * BAND, ROW), F32),
        compiler_params=pltpu.CompilerParams(vmem_limit_bytes=VMEM_BYTES),
        name="averages",
    )(dom, arrived, jnp.asarray(squares))


def on_device(particles, references, class_block, class_local, rotation, shifts, defocus):
    dom = lax.axis_index("dom").astype(jnp.int32).reshape(1)
    core = dom % 2
    full_table, split_table = dft_rows()
    table = jnp.asarray(split_table)
    gathered = lax.all_gather(own_harmonics(core, references, table), "cls", axis=0, tiled=False)
    scalars = jnp.stack(
        [shifts[:, 0], shifts[:, 1], defocus, rotation, class_block[:, 0], class_local], axis=0
    )
    own, other, spread = prepare(core, particles, scalars, table, full_table)
    swap = [(i, i ^ 1) for i in range(DOM)]
    far = lax.ppermute(other, "dom", swap)
    arrived = lax.all_to_all(spread.reshape(DOM, UROWS, 128), "dom", 0, 0, tiled=True)
    sums = lax.all_to_all(class_sums(arrived), "cls", 0, 0, tiled=True)
    class_average = averages(dom, sums).reshape(KD, BAND, ROW)
    kept, sent, norm = fold(core, gathered, own, far, defocus.reshape(PD, 1))
    came = lax.ppermute(sent, "dom", swap)
    best_score = scores(core, kept, came, norm).reshape(PD)
    return (best_score, class_average)


def solution(mesh):
    placed = (
        P(("dom", "cls"), None, None),
        P("cls", None, None),
        P(("dom", "cls"), None),
        P(("dom", "cls")),
        P(("dom", "cls")),
        P(("dom", "cls"), None),
        P(("dom", "cls")),
    )
    return jax.shard_map(
        on_device,
        mesh=mesh,
        in_specs=placed,
        out_specs=(P(("dom", "cls")), P("cls", "dom", None)),
        check_vma=False,
    )
```

```python
import math

import jax
import jax.numpy as jnp
import ml_dtypes
import numpy as np
from jax import lax
from jax.experimental import pallas as pl
from jax.experimental.pallas import tpu as pltpu
from jax.sharding import PartitionSpec as P

ROT = 36
BOX = 128
NBINS = 16
EPSILON = 1e-06
CYC = 64
ANG = 144
ROW = 2 * ANG
SHIFT = 5
PD = 48
KD = 25
OWN = 16
DOM = 8
BAND = CYC // DOM
UNITS = 18
HALF = UNITS // 2
MH = HALF * 8
HEAD = 192
NORM0 = 96
HROWS = HEAD + MH * 24
CHUNKS = 19
UROWS = CHUNKS * PD
SROWS = 480
KPAD = 512
F32 = jnp.float32
BF16 = jnp.bfloat16
VMEM_BYTES = 50 * 1024 * 1024
NT = (((1,), (1,)), ((), ()))


def unit_harmonics():
    rows = []
    for unit in range(UNITS):
        plus, minus = (0, 18) if unit == 0 else (unit, ROT - unit)
        rows.append([plus + ROT * q for q in range(4)] + [minus + ROT * q for q in range(4)])
    return np.array(rows).reshape(2, MH)


def dft_rows():
    turn = np.arange(ANG)[:, None] * np.arange(ANG)[None, :] % ANG
    angle = turn.astype(np.float32) * np.float32(2.0 * math.pi / ANG)
    cosine = np.cos(angle.astype(np.float64))
    sine = np.sin(angle.astype(np.float64))
    upper = np.concatenate([cosine, -sine], axis=1)
    lower = np.concatenate([sine, cosine], axis=1)
    full = np.concatenate([upper, lower], axis=0).astype(np.float32).astype(ml_dtypes.bfloat16)
    halves = unit_harmonics()
    split = []
    for core in range(2):
        mine, other = halves[core], halves[1 - core]
        columns = np.concatenate([mine, ANG + mine, other, ANG + other])
        split.append(full[:, columns].T)
    return full, np.stack(split)


def wide_columns(full):
    order = np.concatenate([np.arange(256)] + [np.arange(256, 288)] * 4)
    swapped = np.concatenate([-full[:, ANG:], full[:, :ANG]], axis=1)
    return np.concatenate([full[:, order], swapped[:, order]], axis=1), order


def turn_rows(order):
    harmonic = order % ANG
    turn = np.arange(ROT)[:, None] * 4 * harmonic[None, :] % ANG
    angle = turn * (2.0 * math.pi / ANG)
    angle = angle.reshape(ROT, 3, 128)
    return np.cos(angle).astype(np.float32), np.sin(angle).astype(np.float32)


def ctf_values():
    radius = (np.arange(CYC) + 1) / CYC
    level = np.arange(NBINS) / NBINS
    phase = math.pi * (3.0 + 9.0 * level[:, None]) * (radius * radius)[None, :]
    return 0.995 * np.sin(phase) + 0.1 * np.cos(phase)


def shift_rows():
    angle = np.arange(ANG) * (2.0 * math.pi / ANG)
    scale = 2.0 * math.pi / BOX * np.arange(CYC)
    size = np.arange(SHIFT + 1)
    out = []
    for beam in (np.cos(angle), np.sin(angle)):
        phase = size[:, None, None] * scale[None, :, None] * beam[None, None, :]
        phase = np.concatenate([phase, phase], axis=2)
        out += [np.cos(phase), np.sin(phase)]
    return np.stack(out).astype(np.float32)


def swap_matrix():
    swap = np.zeros((ROW, ROW), np.float32)
    index = np.arange(ANG)
    swap[ANG + index, index] = -1.0
    swap[index, ANG + index] = 1.0
    return swap.astype(ml_dtypes.bfloat16)


def pair_signs():
    signs = np.zeros((2, 3, MH, 128), np.float32)
    for core in range(2):
        for row in range(MH):
            unit, place = core * HALF + row // 8, row % 8
            if unit == 0:
                signs[core, 0 if place < 4 else 1, row] = 1.0
            else:
                signs[core, 0, row] = 1.0
                flip = 1.0 if place < 4 else -1.0
                signs[core, 2, row, :64] = -flip
                signs[core, 2, row, 64:] = flip
    return signs


def whole(shape):
    return pl.BlockSpec(shape, lambda *_: (0,) * len(shape))


def merge_halves(real, imag, low):
    first = jnp.where(low, real, pltpu.roll(imag, 64, 1))
    second = jnp.where(low, pltpu.roll(real, 64, 1), imag)
    return first, second


def harmonics_kernel(core, refs, table, squares, out, scratch, energy, norms):
    scratch[0:HEAD, :] = jnp.zeros((HEAD, 128), F32)
    energy[...] = jnp.zeros_like(energy)
    low = lax.broadcasted_iota(jnp.int32, (MH, 128), 1) < 64
    rows = table[0]

    def place(klass, value):
        if klass < 24:
            scratch[pl.ds(HEAD + klass, MH, stride=24), :] = value
        else:
            scratch[0:MH, :] = value

    for group in range(7):
        start, width = (group * 256, 256) if group < 6 else (KD * CYC - 128, 128)
        full = lax.dot_general(rows, refs[start : start + width, :], NT, preferred_element_type=F32)
        kept = full.astype(BF16).astype(F32)
        total = jnp.sum(kept * kept, axis=0, keepdims=True)
        if group < 6:
            energy[group : group + 1, :] = total
        else:
            energy[group : group + 1, 0:128] = jnp.where(low[0:1], pltpu.roll(total, 64, 1), 0.0)
        for pair in range(width // 128):
            lanes = slice(pair * 128, pair * 128 + 128)
            first, second = merge_halves(full[0:MH, lanes], full[MH : 2 * MH, lanes], low)
            if group < 6:
                place(group * 4 + pair * 2, first)
                place(group * 4 + pair * 2 + 1, second)
            else:
                place(24, second)
    for sub in range(4):
        power = jnp.dot(
            energy[...], squares[sub], precision=lax.Precision.HIGHEST, preferred_element_type=F32
        )
        norms[pl.ds(sub, 8, stride=4), :] = power
    scale = (1.0 / ANG) / jnp.sqrt(norms[...] * (1.0 / ANG) + EPSILON)
    scale = jnp.where(lax.broadcasted_iota(jnp.int32, (32, 128), 1) < NBINS, scale, 0.0)
    high = scale.astype(BF16).astype(F32)
    scratch[NORM0 : NORM0 + 32, :] = high + pltpu.roll(scale - high, NBINS, 1)
    out[...] = scratch[...].astype(BF16)


def own_harmonics(core, references, table):
    squares = np.zeros((4, 256, 128), np.float32)
    ctf = ctf_values()
    for sub in range(4):
        squares[sub, 64 * sub : 64 * sub + 64, :NBINS] = (ctf * ctf).T
    return pl.pallas_call(
        harmonics_kernel,
        grid_spec=pltpu.PrefetchScalarGridSpec(
            num_scalar_prefetch=1,
            grid=(1,),
            in_specs=[
                whole((KD * CYC, ROW)),
                pl.BlockSpec((1, ROW, ROW), lambda i, core: (core[0], 0, 0)),
                whole((4, 256, 128)),
            ],
            out_specs=whole((HROWS, 128)),
            scratch_shapes=[
                pltpu.VMEM((HROWS, 128), F32),
                pltpu.VMEM((8, 256), F32),
                pltpu.VMEM((32, 128), F32),
            ],
        ),
        out_shape=jax.ShapeDtypeStruct((HROWS, 128), BF16),
        compiler_params=pltpu.CompilerParams(vmem_limit_bytes=VMEM_BYTES),
        name="harmonics",
    )(core, references.reshape(KD * CYC, ROW), table, jnp.asarray(squares))


def prepare_kernel(
    scalars,
    parts,
    table,
    wide,
    swap,
    phases,
    turn_cos,
    turn_sin,
    ctf_lanes,
    ctf_rows,
    mine,
    other,
    spread,
    weighted,
    turned,
    tails,
):
    step = pl.program_id(0)
    data = parts[...]
    crossed = jnp.dot(data, swap[...], preferred_element_type=F32)
    lane = lax.broadcasted_iota(jnp.int32, (1, 128), 1)
    shifted = []
    for sub in range(4):
        index = step * 4 + sub
        move_x = scalars[0, index]
        move_y = scalars[1, index]
        sign_x = jnp.where(move_x < 0, -1.0, 1.0)
        sign_y = jnp.where(move_y < 0, -1.0, 1.0)
        size_x = jnp.abs(move_x)
        size_y = jnp.abs(move_y)
        cos_x = phases[0, size_x]
        sin_x = phases[1, size_x] * sign_x
        cos_y = phases[2, size_y]
        sin_y = phases[3, size_y] * sign_y
        cosine = cos_x * cos_y - sin_x * sin_y
        sine = sin_x * cos_y + cos_x * sin_y
        rows = slice(sub * CYC, sub * CYC + CYC)
        moved = data[rows].astype(F32) * cosine + crossed[rows] * sine
        shifted.append(moved.astype(BF16))
    shifted = jnp.concatenate(shifted, axis=0)
    full = lax.dot_general(table[0], shifted, NT, preferred_element_type=F32)
    low = lax.broadcasted_iota(jnp.int32, (MH, 128), 1) < 64
    for pair in range(2):
        lanes = slice(pair * 128, pair * 128 + 128)
        for side in range(2):
            base = side * 2 * MH
            both = merge_halves(
                full[base : base + MH, lanes], full[base + MH : base + 2 * MH, lanes], low
            )
            for which in range(2):
                index = step * 4 + pair * 2 + which
                contrast = ctf_rows[pl.ds(scalars[2, index], 1), :]
                weighted[pl.ds(side * MH * PD + index, MH, stride=PD), :] = both[which] * contrast
    natural = jnp.dot(shifted, wide[...], preferred_element_type=F32)
    group = lax.broadcasted_iota(jnp.int32, (16, 128), 1) // 32
    for sub in range(4):
        index = step * 4 + sub
        rows = slice(sub * CYC, sub * CYC + CYC)
        rotation = scalars[3, index]
        contrast = ctf_lanes[scalars[2, index]]
        for tile in range(3):
            lanes = slice(tile * 128, tile * 128 + 128)
            cos_rot = turn_cos[rotation, tile : tile + 1, :]
            sin_rot = turn_sin[rotation, tile : tile + 1, :]
            there = slice(384 + tile * 128, 384 + tile * 128 + 128)
            value = contrast * (natural[rows, lanes] * cos_rot + natural[rows, there] * sin_rot)
            if tile < 2:
                for band in range(DOM):
                    turned[pl.ds(band * UROWS + tile * PD + index, BAND, stride=2 * PD), :] = value[
                        band * BAND : band * BAND + BAND
                    ]
            else:
                tails[...] = value
                packed = tails[pl.ds(0, 16, stride=4), :]
                for place in range(1, 4):
                    packed = jnp.where(group == place, tails[pl.ds(place, 16, stride=4), :], packed)
                tails[0:16, :] = packed
                for piece in range(2):
                    turned[pl.ds((16 + piece) * PD + index, DOM, stride=UROWS), :] = tails[
                        pl.ds(piece, DOM, stride=2), :
                    ]
        label = jnp.where(lane == scalars[2, index], 1.0, 0.0)
        label = jnp.where(lane == 16, scalars[4, index].astype(F32), label)
        label = jnp.where(lane == 17, scalars[5, index].astype(F32), label)
        turned[pl.ds(18 * PD + index, DOM, stride=UROWS), :] = jnp.broadcast_to(label, (DOM, 128))

    @pl.when(step == PD // 4 - 1)
    def _():
        mine[...] = weighted[0 : MH * PD, :].astype(BF16)
        other[...] = weighted[MH * PD :, :].astype(BF16)
        spread[...] = turned[...].astype(BF16)


def prepare(core, particles, scalars, table, full_table):
    wide, order = wide_columns(full_table)
    turn_cos, turn_sin = turn_rows(order)
    ctf = ctf_values().astype(np.float32)
    ctf_lanes = np.repeat(ctf[:, :, None], 128, axis=2)
    ctf_both = np.concatenate([ctf, ctf], axis=1)
    half_shape = jax.ShapeDtypeStruct((MH * PD, 128), BF16)

    def kernel(core, *rest):
        prepare_kernel(*rest)

    return pl.pallas_call(
        kernel,
        grid_spec=pltpu.PrefetchScalarGridSpec(
            num_scalar_prefetch=2,
            grid=(PD // 4,),
            in_specs=[
                pl.BlockSpec((4 * CYC, ROW), lambda i, core, sc: (i, 0)),
                pl.BlockSpec((1, ROW, ROW), lambda i, core, sc: (core[0], 0, 0)),
                whole((ROW, 768)),
                whole((ROW, ROW)),
                whole((4, SHIFT + 1, CYC, ROW)),
                whole((ROT, 3, 128)),
                whole((ROT, 3, 128)),
                whole((NBINS, CYC, 128)),
                whole((NBINS, 128)),
            ],
            out_specs=[
                whole((MH * PD, 128)),
                whole((MH * PD, 128)),
                whole((DOM * UROWS, 128)),
            ],
            scratch_shapes=[
                pltpu.VMEM((2 * MH * PD, 128), F32),
                pltpu.VMEM((DOM * UROWS, 128), F32),
                pltpu.VMEM((CYC, 128), F32),
            ],
        ),
        out_shape=[half_shape, half_shape, jax.ShapeDtypeStruct((DOM * UROWS, 128), BF16)],
        compiler_params=pltpu.CompilerParams(vmem_limit_bytes=VMEM_BYTES),
        name="prepare",
    )(
        core,
        scalars,
        particles.reshape(PD * CYC, ROW),
        table,
        jnp.asarray(wide),
        jnp.asarray(swap_matrix()),
        jnp.asarray(shift_rows()),
        jnp.asarray(turn_cos),
        jnp.asarray(turn_sin),
        jnp.asarray(ctf_lanes),
        jnp.asarray(ctf_both),
    )


def fold_kernel(*refs):
    core, pieces, heads = refs[0], refs[1:11], refs[11:16]
    own, far, signs, bins, kept, sent, norm, held, last, wide_rows, scale_rows = refs[16:]
    unit = pl.program_id(0)

    def blocks(parts):
        for group in range(3):
            for place in range(4):
                yield group, place, parts[group], place
        for place in range(4):
            yield 3, place, parts[3 + place // 2], place % 2

    @pl.when(unit == 0)
    def _():
        held[...] = jnp.zeros_like(held)
        scale_rows[...] = jnp.zeros_like(scale_rows)
        for group, place, ref, row in blocks(heads):
            slot = group * 4 + place
            values = ref[row, 0:80, :].astype(F32)
            last[pl.ds(slot, MH, stride=OWN), :] = values[0:MH]
            scales = ref[row, NORM0 : NORM0 + 32, :].astype(F32)
            scale_rows[slot * 24 : slot * 24 + 24, :] = scales[0:24]
            scale_rows[OWN * 24 + slot : OWN * 24 + slot + 1, :] = scales[24:25]
        lane = lax.broadcasted_iota(jnp.int32, (PD, 128), 1)
        hits = jnp.where((lane == bins[...]) | (lane == bins[...] + NBINS), 1.0, 0.0).astype(BF16)
        table = scale_rows[...].astype(BF16)
        norm[...] = lax.dot_general(hits, table, NT, preferred_element_type=F32)

    parts_a, parts_b = [], []
    for place in range(8):
        row = jnp.concatenate([own[place], far[place]], axis=0).astype(F32)
        factor = signs[0, :, place : place + 1, :]
        parts_a.append((row * factor[0]).astype(BF16))
        parts_b.append((row * factor[1] + pltpu.roll(row, 64, 1) * factor[2]).astype(BF16))
    left = jnp.concatenate(
        [jnp.concatenate(parts_a, axis=1), jnp.concatenate(parts_b, axis=1)], axis=0
    )

    def fill(parts, first):
        by_slot = {}
        for group, place, ref, row in blocks(parts):
            by_slot[group * 4 + place if first else place * 4 + group] = (ref, row)
        for pair in range(4):
            for two in range(OWN // 2):
                slabs = []
                for slot in (2 * two, 2 * two + 1):
                    ref, row = by_slot[slot]
                    slabs.append(ref[row, pair * 48 : pair * 48 + 48, :].astype(F32))
                for side in range(2):
                    place = pair * 2 + side
                    lanes = slice(place * 128, place * 128 + 128)
                    both = jnp.concatenate(
                        [slab[side * 24 : side * 24 + 24] for slab in slabs], axis=0
                    )
                    held[two * 48 : two * 48 + 48, lanes] = both.astype(BF16)

    @pl.when(unit < 4)
    def _():
        fill(pieces[0:5], True)

    @pl.when(unit >= 4)
    def _():
        fill(pieces[5:10], False)

    for place in range(8):
        lanes = slice(place * 128, place * 128 + 128)
        start = pl.multiple_of((unit * 8 + place) * OWN, OWN)
        held[OWN * 24 : OWN * KD, lanes] = last[pl.ds(start, OWN), :].astype(BF16)
    folded = lax.dot_general(left, held[...], NT, preferred_element_type=F32)
    kept[0] = folded[0:PD]
    sent[0] = folded[PD : 2 * PD]
    kept[1] = folded[2 * PD : 3 * PD]
    sent[1] = folded[3 * PD : 4 * PD]


def fold(core, halves, own, far, bins):
    piece = jax.ShapeDtypeStruct((UNITS, PD, KPAD), F32)
    first, second = halves
    lead = [4, 4, 4, 2, 2]
    specs = [
        pl.BlockSpec((n, HEAD, 128), lambda i, core: (0, jnp.minimum(i + 1, 4), 0)) for n in lead
    ]
    specs += [
        pl.BlockSpec((n, HEAD, 128), lambda i, core: (0, jnp.maximum(i - 4, 0), 0)) for n in lead
    ]
    specs += [pl.BlockSpec((n, HEAD, 128), lambda i, core: (0, 0, 0)) for n in lead]
    return pl.pallas_call(
        fold_kernel,
        grid_spec=pltpu.PrefetchScalarGridSpec(
            num_scalar_prefetch=1,
            grid=(HALF,),
            in_specs=specs
            + [
                pl.BlockSpec((8, PD, 128), lambda i, core: (i, 0, 0)),
                pl.BlockSpec((8, PD, 128), lambda i, core: (i, 0, 0)),
                pl.BlockSpec((1, 3, 8, 128), lambda i, core: (core[0], 0, i, 0)),
                whole((PD, 1)),
            ],
            out_specs=[
                pl.BlockSpec((2, PD, KPAD), lambda i, core: (i, 0, 0)),
                pl.BlockSpec((2, PD, KPAD), lambda i, core: (i, 0, 0)),
                whole((PD, KPAD)),
            ],
            scratch_shapes=[
                pltpu.VMEM((KPAD, 1024), BF16),
                pltpu.VMEM((MH * OWN, 128), F32),
                pltpu.VMEM((OWN * 32, 128), F32),
                pltpu.VMEM((KPAD, 128), F32),
            ],
        ),
        out_shape=[piece, piece, jax.ShapeDtypeStruct((PD, KPAD), F32)],
        compiler_params=pltpu.CompilerParams(vmem_limit_bytes=VMEM_BYTES),
        name="fold",
    )(
        core,
        *first,
        *second,
        *first,
        own.reshape(MH, PD, 128),
        far.reshape(MH, PD, 128),
        jnp.asarray(pair_signs()),
        bins,
    )


def shifted_by(value, along_x, along_z):
    moves = [
        (x * 4 + z, (x + along_x) % 4 * 4 + (z + along_z) % 4) for x in range(4) for z in range(4)
    ]
    return lax.ppermute(value, "cls", moves)


def ring(value, unit_x, unit_z):
    half = value.shape[0] // 2
    before = shifted_by(value, unit_x, unit_z)
    after = shifted_by(value, -unit_x, -unit_z)
    return [
        before,
        after,
        shifted_by(before[:half], unit_x, unit_z),
        shifted_by(after[half:], -unit_x, -unit_z),
    ]


def gather_blocks(value):
    half = value.shape[0] // 2
    halves = []
    for part, (unit_x, unit_z) in ((value[:half], (1, 0)), (value[half:], (0, 1))):
        row = jnp.concatenate([part] + ring(part, unit_x, unit_z), axis=0)
        pieces = [row] + ring(row, unit_z, unit_x)
        halves.append([piece.reshape(-1, half, 128) for piece in pieces])
    return halves


def weigh(total, coefficient, value):
    if abs(coefficient) < 1e-12:
        return total
    if abs(coefficient - 1.0) < 1e-12:
        return value if total is None else total + value
    if abs(coefficient + 1.0) < 1e-12:
        return -value if total is None else total - value
    term = value * coefficient
    return term if total is None else total + term


def best_rotation(cosines, sines):
    best = None
    for parity in range(2):
        sign = 1.0 if parity == 0 else -1.0
        even = {0: cosines[0] + sign * cosines[18]}
        odd = {}
        for unit in range(1, 9):
            even[unit] = cosines[unit] + sign * cosines[18 - unit]
            odd[unit] = sines[unit] - sign * sines[18 - unit]
        even[9] = cosines[9]
        odd[9] = sines[9]
        for rotation in range(parity, 10, 2):
            sums = {}
            for name, values, wave in (("e", even, math.cos), ("o", odd, math.sin)):
                for rest in range(2):
                    total = None
                    for unit, value in values.items():
                        if unit % 2 == rest:
                            angle = math.pi * ((unit * rotation) % 36) / 18.0
                            total = weigh(total, wave(angle), value)
                    sums[name, rest] = total

            def joined(first, second, flip):
                if first is None and second is None:
                    return None
                if second is None:
                    return first
                if first is None:
                    return second
                return first - second if flip else first + second

            for flip in (False, True) if rotation < 9 else (False,):
                value = joined(sums["e", 0], sums["e", 1], flip)
                swing = joined(sums["o", 1], sums["o", 0], flip)
                if swing is not None:
                    value = value + jnp.abs(swing)
                best = value if best is None else jnp.maximum(best, value)
    return best


def score_kernel(core, kept, came, norm, out):
    def score(low, high):
        for block in range(PD // 8):
            rows = slice(block * 8, block * 8 + 8)
            best = None
            for tile in range(KPAD // 128):
                lanes = slice(tile * 128, tile * 128 + 128)
                cosines, sines = {}, {}
                for unit in range(UNITS):
                    source = low if unit < HALF else high
                    place = unit % HALF * 2
                    cosines[unit] = source[place, rows, lanes]
                    sines[unit] = source[place + 1, rows, lanes]
                cosines[18] = sines[0]
                value = best_rotation(cosines, sines) * norm[rows, lanes]
                if tile == 3:
                    lane = lax.broadcasted_iota(jnp.int32, (8, 128), 1)
                    value = jnp.where(lane < OWN * KD - 384, value, -3e38)
                best = value if best is None else jnp.maximum(best, value)
            out[rows, :] = jnp.max(best, axis=1, keepdims=True)

    @pl.when(core[0] == 0)
    def _():
        score(kept, came)

    @pl.when(core[0] == 1)
    def _():
        score(came, kept)


def scores(core, kept, came, norm):
    return pl.pallas_call(
        score_kernel,
        grid_spec=pltpu.PrefetchScalarGridSpec(
            num_scalar_prefetch=1,
            grid=(1,),
            in_specs=[whole((UNITS, PD, KPAD)), whole((UNITS, PD, KPAD)), whole((PD, KPAD))],
            out_specs=whole((PD, 1)),
        ),
        out_shape=jax.ShapeDtypeStruct((PD, 1), F32),
        compiler_params=pltpu.CompilerParams(vmem_limit_bytes=VMEM_BYTES),
        name="scores",
    )(core, kept, came, norm)


def class_sum_kernel(arrived, out, last):
    labels = arrived[:, 18 * PD : 19 * PD, :].astype(F32).reshape(DOM * PD, 128)
    block = labels[:, 16:17]
    local = labels[:, 17:18]
    row = jnp.where(local < 23.5, block * 24.0 + local, block + 384.0)
    lane = lax.broadcasted_iota(jnp.int32, (DOM * PD, KPAD), 1).astype(F32)
    hits = jnp.where(lane == row, 1.0, 0.0).T[0 : OWN * KD].astype(BF16)
    last[...] = jnp.zeros_like(last)
    for pair in range(10):
        pieces = [2 * pair, 2 * pair + 1] if pair < 9 else [18]
        right = jnp.concatenate(
            [arrived[:, c * PD : c * PD + PD, :].reshape(DOM * PD, 128) for c in pieces], axis=1
        )
        total = jnp.dot(hits, right, preferred_element_type=F32)
        sums = [total[:, i * 128 : i * 128 + 128] for i in range(len(pieces))]
        for place, value in zip(pieces, sums):
            last[pl.ds(24 + place, OWN, stride=48), :] = value[OWN * 24 :]
        if pair < 9:
            both = jnp.concatenate(
                [value[0 : OWN * 24].reshape(OWN, 24, 128) for value in sums], axis=1
            )
            out[:, pair * 48 : pair * 48 + 48, :] = both.astype(BF16)
        else:
            for owner in range(OWN):
                last[owner * 48 : owner * 48 + 24, :] = sums[0][owner * 24 : owner * 24 + 24]
    out[:, 432:480, :] = last[...].reshape(OWN, 48, 128).astype(BF16)


def class_sums(arrived):
    return pl.pallas_call(
        class_sum_kernel,
        in_specs=[pl.BlockSpec(memory_space=pltpu.VMEM)],
        out_specs=pl.BlockSpec(memory_space=pltpu.VMEM),
        scratch_shapes=[pltpu.VMEM((OWN * 48, 128), F32)],
        out_shape=jax.ShapeDtypeStruct((OWN, SROWS, 128), BF16),
        compiler_params=pltpu.CompilerParams(vmem_limit_bytes=VMEM_BYTES),
        name="class_sums",
    )(arrived)


def average_kernel(dom, arrived, squares, out, left, middle, right):
    total = arrived[0].astype(F32)
    for source in range(1, OWN):
        total = total + arrived[source].astype(F32)
    counts = jnp.concatenate([total[432:456], total[472:480]], axis=0)
    below = jnp.dot(counts, squares[0], precision=lax.Precision.HIGHEST, preferred_element_type=F32)
    below = below + 1.0
    for cycle in range(BAND):
        usual = below[0:24, cycle : cycle + 1]
        final = below[26:27, cycle : cycle + 1]
        for tile, target in ((0, left), (1, middle), (2, right)):
            if tile < 2:
                piece, turn = cycle * 2 + tile, 0
            else:
                piece, turn = 16 + cycle // 4, (128 - cycle % 4 * 32) % 128
            value = total[piece * 24 : piece * 24 + 24] / usual
            end = total[456 + piece : 457 + piece] / final
            if turn:
                value = pltpu.roll(value, turn, 1)
                end = pltpu.roll(end, turn, 1)
            target[pl.ds(cycle, 24, stride=BAND), :] = value
            target[24 * BAND + cycle : 24 * BAND + cycle + 1, :] = end
    out[:, 0:128] = left[...]
    out[:, 128:256] = middle[...]
    out[:, 256:288] = right[:, 0:32]


def averages(dom, arrived):
    ctf = ctf_values()
    squares = np.zeros((DOM, 128, 128), np.float32)
    for band in range(DOM):
        squares[band, :NBINS, :BAND] = (ctf * ctf)[:, band * BAND : band * BAND + BAND]
    return pl.pallas_call(
        average_kernel,
        grid_spec=pltpu.PrefetchScalarGridSpec(
            num_scalar_prefetch=1,
            grid=(1,),
            in_specs=[
                whole((OWN, SROWS, 128)),
                pl.BlockSpec((1, 128, 128), lambda i, dom: (dom[0], 0, 0)),
            ],
            out_specs=whole((KD * BAND, ROW)),
            scratch_shapes=[pltpu.VMEM((KD * BAND, 128), F32)] * 3,
        ),
        out_shape=jax.ShapeDtypeStruct((KD * BAND, ROW), F32),
        compiler_params=pltpu.CompilerParams(vmem_limit_bytes=VMEM_BYTES),
        name="averages",
    )(dom, arrived, jnp.asarray(squares))


def on_device(particles, references, class_block, class_local, rotation, shifts, defocus):
    dom = lax.axis_index("dom").astype(jnp.int32).reshape(1)
    core = dom % 2
    full_table, split_table = dft_rows()
    table = jnp.asarray(split_table)
    gathered = gather_blocks(own_harmonics(core, references, table))
    scalars = jnp.stack(
        [shifts[:, 0], shifts[:, 1], defocus, rotation, class_block[:, 0], class_local], axis=0
    )
    own, other, spread = prepare(core, particles, scalars, table, full_table)
    swap = [(i, i ^ 1) for i in range(DOM)]
    far = lax.ppermute(other, "dom", swap)
    arrived = lax.all_to_all(spread.reshape(DOM, UROWS, 128), "dom", 0, 0, tiled=True)
    sums = lax.all_to_all(class_sums(arrived), "cls", 0, 0, tiled=True)
    class_average = averages(dom, sums).reshape(KD, BAND, ROW)
    kept, sent, norm = fold(core, gathered, own, far, defocus.reshape(PD, 1))
    came = lax.ppermute(sent, "dom", swap)
    best_score = scores(core, kept, came, norm).reshape(PD)
    return (best_score, class_average)


def solution(mesh):
    placed = (
        P(("dom", "cls"), None, None),
        P("cls", None, None),
        P(("dom", "cls"), None),
        P(("dom", "cls")),
        P(("dom", "cls")),
        P(("dom", "cls"), None),
        P(("dom", "cls")),
    )
    return jax.shard_map(
        on_device,
        mesh=mesh,
        in_specs=placed,
        out_specs=(P(("dom", "cls")), P("cls", "dom", None)),
        check_vma=False,
    )
```

```python
import functools
import math

import jax
import jax.numpy as jnp
import ml_dtypes
import numpy as np
from jax import lax
from jax.experimental import pallas as pl
from jax.experimental.pallas import tpu as pltpu
from jax.sharding import PartitionSpec as P

ROT = 36
BOX = 128
NBINS = 16
EPSILON = 1e-06
CYC = 64
ANG = 144
ROW = 2 * ANG
SHIFT = 5
PD = 48
KD = 25
OWN = 16
DOM = 8
BAND = CYC // DOM
UNITS = 18
HALF = UNITS // 2
MH = HALF * 8
HEAD = 192
NORM0 = 96
HROWS = HEAD + MH * 24
HH = 40
MP = 2 * HH
CHUNKS = 19
UROWS = CHUNKS * PD
SROWS = 480
KPAD = 512
STEP = 16
F32 = jnp.float32
BF16 = jnp.bfloat16
VMEM_BYTES = 58 * 1024 * 1024
NT = (((1,), (1,)), ((), ()))


def unit_harmonics():
    rows = []
    for unit in range(UNITS):
        plus, minus = (0, 18) if unit == 0 else (unit, ROT - unit)
        rows.append([plus + ROT * q for q in range(4)] + [minus + ROT * q for q in range(4)])
    return np.array(rows).reshape(2, MH)


def dft_rows():
    turn = np.arange(ANG)[:, None] * np.arange(ANG)[None, :] % ANG
    angle = turn.astype(np.float32) * np.float32(2.0 * math.pi / ANG)
    cosine = np.cos(angle.astype(np.float64))
    sine = np.sin(angle.astype(np.float64))
    upper = np.concatenate([cosine, -sine], axis=1)
    lower = np.concatenate([sine, cosine], axis=1)
    full = np.concatenate([upper, lower], axis=0).astype(np.float32).astype(ml_dtypes.bfloat16)
    halves = unit_harmonics()
    split = []
    for core in range(2):
        mine, other = halves[core], halves[1 - core]
        rows = np.zeros((4 * MP, ROW), ml_dtypes.bfloat16)
        for index, columns in enumerate((mine, ANG + mine, other, ANG + other)):
            for parity in range(2):
                start = index * MP + parity * HH
                rows[start : start + MH // 2] = full[:, columns[parity::2]].T
        split.append(rows)
    return full, np.stack(split)


def wide_columns(full):
    order = np.concatenate([np.arange(256)] + [np.arange(256, 288)] * 4)
    swapped = np.concatenate([-full[:, ANG:], full[:, :ANG]], axis=1)
    return np.concatenate([full[:, order], swapped[:, order]], axis=1), order


def turn_rows(order):
    harmonic = order % ANG
    turn = np.arange(ROT)[:, None] * 4 * harmonic[None, :] % ANG
    angle = turn * (2.0 * math.pi / ANG)
    angle = angle.reshape(ROT, 3, 128)
    rest = np.zeros((ROT, 2, 128))
    return np.concatenate([np.cos(angle), np.sin(angle), rest], axis=1).astype(np.float32)


def ctf_values():
    radius = (np.arange(CYC) + 1) / CYC
    level = np.arange(NBINS) / NBINS
    phase = math.pi * (3.0 + 9.0 * level[:, None]) * (radius * radius)[None, :]
    return 0.995 * np.sin(phase) + 0.1 * np.cos(phase)


def shift_rows():
    angle = np.arange(ANG) * (2.0 * math.pi / ANG)
    scale = 2.0 * math.pi / BOX * np.concatenate([np.arange(8), 8 * np.arange(8)])
    size = np.arange(SHIFT + 1)
    out = []
    for beam in (np.cos(angle), np.sin(angle)):
        phase = size[:, None, None] * scale[None, :, None] * beam[None, None, :]
        phase = np.concatenate([phase, phase], axis=2)
        out += [np.cos(phase), np.sin(phase)]
    return np.stack(out).astype(np.float32)


def swap_matrix():
    swap = np.zeros((ROW, ROW), np.float32)
    index = np.arange(ANG)
    swap[ANG + index, index] = -1.0
    swap[index, ANG + index] = 1.0
    return swap.astype(ml_dtypes.bfloat16)


def pair_signs():
    signs = np.zeros((2, 3, MH, 128), np.float32)
    for core in range(2):
        for row in range(MH):
            unit, place = core * HALF + row // 8, row % 8
            if unit == 0:
                signs[core, 0 if place < 4 else 1, row] = 1.0
            else:
                signs[core, 0, row] = 1.0
                flip = 1.0 if place < 4 else -1.0
                signs[core, 2, row, :64] = -flip
                signs[core, 2, row, 64:] = flip
    signs = np.pad(signs.transpose(0, 2, 1, 3), ((0, 0), (0, 0), (0, 5), (0, 0)))
    return signs


def whole(shape):
    return pl.BlockSpec(shape, lambda *_: (0,) * len(shape))


def merge_halves(real, imag, low):
    first = jnp.where(low, real, pltpu.roll(imag, 64, 1))
    second = jnp.where(low, pltpu.roll(real, 64, 1), imag)
    return first, second


def harmonics_kernel(
    core, refs_any, table_any, squares_any, out, refs, table, squares, scratch, energy, norms, sems
):
    copies = [pltpu.make_async_copy(table_any.at[core[0]], table, sems.at[0])]
    for index in range(4):
        chunk = pl.ds(index * 512, 512 if index < 3 else 64)
        copies.append(
            pltpu.make_async_copy(refs_any.at[chunk, :], refs.at[chunk, :], sems.at[index + 1])
        )
    copies.append(pltpu.make_async_copy(squares_any, squares, sems.at[5]))
    for copy in copies:
        copy.start()
    scratch[0:HEAD, :] = jnp.zeros((HEAD, 128), F32)
    energy[...] = jnp.zeros_like(energy)
    low = lax.broadcasted_iota(jnp.int32, (MP, 128), 1) < 64
    copies[0].wait()
    rows = table[...]

    def place(klass, value):
        if klass == 24:
            scratch[0:MP, :] = value
            return
        for parity in range(2):
            start = HEAD + (parity * 16 + klass if klass < 16 else 16 + parity * 8 + klass)
            piece = value[parity * HH : parity * HH + MH // 2]
            scratch[pl.ds(start, MH // 2, stride=48), :] = piece

    for group in range(7):
        start, width = (group * 256, 256) if group < 6 else (KD * CYC - 128, 128)
        if group % 2 == 0:
            copies[1 + group // 2].wait()
        full = lax.dot_general(rows, refs[start : start + width, :], NT, preferred_element_type=F32)
        kept = full.astype(BF16).astype(F32)
        total = jnp.sum(kept * kept, axis=0, keepdims=True)
        if group < 6:
            energy[group : group + 1, :] = total
        else:
            energy[group : group + 1, 0:128] = jnp.where(low[0:1], pltpu.roll(total, 64, 1), 0.0)
        for pair in range(width // 128):
            lanes = slice(pair * 128, pair * 128 + 128)
            first, second = merge_halves(full[0:MP, lanes], full[MP : 2 * MP, lanes], low)
            if group < 6:
                place(group * 4 + pair * 2, first)
                place(group * 4 + pair * 2 + 1, second)
            else:
                place(24, second)
    copies[5].wait()
    for sub in range(4):
        lanes = slice(sub // 2 * 128, sub // 2 * 128 + 128)
        power = jnp.dot(
            energy[:, lanes],
            squares[sub % 2],
            precision=lax.Precision.HIGHEST,
            preferred_element_type=F32,
        )
        norms[pl.ds(sub, 8, stride=4), :] = power
    scale = (1.0 / ANG) / jnp.sqrt(norms[...] * (1.0 / ANG) + EPSILON)
    scale = jnp.where(lax.broadcasted_iota(jnp.int32, (32, 128), 1) < NBINS, scale, 0.0)
    high = scale.astype(BF16).astype(F32)
    scratch[NORM0 : NORM0 + 32, :] = high + pltpu.roll(scale - high, NBINS, 1)
    out[...] = scratch[...].astype(BF16)


def own_harmonics(core, references, table):
    squares = np.zeros((2, 128, 128), np.float32)
    ctf = ctf_values()
    for sub in range(2):
        squares[sub, 64 * sub : 64 * sub + 64, :NBINS] = (ctf * ctf).T
    return pl.pallas_call(
        harmonics_kernel,
        in_specs=[
            pl.BlockSpec(memory_space=pltpu.SMEM),
            pl.BlockSpec(memory_space=pl.ANY),
            pl.BlockSpec(memory_space=pl.ANY),
            pl.BlockSpec(memory_space=pl.ANY),
        ],
        out_specs=pl.BlockSpec(memory_space=pltpu.VMEM),
        scratch_shapes=[
            pltpu.VMEM((KD * CYC, ROW), BF16),
            pltpu.VMEM((4 * MP, ROW), BF16),
            pltpu.VMEM((2, 128, 128), F32),
            pltpu.VMEM((HROWS, 128), F32),
            pltpu.VMEM((8, 256), F32),
            pltpu.VMEM((32, 128), F32),
            pltpu.SemaphoreType.DMA((6,)),
        ],
        out_shape=jax.ShapeDtypeStruct((HROWS, 128), BF16),
        compiler_params=pltpu.CompilerParams(vmem_limit_bytes=VMEM_BYTES),
        cost_estimate=pl.CostEstimate(
            flops=4000000000, bytes_accessed=12000000, transcendentals=0
        ),
        name="harmonics",
    )(core, references.reshape(KD * CYC, ROW), table, jnp.asarray(squares))


def shift_group(scalars, first, data, swap, phases):
    crossed = jnp.dot(data, swap, preferred_element_type=F32)
    shifted = []
    for sub in range(4):
        move_x = scalars[0, first + sub]
        move_y = scalars[1, first + sub]
        sign_x = jnp.where(move_x < 0, -1.0, 1.0)
        sign_y = jnp.where(move_y < 0, -1.0, 1.0)
        size_x = jnp.abs(move_x)
        size_y = jnp.abs(move_y)
        cos_x = phases[0, size_x]
        sin_x = phases[1, size_x] * sign_x
        cos_y = phases[2, size_y]
        sin_y = phases[3, size_y] * sign_y
        cosine = cos_x * cos_y - sin_x * sin_y
        sine = sin_x * cos_y + cos_x * sin_y
        near_cos, near_sin = cosine[0:8], sine[0:8]
        for jump in range(8):
            far_cos = cosine[8 + jump : 9 + jump]
            far_sin = sine[8 + jump : 9 + jump]
            rows = slice(sub * CYC + jump * 8, sub * CYC + jump * 8 + 8)
            value = data[rows].astype(F32) * (near_cos * far_cos - near_sin * far_sin)
            value = value + crossed[rows] * (near_sin * far_cos + near_cos * far_sin)
            shifted.append(value)
    return jnp.concatenate(shifted, axis=0).astype(BF16)


def spread_kernel(scalars, parts, wide, swap, phases, turn, ctf_columns, spread, turned, tails):
    step = pl.program_id(0)
    lane = lax.broadcasted_iota(jnp.int32, (1, 128), 1)
    group = lax.broadcasted_iota(jnp.int32, (16, 128), 1) // 32

    def one_group(quad, carry):
        first = step * STEP + quad * 4
        start = pl.multiple_of(quad * 256, 256)
        data = parts[pl.ds(start, 256), :]
        shifted = shift_group(scalars, first, data, swap[...], phases)
        natural = jnp.dot(shifted, wide[...], preferred_element_type=F32)
        for sub in range(4):
            index = first + sub
            rows = slice(sub * CYC, sub * CYC + CYC)
            angles = turn[scalars[3, index]]
            chosen = jnp.where(lane == scalars[2, index], ctf_columns[...], 0.0)
            contrast = jnp.sum(chosen, axis=1, keepdims=True)
            for tile in range(3):
                lanes = slice(tile * 128, tile * 128 + 128)
                cos_rot = angles[tile : tile + 1, :]
                sin_rot = angles[tile + 3 : tile + 4, :]
                there = slice(384 + tile * 128, 384 + tile * 128 + 128)
                value = natural[rows, lanes] * cos_rot + natural[rows, there] * sin_rot
                value = contrast * value
                if tile < 2:
                    for band in range(DOM):
                        begin = band * UROWS + tile * PD + index
                        piece = value[band * BAND : band * BAND + BAND]
                        turned[pl.ds(begin, BAND, stride=2 * PD), :] = piece
                else:
                    tails[sub] = value
                    packed = tails[sub, pl.ds(0, 16, stride=4), :]
                    for place in range(1, 4):
                        other = tails[sub, pl.ds(place, 16, stride=4), :]
                        packed = jnp.where(group == place, other, packed)
                    tails[sub, 0:16, :] = packed
                    for half in range(2):
                        piece = tails[sub, pl.ds(half, DOM, stride=2), :]
                        turned[pl.ds((16 + half) * PD + index, DOM, stride=UROWS), :] = piece
            label = jnp.where(lane == scalars[2, index], 1.0, 0.0)
            label = jnp.where(lane == 16, scalars[4, index].astype(F32), label)
            label = jnp.where(lane == 17, scalars[5, index].astype(F32), label)
            label = jnp.broadcast_to(label, (DOM, 128))
            turned[pl.ds(18 * PD + index, DOM, stride=UROWS), :] = label
        return carry

    lax.fori_loop(0, STEP // 4, one_group, 0)

    @pl.when(step == PD // STEP - 1)
    def _():
        spread[...] = turned[...].astype(BF16)


def spread_bands(particles, scalars, full_table):
    wide, order = wide_columns(full_table)
    ctf_columns = np.zeros((CYC, 128), np.float32)
    ctf_columns[:, :NBINS] = ctf_values().T
    return pl.pallas_call(
        spread_kernel,
        grid_spec=pltpu.PrefetchScalarGridSpec(
            num_scalar_prefetch=1,
            grid=(PD // STEP,),
            in_specs=[
                pl.BlockSpec((STEP * CYC, ROW), lambda i, sc: (i, 0)),
                whole((ROW, 768)),
                whole((ROW, ROW)),
                whole((4, SHIFT + 1, 16, ROW)),
                whole((ROT, 8, 128)),
                whole((CYC, 128)),
            ],
            out_specs=whole((DOM * UROWS, 128)),
            scratch_shapes=[
                pltpu.VMEM((DOM * UROWS, 128), F32),
                pltpu.VMEM((4, CYC, 128), F32),
            ],
        ),
        out_shape=jax.ShapeDtypeStruct((DOM * UROWS, 128), BF16),
        compiler_params=pltpu.CompilerParams(vmem_limit_bytes=VMEM_BYTES // 2),
        cost_estimate=pl.CostEstimate(
            flops=9000000000, bytes_accessed=27000000, transcendentals=0
        ),
        name="spread",
    )(
        scalars,
        particles,
        jnp.asarray(wide),
        jnp.asarray(swap_matrix()),
        jnp.asarray(shift_rows()),
        jnp.asarray(turn_rows(order)),
        jnp.asarray(ctf_columns),
    )


def weight_kernel(core, scalars, parts, table, swap, phases, ctf_rows, mine, other, weighted):
    step = pl.program_id(0)
    low = lax.broadcasted_iota(jnp.int32, (MP, 128), 1) < 64

    def one_group(quad, carry):
        first = step * STEP + quad * 4
        start = pl.multiple_of(quad * 256, 256)
        data = parts[pl.ds(start, 256), :]
        shifted = shift_group(scalars, first, data, swap[...], phases)
        full = lax.dot_general(table[0], shifted, NT, preferred_element_type=F32)
        for pair in range(2):
            lanes = slice(pair * 128, pair * 128 + 128)
            for side in range(2):
                base = side * 2 * MP
                both = merge_halves(
                    full[base : base + MP, lanes], full[base + MP : base + 2 * MP, lanes], low
                )
                for which in range(2):
                    index = first + pair * 2 + which
                    contrast = ctf_rows[pl.ds(scalars[2, index], 1), :]
                    value = both[which] * contrast
                    for parity in range(2):
                        begin = (side * MH + parity) * PD + index
                        piece = value[parity * HH : parity * HH + MH // 2]
                        weighted[pl.ds(begin, MH // 2, stride=2 * PD), :] = piece
        return carry

    lax.fori_loop(0, STEP // 4, one_group, 0)

    @pl.when(step == PD // STEP - 1)
    def _():
        mine[...] = weighted[0 : MH * PD, :].astype(BF16)
        other[...] = weighted[MH * PD :, :].astype(BF16)


def weighted_spectra(core, particles, scalars, table):
    ctf = ctf_values().astype(np.float32)
    half_shape = jax.ShapeDtypeStruct((MH * PD, 128), BF16)
    return pl.pallas_call(
        weight_kernel,
        grid_spec=pltpu.PrefetchScalarGridSpec(
            num_scalar_prefetch=2,
            grid=(PD // STEP,),
            in_specs=[
                pl.BlockSpec((STEP * CYC, ROW), lambda i, core, sc: (i, 0)),
                pl.BlockSpec((1, 4 * MP, ROW), lambda i, core, sc: (core[0], 0, 0)),
                whole((ROW, ROW)),
                whole((4, SHIFT + 1, 16, ROW)),
                whole((NBINS, 128)),
            ],
            out_specs=[whole((MH * PD, 128)), whole((MH * PD, 128))],
            scratch_shapes=[pltpu.VMEM((2 * MH * PD, 128), F32)],
        ),
        out_shape=[half_shape, half_shape],
        compiler_params=pltpu.CompilerParams(vmem_limit_bytes=VMEM_BYTES // 2),
        cost_estimate=pl.CostEstimate(
            flops=10000000000, bytes_accessed=30000000, transcendentals=0
        ),
        name="weights",
    )(
        core,
        scalars,
        particles,
        table,
        jnp.asarray(swap_matrix()),
        jnp.asarray(shift_rows()),
        jnp.asarray(np.concatenate([ctf, ctf], axis=1)),
    )


def fold_kernel(layout, count, core, *refs):
    pieces = refs[:count]
    own, far, signs, bins, kept_out, sent_out, norm = refs[count : count + 7]
    kept, sent, blocks, held, last, scale_rows, arrivals, leaving = refs[count + 7 :]
    copies = []
    for index, (slot, start, rows, first) in enumerate(layout):
        source = pieces[index].at[pl.ds(first, rows), :]
        target = blocks.at[slot, pl.ds(start, rows), :]
        copies.append(pltpu.make_async_copy(source, target, arrivals.at[index]))
    for copy in copies:
        copy.start()
    held[OWN * KD :, :] = jnp.zeros((KPAD - OWN * KD, 1024), BF16)
    scale_rows[...] = jnp.zeros_like(scale_rows)
    lane = lax.broadcasted_iota(jnp.int32, (PD, 128), 1)
    hits = jnp.where((lane == bins[...]) | (lane == bins[...] + NBINS), 1.0, 0.0).astype(BF16)

    def outgoing(unit):
        both = pl.ds(2 * unit, 2)
        return (
            pltpu.make_async_copy(sent.at[both], sent_out.at[both], leaving.at[unit, 0]),
            pltpu.make_async_copy(kept.at[both], kept_out.at[both], leaving.at[unit, 1]),
        )

    def one_unit(unit, carry):
        parts_a, parts_b = [], []
        for place in range(8):
            harmonic = unit * 8 + place
            row = jnp.concatenate([own[harmonic], far[harmonic]], axis=0).astype(F32)
            factor = signs[core[0], harmonic]
            parts_a.append((row * factor[0:1]).astype(BF16))
            swapped = pltpu.roll(row, 64, 1) * factor[2:3]
            parts_b.append((row * factor[1:2] + swapped).astype(BF16))
        left = jnp.concatenate(
            [jnp.concatenate(parts_a, axis=1), jnp.concatenate(parts_b, axis=1)], axis=0
        )
        for pair in range(4):
            start = pl.multiple_of(HEAD + unit * 192 + pair * 48, 16)
            for parity in range(2):
                place = pair * 2 + parity
                lanes = slice(place * 128, place * 128 + 128)
                for slot in range(OWN):
                    held[slot * 16 : slot * 16 + 16, lanes] = blocks[
                        slot, pl.ds(start + parity * 16, 16), :
                    ]
                begin = pl.multiple_of((parity * HH + unit * 4 + pair) * OWN, OWN)
                held[OWN * 24 : OWN * KD, lanes] = last[pl.ds(begin, OWN), :].astype(BF16)
            for slot in range(0, OWN, 2):
                one = blocks[slot, pl.ds(start + 32, 16), :].astype(F32)
                two = blocks[slot + 1, pl.ds(start + 32, 16), :].astype(F32)
                for parity in range(2):
                    place = pair * 2 + parity
                    lanes = slice(place * 128, place * 128 + 128)
                    rows = slice(parity * 8, parity * 8 + 8)
                    both = jnp.concatenate([one[rows], two[rows]], axis=0).astype(BF16)
                    held[256 + slot * 8 : 256 + slot * 8 + 16, lanes] = both
        folded = lax.dot_general(left, held[...], NT, preferred_element_type=F32).astype(BF16)
        kept[2 * unit] = folded[0:PD]
        sent[2 * unit] = folded[PD : 2 * PD]
        kept[2 * unit + 1] = folded[2 * PD : 3 * PD]
        sent[2 * unit + 1] = folded[3 * PD : 4 * PD]
        for copy in outgoing(unit):
            copy.start()
        return carry

    for copy, (slot, start, rows, first) in zip(copies, layout):
        if start < HROWS // 2:
            copy.wait()
    for slot in range(OWN):
        last[pl.ds(slot, MP, stride=OWN), :] = blocks[slot, 0:MP, :].astype(F32)
        scales = blocks[slot, NORM0 : NORM0 + 32, :].astype(F32)
        scale_rows[slot * 16 : slot * 16 + 16, :] = scales[0:16]
        scale_rows[256 + slot * 8 : 256 + slot * 8 + 8, :] = scales[16:24]
        scale_rows[OWN * 24 + slot : OWN * 24 + slot + 1, :] = scales[24:25]
    table = scale_rows[...].astype(BF16)
    norm[...] = lax.dot_general(hits, table, NT, preferred_element_type=F32)
    lax.fori_loop(0, 4, one_unit, 0)
    for copy, (slot, start, rows, first) in zip(copies, layout):
        if start >= HROWS // 2:
            copy.wait()
    lax.fori_loop(4, HALF, one_unit, 0)
    for unit in range(HALF):
        for copy in outgoing(unit):
            copy.wait()


def fold(core, arrived, own, far, bins):
    layout = tuple((slot, start, rows, first) for slot, start, rows, first, _ in arrived)
    count = len(layout)
    piece = jax.ShapeDtypeStruct((UNITS, PD, KPAD), BF16)
    vmem = pl.BlockSpec(memory_space=pltpu.VMEM)
    return pl.pallas_call(
        functools.partial(fold_kernel, layout, count),
        in_specs=[pl.BlockSpec(memory_space=pltpu.SMEM)]
        + [pl.BlockSpec(memory_space=pl.ANY)] * count
        + [vmem] * 4,
        out_specs=[pl.BlockSpec(memory_space=pl.ANY)] * 2 + [vmem],
        scratch_shapes=[
            pltpu.VMEM((UNITS, PD, KPAD), BF16),
            pltpu.VMEM((UNITS, PD, KPAD), BF16),
            pltpu.VMEM((OWN, HROWS, 128), BF16),
            pltpu.VMEM((KPAD, 1024), BF16),
            pltpu.VMEM((MP * OWN, 128), F32),
            pltpu.VMEM((KPAD, 128), F32),
            pltpu.SemaphoreType.DMA((count,)),
            pltpu.SemaphoreType.DMA((HALF, 2)),
        ],
        out_shape=[piece, piece, jax.ShapeDtypeStruct((PD, KPAD), F32)],
        compiler_params=pltpu.CompilerParams(vmem_limit_bytes=VMEM_BYTES),
        cost_estimate=pl.CostEstimate(
            flops=9000000000, bytes_accessed=27000000, transcendentals=0
        ),
        name="fold",
    )(
        core,
        *[value for *_, value in arrived],
        own.reshape(MH, PD, 128),
        far.reshape(MH, PD, 128),
        jnp.asarray(pair_signs()),
        bins,
    )


def moved_by(value, along_x, along_z):
    moves = [
        (x * 4 + z, (x + along_x) % 4 * 4 + (z + along_z) % 4) for x in range(4) for z in range(4)
    ]
    return lax.ppermute(value, "cls", moves)


def join_kernel(left, right, two_x, down, up, two_z, low, high, held, sems):
    half = HROWS // 2
    inward, outward = [], []
    for index, source in enumerate((left, right, two_x, down, up, two_z)):
        first = 0 if index < 3 else half
        target = (low if index < 3 else high).at[pl.ds(index % 3 * half, half), :]
        inward.append(
            pltpu.make_async_copy(source.at[pl.ds(first, half), :], held.at[index], sems.at[index])
        )
        outward.append(pltpu.make_async_copy(held.at[index], target, sems.at[6 + index]))
    for copy in inward:
        copy.start()
    for come, go in zip(inward, outward):
        come.wait()
        go.start()
    for copy in outward:
        copy.wait()


def join(*blocks):
    anywhere = pl.BlockSpec(memory_space=pl.ANY)
    rows = jax.ShapeDtypeStruct((3 * HROWS // 2, 128), BF16)
    return pl.pallas_call(
        join_kernel,
        in_specs=[anywhere] * 6,
        out_specs=[anywhere] * 2,
        scratch_shapes=[
            pltpu.VMEM((6, HROWS // 2, 128), BF16),
            pltpu.SemaphoreType.DMA((12,)),
        ],
        out_shape=[rows, rows],
        compiler_params=pltpu.CompilerParams(vmem_limit_bytes=VMEM_BYTES),
        cost_estimate=pl.CostEstimate(
            flops=2000000000, bytes_accessed=6000000, transcendentals=0
        ),
        name="join",
    )(*blocks)


def cut_kernel(low_before, low_after, high_before, high_after, *refs):
    outs, held, sems = refs[:4], refs[4], refs[5]
    part = 3 * HROWS // 4
    inward, outward = [], []
    for index, source in enumerate((low_before, low_after, high_before, high_after)):
        chunk = pl.ds(index % 2 * part, part)
        inward.append(pltpu.make_async_copy(source.at[chunk, :], held.at[index], sems.at[index]))
        outward.append(pltpu.make_async_copy(held.at[index], outs[index], sems.at[4 + index]))
    for copy in inward:
        copy.start()
    for come, go in zip(inward, outward):
        come.wait()
        go.start()
    for copy in outward:
        copy.wait()


def cut(*rows):
    anywhere = pl.BlockSpec(memory_space=pl.ANY)
    part = jax.ShapeDtypeStruct((3 * HROWS // 4, 128), BF16)
    return pl.pallas_call(
        cut_kernel,
        in_specs=[anywhere] * 4,
        out_specs=[anywhere] * 4,
        scratch_shapes=[
            pltpu.VMEM((4, 3 * HROWS // 4, 128), BF16),
            pltpu.SemaphoreType.DMA((8,)),
        ],
        out_shape=[part] * 4,
        compiler_params=pltpu.CompilerParams(vmem_limit_bytes=VMEM_BYTES),
        cost_estimate=pl.CostEstimate(
            flops=2000000000, bytes_accessed=6000000, transcendentals=0
        ),
        name="cut",
    )(*rows)


def gather_blocks(block):
    half, part = HROWS // 2, 3 * HROWS // 4
    steps = (-1, 1, 2)
    by_x = [moved_by(block, -step, 0) for step in steps]
    by_z = [moved_by(block, 0, -step) for step in steps]
    low_rows, high_rows = join(*by_x, *by_z)
    low_far = [moved_by(low_rows, 0, 1), moved_by(low_rows, 0, -1)]
    high_far = [moved_by(high_rows, 1, 0), moved_by(high_rows, -1, 0)]
    parts = cut(*low_far, *high_far)
    low_two = moved_by(parts[0], 0, 1), moved_by(parts[1], 0, -1)
    high_two = moved_by(parts[2], 1, 0), moved_by(parts[3], -1, 0)

    def slot(x, z):
        return x % 4 * 4 + z % 4

    pieces = []
    for start in (0, half):
        pieces.append((slot(0, 0), start, half, start, block))
        pieces += [(slot(step, 0), start, half, start, by_x[i]) for i, step in enumerate(steps)]
        pieces += [(slot(0, step), start, half, start, by_z[i]) for i, step in enumerate(steps)]
        near, two = (low_far, low_two) if start == 0 else (high_far, high_two)
        for j, inner in enumerate(steps):
            for i, outer in enumerate(steps[:2]):
                place = slot(inner, outer) if start == 0 else slot(outer, inner)
                pieces.append((place, start, half, j * half, near[i]))
            place = slot(inner, 2) if start == 0 else slot(2, inner)
            for i in range(2):
                first = max(j * half, i * part)
                last = min(j * half + half, i * part + part)
                if first < last:
                    begin = start + first - j * half
                    pieces.append((place, begin, last - first, first - i * part, two[i]))
    return pieces, low_rows


def weigh(total, coefficient, value):
    if abs(coefficient) < 1e-12:
        return total
    if abs(coefficient - 1.0) < 1e-12:
        return value if total is None else total + value
    if abs(coefficient + 1.0) < 1e-12:
        return -value if total is None else total - value
    term = value * coefficient
    return term if total is None else total + term


def best_rotation(cosines, sines):
    best = None
    for parity in range(2):
        sign = 1.0 if parity == 0 else -1.0
        even = {0: cosines[0] + sign * cosines[18]}
        odd = {}
        for unit in range(1, 9):
            even[unit] = cosines[unit] + sign * cosines[18 - unit]
            odd[unit] = sines[unit] - sign * sines[18 - unit]
        even[9] = cosines[9]
        odd[9] = sines[9]
        for rotation in range(parity, 10, 2):
            sums = {}
            for name, values, wave in (("e", even, math.cos), ("o", odd, math.sin)):
                for rest in range(2):
                    total = None
                    for unit, value in values.items():
                        if unit % 2 == rest:
                            angle = math.pi * ((unit * rotation) % 36) / 18.0
                            total = weigh(total, wave(angle), value)
                    sums[name, rest] = total

            def joined(first, second, flip):
                if first is None and second is None:
                    return None
                if second is None:
                    return first
                if first is None:
                    return second
                return first - second if flip else first + second

            for flip in (False, True) if rotation < 9 else (False,):
                value = joined(sums["e", 0], sums["e", 1], flip)
                swing = joined(sums["o", 1], sums["o", 0], flip)
                if swing is not None:
                    value = value + jnp.abs(swing)
                best = value if best is None else jnp.maximum(best, value)
    return best


def score_kernel(core, kept, came, norm, out):
    def score(low, high):
        for block in range(2):
            rows = slice(block * 8, block * 8 + 8)
            every = slice(0, 16)
            best = None
            for tile in range(KPAD // 128):
                lanes = slice(tile * 128, tile * 128 + 128)
                cosines, sines = {}, {}
                for unit in range(UNITS):
                    source = low if unit < HALF else high
                    place = unit % HALF * 2
                    cosines[unit] = source[place, every, lanes].astype(F32)[rows]
                    sines[unit] = source[place + 1, every, lanes].astype(F32)[rows]
                cosines[18] = sines[0]
                value = best_rotation(cosines, sines) * norm[rows, lanes]
                if tile == 3:
                    lane = lax.broadcasted_iota(jnp.int32, (8, 128), 1)
                    value = jnp.where(lane < OWN * KD - 384, value, -3e38)
                best = value if best is None else jnp.maximum(best, value)
            out[rows, :] = jnp.max(best, axis=1, keepdims=True)

    @pl.when(core[0] == 0)
    def _():
        score(kept, came)

    @pl.when(core[0] == 1)
    def _():
        score(came, kept)


def scores(core, kept, came, norm):
    return pl.pallas_call(
        score_kernel,
        grid_spec=pltpu.PrefetchScalarGridSpec(
            num_scalar_prefetch=1,
            grid=(PD // 16,),
            in_specs=[
                pl.BlockSpec((UNITS, 16, KPAD), lambda i, core: (0, i, 0)),
                pl.BlockSpec((UNITS, 16, KPAD), lambda i, core: (0, i, 0)),
                pl.BlockSpec((16, KPAD), lambda i, core: (i, 0)),
            ],
            out_specs=pl.BlockSpec((16, 1), lambda i, core: (i, 0)),
        ),
        out_shape=jax.ShapeDtypeStruct((PD, 1), F32),
        compiler_params=pltpu.CompilerParams(vmem_limit_bytes=VMEM_BYTES),
        cost_estimate=pl.CostEstimate(
            flops=3000000000, bytes_accessed=9000000, transcendentals=0
        ),
        name="scores",
    )(core, kept, came, norm)


def class_sum_kernel(arrived, out, last):
    labels = arrived[:, 18 * PD : 19 * PD, :].astype(F32).reshape(DOM * PD, 128)
    block = labels[:, 16:17]
    local = labels[:, 17:18]
    row = jnp.where(local < 23.5, block * 24.0 + local, block + 384.0)
    lane = lax.broadcasted_iota(jnp.int32, (DOM * PD, KPAD), 1).astype(F32)
    hits = jnp.where(lane == row, 1.0, 0.0).T[0 : OWN * KD].astype(BF16)
    last[...] = jnp.zeros_like(last)
    for pair in range(10):
        pieces = [2 * pair, 2 * pair + 1] if pair < 9 else [18]
        right = jnp.concatenate(
            [arrived[:, c * PD : c * PD + PD, :].reshape(DOM * PD, 128) for c in pieces], axis=1
        )
        total = jnp.dot(hits, right, preferred_element_type=F32)
        sums = [total[:, i * 128 : i * 128 + 128] for i in range(len(pieces))]
        for place, value in zip(pieces, sums):
            last[pl.ds(24 + place, OWN, stride=48), :] = value[OWN * 24 :]
        if pair < 9:
            both = jnp.concatenate(
                [value[0 : OWN * 24].reshape(OWN, 24, 128) for value in sums], axis=1
            )
            out[:, pair * 48 : pair * 48 + 48, :] = both.astype(BF16)
        else:
            for owner in range(OWN):
                last[owner * 48 : owner * 48 + 24, :] = sums[0][owner * 24 : owner * 24 + 24]
    out[:, 432:480, :] = last[...].reshape(OWN, 48, 128).astype(BF16)


def class_sums(arrived):
    return pl.pallas_call(
        class_sum_kernel,
        in_specs=[pl.BlockSpec(memory_space=pltpu.VMEM)],
        out_specs=pl.BlockSpec(memory_space=pltpu.VMEM),
        scratch_shapes=[pltpu.VMEM((OWN * 48, 128), F32)],
        out_shape=jax.ShapeDtypeStruct((OWN, SROWS, 128), BF16),
        compiler_params=pltpu.CompilerParams(vmem_limit_bytes=VMEM_BYTES),
        cost_estimate=pl.CostEstimate(
            flops=3000000000, bytes_accessed=9000000, transcendentals=0
        ),
        name="class_sums",
    )(arrived)


def average_kernel(dom, arrived, squares, out, left, middle, right):
    total = arrived[0].astype(F32)
    for source in range(1, OWN):
        total = total + arrived[source].astype(F32)
    counts = jnp.concatenate([total[432:456], total[472:480]], axis=0)
    below = jnp.dot(counts, squares[0], precision=lax.Precision.HIGHEST, preferred_element_type=F32)
    below = below + 1.0
    for cycle in range(BAND):
        usual = below[0:24, cycle : cycle + 1]
        final = below[26:27, cycle : cycle + 1]
        for tile, target in ((0, left), (1, middle), (2, right)):
            if tile < 2:
                piece, turn = cycle * 2 + tile, 0
            else:
                piece, turn = 16 + cycle // 4, (128 - cycle % 4 * 32) % 128
            value = total[piece * 24 : piece * 24 + 24] / usual
            end = total[456 + piece : 457 + piece] / final
            if turn:
                value = pltpu.roll(value, turn, 1)
                end = pltpu.roll(end, turn, 1)
            target[pl.ds(cycle, 24, stride=BAND), :] = value
            target[24 * BAND + cycle : 24 * BAND + cycle + 1, :] = end
    out[:, 0:128] = left[...]
    out[:, 128:256] = middle[...]
    out[:, 256:288] = right[:, 0:32]


def averages(dom, arrived):
    ctf = ctf_values()
    squares = np.zeros((DOM, 128, 128), np.float32)
    for band in range(DOM):
        squares[band, :NBINS, :BAND] = (ctf * ctf)[:, band * BAND : band * BAND + BAND]
    return pl.pallas_call(
        average_kernel,
        grid_spec=pltpu.PrefetchScalarGridSpec(
            num_scalar_prefetch=1,
            grid=(1,),
            in_specs=[
                whole((OWN, SROWS, 128)),
                pl.BlockSpec((1, 128, 128), lambda i, dom: (dom[0], 0, 0)),
            ],
            out_specs=whole((KD * BAND, ROW)),
            scratch_shapes=[pltpu.VMEM((KD * BAND, 128), F32)] * 3,
        ),
        out_shape=jax.ShapeDtypeStruct((KD * BAND, ROW), F32),
        compiler_params=pltpu.CompilerParams(vmem_limit_bytes=VMEM_BYTES),
        cost_estimate=pl.CostEstimate(
            flops=2000000000, bytes_accessed=6000000, transcendentals=0
        ),
        name="averages",
    )(dom, arrived, jnp.asarray(squares))


def on_device(particles, references, class_block, class_local, rotation, shifts, defocus):
    dom = lax.axis_index("dom").astype(jnp.int32).reshape(1)
    core = dom % 2
    full_table, split_table = dft_rows()
    table = jnp.asarray(split_table)
    gathered, joined = gather_blocks(own_harmonics(core, references, table))
    scalars = jnp.stack(
        [shifts[:, 0], shifts[:, 1], defocus, rotation, class_block[:, 0], class_local], axis=0
    )
    rows = particles.reshape(PD * CYC, ROW)
    spread = spread_bands(rows, scalars, full_table)
    late_scalars, _ = lax.optimization_barrier((scalars, joined))
    own, other = weighted_spectra(core, rows, late_scalars, table)
    swap = [(i, i ^ 1) for i in range(DOM)]
    far = lax.ppermute(other, "dom", swap)
    arrived = lax.all_to_all(spread.reshape(DOM, UROWS, 128), "dom", 0, 0, tiled=True)
    sums = lax.all_to_all(class_sums(arrived), "cls", 0, 0, tiled=True)
    class_average = averages(dom, sums).reshape(KD, BAND, ROW)
    kept, sent, norm = fold(core, gathered, own, far, defocus.reshape(PD, 1))
    came = lax.ppermute(sent, "dom", swap)
    best_score = scores(core, kept, came, norm).reshape(PD)
    return (best_score, class_average)


def solution(mesh):
    placed = (
        P(("dom", "cls"), None, None),
        P("cls", None, None),
        P(("dom", "cls"), None),
        P(("dom", "cls")),
        P(("dom", "cls")),
        P(("dom", "cls"), None),
        P(("dom", "cls")),
    )
    return jax.shard_map(
        on_device,
        mesh=mesh,
        in_specs=placed,
        out_specs=(P(("dom", "cls")), P("cls", "dom", None)),
        check_vma=False,
    )
```

```python
import functools
import math

import jax
import jax.numpy as jnp
import ml_dtypes
import numpy as np
from jax import lax
from jax.experimental import pallas as pl
from jax.experimental.pallas import tpu as pltpu
from jax.sharding import PartitionSpec as P

ROT = 36
BOX = 128
NBINS = 16
EPSILON = 1e-06
CYC = 64
ANG = 144
ROW = 2 * ANG
SHIFT = 5
PD = 48
KD = 25
OWN = 16
DOM = 8
BAND = CYC // DOM
UNITS = 18
HALF = UNITS // 2
MH = HALF * 8
HEAD = 192
NORM0 = 96
HROWS = HEAD + MH * 24
HH = 40
MP = 2 * HH
CHUNKS = 19
UROWS = CHUNKS * PD
SROWS = 480
KPAD = 512
STEP = 16
F32 = jnp.float32
BF16 = jnp.bfloat16
VMEM_BYTES = 58 * 1024 * 1024
NT = (((1,), (1,)), ((), ()))


def unit_harmonics():
    rows = []
    for unit in range(UNITS):
        plus, minus = (0, 18) if unit == 0 else (unit, ROT - unit)
        rows.append([plus + ROT * q for q in range(4)] + [minus + ROT * q for q in range(4)])
    return np.array(rows).reshape(2, MH)


def dft_rows():
    turn = np.arange(ANG)[:, None] * np.arange(ANG)[None, :] % ANG
    angle = turn.astype(np.float32) * np.float32(2.0 * math.pi / ANG)
    cosine = np.cos(angle.astype(np.float64))
    sine = np.sin(angle.astype(np.float64))
    upper = np.concatenate([cosine, -sine], axis=1)
    lower = np.concatenate([sine, cosine], axis=1)
    full = np.concatenate([upper, lower], axis=0).astype(np.float32).astype(ml_dtypes.bfloat16)
    halves = unit_harmonics()
    split = []
    for core in range(2):
        mine, other = halves[core], halves[1 - core]
        rows = np.zeros((4 * MP, ROW), ml_dtypes.bfloat16)
        for index, columns in enumerate((mine, ANG + mine, other, ANG + other)):
            for parity in range(2):
                start = index * MP + parity * HH
                rows[start : start + MH // 2] = full[:, columns[parity::2]].T
        split.append(rows)
    return full, np.stack(split)


def wide_columns(full):
    order = np.concatenate([np.arange(256)] + [np.arange(256, 288)] * 4)
    swapped = np.concatenate([-full[:, ANG:], full[:, :ANG]], axis=1)
    return np.concatenate([full[:, order], swapped[:, order]], axis=1), order


def turn_rows(order):
    harmonic = order % ANG
    turn = np.arange(ROT)[:, None] * 4 * harmonic[None, :] % ANG
    angle = turn * (2.0 * math.pi / ANG)
    angle = angle.reshape(ROT, 3, 128)
    rest = np.zeros((ROT, 2, 128))
    return np.concatenate([np.cos(angle), np.sin(angle), rest], axis=1).astype(np.float32)


def ctf_values():
    radius = (np.arange(CYC) + 1) / CYC
    level = np.arange(NBINS) / NBINS
    phase = math.pi * (3.0 + 9.0 * level[:, None]) * (radius * radius)[None, :]
    return 0.995 * np.sin(phase) + 0.1 * np.cos(phase)


def shift_rows():
    angle = np.arange(ANG) * (2.0 * math.pi / ANG)
    scale = 2.0 * math.pi / BOX * np.concatenate([np.arange(8), 8 * np.arange(8)])
    size = np.arange(SHIFT + 1)
    out = []
    for beam in (np.cos(angle), np.sin(angle)):
        phase = size[:, None, None] * scale[None, :, None] * beam[None, None, :]
        phase = np.concatenate([phase, phase], axis=2)
        out += [np.cos(phase), np.sin(phase)]
    return np.stack(out).astype(np.float32)


def swap_matrix():
    swap = np.zeros((ROW, ROW), np.float32)
    index = np.arange(ANG)
    swap[ANG + index, index] = -1.0
    swap[index, ANG + index] = 1.0
    return swap.astype(ml_dtypes.bfloat16)


def pair_signs():
    signs = np.zeros((2, 3, MH, 128), np.float32)
    for core in range(2):
        for row in range(MH):
            unit, place = core * HALF + row // 8, row % 8
            if unit == 0:
                signs[core, 0 if place < 4 else 1, row] = 1.0
            else:
                signs[core, 0, row] = 1.0
                flip = 1.0 if place < 4 else -1.0
                signs[core, 2, row, :64] = -flip
                signs[core, 2, row, 64:] = flip
    signs = np.pad(signs.transpose(0, 2, 1, 3), ((0, 0), (0, 0), (0, 5), (0, 0)))
    return signs


def whole(shape):
    return pl.BlockSpec(shape, lambda *_: (0,) * len(shape))


def merge_halves(real, imag, low):
    first = jnp.where(low, real, pltpu.roll(imag, 64, 1))
    second = jnp.where(low, pltpu.roll(real, 64, 1), imag)
    return first, second


def harmonics_kernel(
    core, refs_any, table_any, squares_any, out, refs, table, squares, scratch, energy, norms, sems
):
    copies = [pltpu.make_async_copy(table_any.at[core[0]], table, sems.at[0])]
    for index in range(4):
        chunk = pl.ds(index * 512, 512 if index < 3 else 64)
        copies.append(
            pltpu.make_async_copy(refs_any.at[chunk, :], refs.at[chunk, :], sems.at[index + 1])
        )
    copies.append(pltpu.make_async_copy(squares_any, squares, sems.at[5]))
    for copy in copies:
        copy.start()
    scratch[0:HEAD, :] = jnp.zeros((HEAD, 128), F32)
    energy[...] = jnp.zeros_like(energy)
    low = lax.broadcasted_iota(jnp.int32, (MP, 128), 1) < 64
    copies[0].wait()
    rows = table[...]

    def place(klass, value):
        if klass == 24:
            scratch[0:MP, :] = value
            return
        for parity in range(2):
            start = HEAD + (parity * 16 + klass if klass < 16 else 16 + parity * 8 + klass)
            piece = value[parity * HH : parity * HH + MH // 2]
            scratch[pl.ds(start, MH // 2, stride=48), :] = piece

    for group in range(7):
        start, width = (group * 256, 256) if group < 6 else (KD * CYC - 128, 128)
        if group % 2 == 0:
            copies[1 + group // 2].wait()
        full = lax.dot_general(rows, refs[start : start + width, :], NT, preferred_element_type=F32)
        kept = full.astype(BF16).astype(F32)
        total = jnp.sum(kept * kept, axis=0, keepdims=True)
        if group < 6:
            energy[group : group + 1, :] = total
        else:
            energy[group : group + 1, 0:128] = jnp.where(low[0:1], pltpu.roll(total, 64, 1), 0.0)
        for pair in range(width // 128):
            lanes = slice(pair * 128, pair * 128 + 128)
            first, second = merge_halves(full[0:MP, lanes], full[MP : 2 * MP, lanes], low)
            if group < 6:
                place(group * 4 + pair * 2, first)
                place(group * 4 + pair * 2 + 1, second)
            else:
                place(24, second)
    copies[5].wait()
    for sub in range(4):
        lanes = slice(sub // 2 * 128, sub // 2 * 128 + 128)
        power = jnp.dot(
            energy[:, lanes],
            squares[sub % 2],
            precision=lax.Precision.HIGHEST,
            preferred_element_type=F32,
        )
        norms[pl.ds(sub, 8, stride=4), :] = power
    scale = (1.0 / ANG) / jnp.sqrt(norms[...] * (1.0 / ANG) + EPSILON)
    scale = jnp.where(lax.broadcasted_iota(jnp.int32, (32, 128), 1) < NBINS, scale, 0.0)
    high = scale.astype(BF16).astype(F32)
    scratch[NORM0 : NORM0 + 32, :] = high + pltpu.roll(scale - high, NBINS, 1)
    out[...] = scratch[...].astype(BF16)


def own_harmonics(core, references, table):
    squares = np.zeros((2, 128, 128), np.float32)
    ctf = ctf_values()
    for sub in range(2):
        squares[sub, 64 * sub : 64 * sub + 64, :NBINS] = (ctf * ctf).T
    return pl.pallas_call(
        harmonics_kernel,
        in_specs=[
            pl.BlockSpec(memory_space=pltpu.SMEM),
            pl.BlockSpec(memory_space=pl.ANY),
            pl.BlockSpec(memory_space=pl.ANY),
            pl.BlockSpec(memory_space=pl.ANY),
        ],
        out_specs=pl.BlockSpec(memory_space=pltpu.VMEM),
        scratch_shapes=[
            pltpu.VMEM((KD * CYC, ROW), BF16),
            pltpu.VMEM((4 * MP, ROW), BF16),
            pltpu.VMEM((2, 128, 128), F32),
            pltpu.VMEM((HROWS, 128), F32),
            pltpu.VMEM((8, 256), F32),
            pltpu.VMEM((32, 128), F32),
            pltpu.SemaphoreType.DMA((6,)),
        ],
        out_shape=jax.ShapeDtypeStruct((HROWS, 128), BF16),
        compiler_params=pltpu.CompilerParams(vmem_limit_bytes=VMEM_BYTES),
        cost_estimate=pl.CostEstimate(
            flops=4000000000, bytes_accessed=12000000, transcendentals=0
        ),
        name="harmonics",
    )(core, references.reshape(KD * CYC, ROW), table, jnp.asarray(squares))


def shift_group(scalars, first, data, swap, phases):
    crossed = jnp.dot(data, swap, preferred_element_type=F32)
    shifted = []
    for sub in range(4):
        move_x = scalars[0, first + sub]
        move_y = scalars[1, first + sub]
        sign_x = jnp.where(move_x < 0, -1.0, 1.0)
        sign_y = jnp.where(move_y < 0, -1.0, 1.0)
        size_x = jnp.abs(move_x)
        size_y = jnp.abs(move_y)
        cos_x = phases[0, size_x]
        sin_x = phases[1, size_x] * sign_x
        cos_y = phases[2, size_y]
        sin_y = phases[3, size_y] * sign_y
        cosine = cos_x * cos_y - sin_x * sin_y
        sine = sin_x * cos_y + cos_x * sin_y
        near_cos, near_sin = cosine[0:8], sine[0:8]
        for jump in range(8):
            far_cos = cosine[8 + jump : 9 + jump]
            far_sin = sine[8 + jump : 9 + jump]
            rows = slice(sub * CYC + jump * 8, sub * CYC + jump * 8 + 8)
            value = data[rows].astype(F32) * (near_cos * far_cos - near_sin * far_sin)
            value = value + crossed[rows] * (near_sin * far_cos + near_cos * far_sin)
            shifted.append(value)
    return jnp.concatenate(shifted, axis=0).astype(BF16)


def spread_kernel(scalars, parts, wide, swap, phases, turn, ctf_columns, spread, turned, tails):
    step = pl.program_id(0)
    lane = lax.broadcasted_iota(jnp.int32, (1, 128), 1)
    group = lax.broadcasted_iota(jnp.int32, (16, 128), 1) // 32

    def one_group(quad, carry):
        first = step * STEP + quad * 4
        start = pl.multiple_of(quad * 256, 256)
        data = parts[pl.ds(start, 256), :]
        shifted = shift_group(scalars, first, data, swap[...], phases)
        natural = jnp.dot(shifted, wide[...], preferred_element_type=F32)
        for sub in range(4):
            index = first + sub
            rows = slice(sub * CYC, sub * CYC + CYC)
            angles = turn[scalars[3, index]]
            chosen = jnp.where(lane == scalars[2, index], ctf_columns[...], 0.0)
            contrast = jnp.sum(chosen, axis=1, keepdims=True)
            for tile in range(3):
                lanes = slice(tile * 128, tile * 128 + 128)
                cos_rot = angles[tile : tile + 1, :]
                sin_rot = angles[tile + 3 : tile + 4, :]
                there = slice(384 + tile * 128, 384 + tile * 128 + 128)
                value = natural[rows, lanes] * cos_rot + natural[rows, there] * sin_rot
                value = contrast * value
                if tile < 2:
                    for band in range(DOM):
                        begin = band * UROWS + tile * PD + index
                        piece = value[band * BAND : band * BAND + BAND]
                        turned[pl.ds(begin, BAND, stride=2 * PD), :] = piece
                else:
                    tails[sub] = value
                    packed = tails[sub, pl.ds(0, 16, stride=4), :]
                    for place in range(1, 4):
                        other = tails[sub, pl.ds(place, 16, stride=4), :]
                        packed = jnp.where(group == place, other, packed)
                    tails[sub, 0:16, :] = packed
                    for half in range(2):
                        piece = tails[sub, pl.ds(half, DOM, stride=2), :]
                        turned[pl.ds((16 + half) * PD + index, DOM, stride=UROWS), :] = piece
            label = jnp.where(lane == scalars[2, index], 1.0, 0.0)
            label = jnp.where(lane == 16, scalars[4, index].astype(F32), label)
            label = jnp.where(lane == 17, scalars[5, index].astype(F32), label)
            label = jnp.broadcast_to(label, (DOM, 128))
            turned[pl.ds(18 * PD + index, DOM, stride=UROWS), :] = label
        return carry

    lax.fori_loop(0, STEP // 4, one_group, 0, unroll=True)

    @pl.when(step == PD // STEP - 1)
    def _():
        spread[...] = turned[...].astype(BF16)


def spread_bands(particles, scalars, full_table):
    wide, order = wide_columns(full_table)
    ctf_columns = np.zeros((CYC, 128), np.float32)
    ctf_columns[:, :NBINS] = ctf_values().T
    return pl.pallas_call(
        spread_kernel,
        grid_spec=pltpu.PrefetchScalarGridSpec(
            num_scalar_prefetch=1,
            grid=(PD // STEP,),
            in_specs=[
                pl.BlockSpec((STEP * CYC, ROW), lambda i, sc: (i, 0)),
                whole((ROW, 768)),
                whole((ROW, ROW)),
                whole((4, SHIFT + 1, 16, ROW)),
                whole((ROT, 8, 128)),
                whole((CYC, 128)),
            ],
            out_specs=whole((DOM * UROWS, 128)),
            scratch_shapes=[
                pltpu.VMEM((DOM * UROWS, 128), F32),
                pltpu.VMEM((4, CYC, 128), F32),
            ],
        ),
        out_shape=jax.ShapeDtypeStruct((DOM * UROWS, 128), BF16),
        compiler_params=pltpu.CompilerParams(vmem_limit_bytes=VMEM_BYTES // 2),
        cost_estimate=pl.CostEstimate(
            flops=9000000000, bytes_accessed=27000000, transcendentals=0
        ),
        name="spread",
    )(
        scalars,
        particles,
        jnp.asarray(wide),
        jnp.asarray(swap_matrix()),
        jnp.asarray(shift_rows()),
        jnp.asarray(turn_rows(order)),
        jnp.asarray(ctf_columns),
    )


def weight_kernel(core, scalars, parts, table, swap, phases, ctf_rows, mine, other, weighted):
    step = pl.program_id(0)
    low = lax.broadcasted_iota(jnp.int32, (MP, 128), 1) < 64

    def one_group(quad, carry):
        first = step * STEP + quad * 4
        start = pl.multiple_of(quad * 256, 256)
        data = parts[pl.ds(start, 256), :]
        shifted = shift_group(scalars, first, data, swap[...], phases)
        full = lax.dot_general(table[0], shifted, NT, preferred_element_type=F32)
        for pair in range(2):
            lanes = slice(pair * 128, pair * 128 + 128)
            for side in range(2):
                base = side * 2 * MP
                both = merge_halves(
                    full[base : base + MP, lanes], full[base + MP : base + 2 * MP, lanes], low
                )
                for which in range(2):
                    index = first + pair * 2 + which
                    contrast = ctf_rows[pl.ds(scalars[2, index], 1), :]
                    value = both[which] * contrast
                    for parity in range(2):
                        begin = (side * MH + parity) * PD + index
                        piece = value[parity * HH : parity * HH + MH // 2]
                        weighted[pl.ds(begin, MH // 2, stride=2 * PD), :] = piece
        return carry

    lax.fori_loop(0, STEP // 4, one_group, 0, unroll=True)

    @pl.when(step == PD // STEP - 1)
    def _():
        mine[...] = weighted[0 : MH * PD, :].astype(BF16)
        other[...] = weighted[MH * PD :, :].astype(BF16)


def weighted_spectra(core, particles, scalars, table):
    ctf = ctf_values().astype(np.float32)
    half_shape = jax.ShapeDtypeStruct((MH * PD, 128), BF16)
    return pl.pallas_call(
        weight_kernel,
        grid_spec=pltpu.PrefetchScalarGridSpec(
            num_scalar_prefetch=2,
            grid=(PD // STEP,),
            in_specs=[
                pl.BlockSpec((STEP * CYC, ROW), lambda i, core, sc: (i, 0)),
                pl.BlockSpec((1, 4 * MP, ROW), lambda i, core, sc: (core[0], 0, 0)),
                whole((ROW, ROW)),
                whole((4, SHIFT + 1, 16, ROW)),
                whole((NBINS, 128)),
            ],
            out_specs=[whole((MH * PD, 128)), whole((MH * PD, 128))],
            scratch_shapes=[pltpu.VMEM((2 * MH * PD, 128), F32)],
        ),
        out_shape=[half_shape, half_shape],
        compiler_params=pltpu.CompilerParams(vmem_limit_bytes=VMEM_BYTES // 2),
        cost_estimate=pl.CostEstimate(
            flops=10000000000, bytes_accessed=30000000, transcendentals=0
        ),
        name="weights",
    )(
        core,
        scalars,
        particles,
        table,
        jnp.asarray(swap_matrix()),
        jnp.asarray(shift_rows()),
        jnp.asarray(np.concatenate([ctf, ctf], axis=1)),
    )


def fold_kernel(layout, count, core, *refs):
    pieces = refs[:count]
    own, far, signs, bins, kept_out, sent_out, norm = refs[count : count + 7]
    kept, sent, blocks, held, last, scale_rows, arrivals, leaving = refs[count + 7 :]
    copies = []
    for index, (slot, start, rows, first) in enumerate(layout):
        source = pieces[index].at[pl.ds(first, rows), :]
        target = blocks.at[slot, pl.ds(start, rows), :]
        copies.append(pltpu.make_async_copy(source, target, arrivals.at[index]))
    for copy in copies:
        copy.start()
    held[OWN * KD :, :] = jnp.zeros((KPAD - OWN * KD, 1024), BF16)
    scale_rows[...] = jnp.zeros_like(scale_rows)
    lane = lax.broadcasted_iota(jnp.int32, (PD, 128), 1)
    row = lax.broadcasted_iota(jnp.int32, (PD, 128), 0)
    level = jnp.zeros((PD, 128), jnp.int32)
    for index in range(PD):
        level = jnp.where(row == index, bins[index], level)
    hits = jnp.where((lane == level) | (lane == level + NBINS), 1.0, 0.0).astype(BF16)

    def outgoing(unit):
        both = pl.ds(2 * unit, 2)
        return (
            pltpu.make_async_copy(sent.at[both], sent_out.at[both], leaving.at[unit, 0]),
            pltpu.make_async_copy(kept.at[both], kept_out.at[both], leaving.at[unit, 1]),
        )

    def one_unit(unit, carry):
        parts_a, parts_b = [], []
        for place in range(8):
            harmonic = unit * 8 + place
            row = jnp.concatenate([own[harmonic], far[harmonic]], axis=0).astype(F32)
            factor = signs[core[0], harmonic]
            parts_a.append((row * factor[0:1]).astype(BF16))
            swapped = pltpu.roll(row, 64, 1) * factor[2:3]
            parts_b.append((row * factor[1:2] + swapped).astype(BF16))
        left = jnp.concatenate(
            [jnp.concatenate(parts_a, axis=1), jnp.concatenate(parts_b, axis=1)], axis=0
        )
        for pair in range(4):
            start = pl.multiple_of(HEAD + unit * 192 + pair * 48, 16)
            for parity in range(2):
                place = pair * 2 + parity
                lanes = slice(place * 128, place * 128 + 128)
                for slot in range(OWN):
                    held[slot * 16 : slot * 16 + 16, lanes] = blocks[
                        slot, pl.ds(start + parity * 16, 16), :
                    ]
                begin = pl.multiple_of((parity * HH + unit * 4 + pair) * OWN, OWN)
                held[OWN * 24 : OWN * KD, lanes] = last[pl.ds(begin, OWN), :].astype(BF16)
            for slot in range(0, OWN, 2):
                one = blocks[slot, pl.ds(start + 32, 16), :].astype(F32)
                two = blocks[slot + 1, pl.ds(start + 32, 16), :].astype(F32)
                for parity in range(2):
                    place = pair * 2 + parity
                    lanes = slice(place * 128, place * 128 + 128)
                    rows = slice(parity * 8, parity * 8 + 8)
                    both = jnp.concatenate([one[rows], two[rows]], axis=0).astype(BF16)
                    held[256 + slot * 8 : 256 + slot * 8 + 16, lanes] = both
        folded = lax.dot_general(left, held[...], NT, preferred_element_type=F32).astype(BF16)
        kept[2 * unit] = folded[0:PD]
        sent[2 * unit] = folded[PD : 2 * PD]
        kept[2 * unit + 1] = folded[2 * PD : 3 * PD]
        sent[2 * unit + 1] = folded[3 * PD : 4 * PD]
        for copy in outgoing(unit):
            copy.start()
        return carry

    for copy, (slot, start, rows, first) in zip(copies, layout):
        if start < HROWS // 2:
            copy.wait()
    for slot in range(OWN):
        last[pl.ds(slot, MP, stride=OWN), :] = blocks[slot, 0:MP, :].astype(F32)
        scales = blocks[slot, NORM0 : NORM0 + 32, :].astype(F32)
        scale_rows[slot * 16 : slot * 16 + 16, :] = scales[0:16]
        scale_rows[256 + slot * 8 : 256 + slot * 8 + 8, :] = scales[16:24]
        scale_rows[OWN * 24 + slot : OWN * 24 + slot + 1, :] = scales[24:25]
    table = scale_rows[...].astype(BF16)
    norm[...] = lax.dot_general(hits, table, NT, preferred_element_type=F32)
    lax.fori_loop(0, 4, one_unit, 0, unroll=True)
    for copy, (slot, start, rows, first) in zip(copies, layout):
        if start >= HROWS // 2:
            copy.wait()
    lax.fori_loop(4, HALF, one_unit, 0, unroll=True)
    for unit in range(HALF):
        for copy in outgoing(unit):
            copy.wait()


def fold(core, arrived, own, far, bins):
    layout = tuple((slot, start, rows, first) for slot, start, rows, first, _ in arrived)
    count = len(layout)
    piece = jax.ShapeDtypeStruct((UNITS, PD, KPAD), BF16)
    vmem = pl.BlockSpec(memory_space=pltpu.VMEM)
    return pl.pallas_call(
        functools.partial(fold_kernel, layout, count),
        in_specs=[pl.BlockSpec(memory_space=pltpu.SMEM)]
        + [pl.BlockSpec(memory_space=pl.ANY)] * count
        + [vmem] * 3
        + [pl.BlockSpec(memory_space=pltpu.SMEM)],
        out_specs=[pl.BlockSpec(memory_space=pl.ANY)] * 2 + [vmem],
        scratch_shapes=[
            pltpu.VMEM((UNITS, PD, KPAD), BF16),
            pltpu.VMEM((UNITS, PD, KPAD), BF16),
            pltpu.VMEM((OWN, HROWS, 128), BF16),
            pltpu.VMEM((KPAD, 1024), BF16),
            pltpu.VMEM((MP * OWN, 128), F32),
            pltpu.VMEM((KPAD, 128), F32),
            pltpu.SemaphoreType.DMA((count,)),
            pltpu.SemaphoreType.DMA((HALF, 2)),
        ],
        out_shape=[piece, piece, jax.ShapeDtypeStruct((PD, KPAD), F32)],
        compiler_params=pltpu.CompilerParams(vmem_limit_bytes=VMEM_BYTES),
        cost_estimate=pl.CostEstimate(
            flops=9000000000, bytes_accessed=27000000, transcendentals=0
        ),
        name="fold",
    )(
        core,
        *[value for *_, value in arrived],
        own.reshape(MH, PD, 128),
        far.reshape(MH, PD, 128),
        jnp.asarray(pair_signs()),
        bins,
    )


def moved_by(value, along_x, along_z):
    moves = [
        (x * 4 + z, (x + along_x) % 4 * 4 + (z + along_z) % 4) for x in range(4) for z in range(4)
    ]
    return lax.ppermute(value, "cls", moves)


def join_kernel(left, right, two_x, down, up, two_z, low, high, held, sems):
    half = HROWS // 2
    inward, outward = [], []
    for index, source in enumerate((left, right, two_x, down, up, two_z)):
        first = 0 if index < 3 else half
        target = (low if index < 3 else high).at[pl.ds(index % 3 * half, half), :]
        inward.append(
            pltpu.make_async_copy(source.at[pl.ds(first, half), :], held.at[index], sems.at[index])
        )
        outward.append(pltpu.make_async_copy(held.at[index], target, sems.at[6 + index]))
    for copy in inward:
        copy.start()
    for come, go in zip(inward, outward):
        come.wait()
        go.start()
    for copy in outward:
        copy.wait()


def join(*blocks):
    anywhere = pl.BlockSpec(memory_space=pl.ANY)
    rows = jax.ShapeDtypeStruct((3 * HROWS // 2, 128), BF16)
    return pl.pallas_call(
        join_kernel,
        in_specs=[anywhere] * 6,
        out_specs=[anywhere] * 2,
        scratch_shapes=[
            pltpu.VMEM((6, HROWS // 2, 128), BF16),
            pltpu.SemaphoreType.DMA((12,)),
        ],
        out_shape=[rows, rows],
        compiler_params=pltpu.CompilerParams(vmem_limit_bytes=VMEM_BYTES),
        cost_estimate=pl.CostEstimate(
            flops=2000000000, bytes_accessed=6000000, transcendentals=0
        ),
        name="join",
    )(*blocks)


def cut_kernel(low_before, low_after, high_before, high_after, *refs):
    outs, held, sems = refs[:4], refs[4], refs[5]
    part = 3 * HROWS // 4
    inward, outward = [], []
    for index, source in enumerate((low_before, low_after, high_before, high_after)):
        chunk = pl.ds(index % 2 * part, part)
        inward.append(pltpu.make_async_copy(source.at[chunk, :], held.at[index], sems.at[index]))
        outward.append(pltpu.make_async_copy(held.at[index], outs[index], sems.at[4 + index]))
    for copy in inward:
        copy.start()
    for come, go in zip(inward, outward):
        come.wait()
        go.start()
    for copy in outward:
        copy.wait()


def cut(*rows):
    anywhere = pl.BlockSpec(memory_space=pl.ANY)
    part = jax.ShapeDtypeStruct((3 * HROWS // 4, 128), BF16)
    return pl.pallas_call(
        cut_kernel,
        in_specs=[anywhere] * 4,
        out_specs=[anywhere] * 4,
        scratch_shapes=[
            pltpu.VMEM((4, 3 * HROWS // 4, 128), BF16),
            pltpu.SemaphoreType.DMA((8,)),
        ],
        out_shape=[part] * 4,
        compiler_params=pltpu.CompilerParams(vmem_limit_bytes=VMEM_BYTES),
        cost_estimate=pl.CostEstimate(
            flops=2000000000, bytes_accessed=6000000, transcendentals=0
        ),
        name="cut",
    )(*rows)


def gather_blocks(block, spread_of):
    half, part = HROWS // 2, 3 * HROWS // 4
    steps = (-1, 1, 2)
    by_x = [moved_by(block, -step, 0) for step in steps]
    by_z = [moved_by(block, 0, -step) for step in steps]
    by_x[2], spread = spread_of(by_x[2])
    low_rows, high_rows = join(*by_x, *by_z)
    low_far = [moved_by(low_rows, 0, 1), moved_by(low_rows, 0, -1)]
    high_far = [moved_by(high_rows, 1, 0), moved_by(high_rows, -1, 0)]
    arrived = lax.all_to_all(spread.reshape(DOM, UROWS, 128), "dom", 0, 0, tiled=True)
    sums = class_sums(arrived)
    low_far, high_far, sums = lax.optimization_barrier((low_far, high_far, sums))
    parts = cut(*low_far, *high_far)
    low_two = moved_by(parts[0], 0, 1), moved_by(parts[1], 0, -1)
    high_two = moved_by(parts[2], 1, 0), moved_by(parts[3], -1, 0)

    def slot(x, z):
        return x % 4 * 4 + z % 4

    pieces = []
    for start in (0, half):
        pieces.append((slot(0, 0), start, half, start, block))
        pieces += [(slot(step, 0), start, half, start, by_x[i]) for i, step in enumerate(steps)]
        pieces += [(slot(0, step), start, half, start, by_z[i]) for i, step in enumerate(steps)]
        near, two = (low_far, low_two) if start == 0 else (high_far, high_two)
        for j, inner in enumerate(steps):
            for i, outer in enumerate(steps[:2]):
                place = slot(inner, outer) if start == 0 else slot(outer, inner)
                pieces.append((place, start, half, j * half, near[i]))
            place = slot(inner, 2) if start == 0 else slot(2, inner)
            for i in range(2):
                first = max(j * half, i * part)
                last = min(j * half + half, i * part + part)
                if first < last:
                    begin = start + first - j * half
                    pieces.append((place, begin, last - first, first - i * part, two[i]))
    return pieces, low_rows, sums


def weigh(total, coefficient, value):
    if abs(coefficient) < 1e-12:
        return total
    if abs(coefficient - 1.0) < 1e-12:
        return value if total is None else total + value
    if abs(coefficient + 1.0) < 1e-12:
        return -value if total is None else total - value
    term = value * coefficient
    return term if total is None else total + term


def best_rotation(cosines, sines):
    best = None
    for parity in range(2):
        sign = 1.0 if parity == 0 else -1.0
        even = {0: cosines[0] + sign * cosines[18]}
        odd = {}
        for unit in range(1, 9):
            even[unit] = cosines[unit] + sign * cosines[18 - unit]
            odd[unit] = sines[unit] - sign * sines[18 - unit]
        even[9] = cosines[9]
        odd[9] = sines[9]
        for rotation in range(parity, 10, 2):
            sums = {}
            for name, values, wave in (("e", even, math.cos), ("o", odd, math.sin)):
                for rest in range(2):
                    total = None
                    for unit, value in values.items():
                        if unit % 2 == rest:
                            angle = math.pi * ((unit * rotation) % 36) / 18.0
                            total = weigh(total, wave(angle), value)
                    sums[name, rest] = total

            def joined(first, second, flip):
                if first is None and second is None:
                    return None
                if second is None:
                    return first
                if first is None:
                    return second
                return first - second if flip else first + second

            for flip in (False, True) if rotation < 9 else (False,):
                value = joined(sums["e", 0], sums["e", 1], flip)
                swing = joined(sums["o", 1], sums["o", 0], flip)
                if swing is not None:
                    value = value + jnp.abs(swing)
                best = value if best is None else jnp.maximum(best, value)
    return best


def score_kernel(core, kept, came, norm, out, found):
    step = pl.program_id(0)

    def score(low, high):
        for block in range(2):
            rows = slice(block * 8, block * 8 + 8)
            every = slice(0, 16)
            best = None
            for tile in range(KPAD // 128):
                lanes = slice(tile * 128, tile * 128 + 128)
                cosines, sines = {}, {}
                for unit in range(UNITS):
                    source = low if unit < HALF else high
                    place = unit % HALF * 2
                    cosines[unit] = source[place, every, lanes].astype(F32)[rows]
                    sines[unit] = source[place + 1, every, lanes].astype(F32)[rows]
                cosines[18] = sines[0]
                value = best_rotation(cosines, sines) * norm[rows, lanes]
                if tile == 3:
                    lane = lax.broadcasted_iota(jnp.int32, (8, 128), 1)
                    value = jnp.where(lane < OWN * KD - 384, value, -3e38)
                best = value if best is None else jnp.maximum(best, value)
            best = jnp.broadcast_to(jnp.max(best, axis=1, keepdims=True), (8, 128))
            found[pl.ds(pl.multiple_of(step * 16 + block * 8, 8), 8), :] = best

    @pl.when(core[0] == 0)
    def _():
        score(kept, came)

    @pl.when(core[0] == 1)
    def _():
        score(came, kept)

    @pl.when(step == PD // 16 - 1)
    def _():
        out[...] = found[...].T[0:1, 0:PD]


def scores(core, kept, came, norm):
    return pl.pallas_call(
        score_kernel,
        grid_spec=pltpu.PrefetchScalarGridSpec(
            num_scalar_prefetch=1,
            grid=(PD // 16,),
            in_specs=[
                pl.BlockSpec((UNITS, 16, KPAD), lambda i, core: (0, i, 0)),
                pl.BlockSpec((UNITS, 16, KPAD), lambda i, core: (0, i, 0)),
                pl.BlockSpec((16, KPAD), lambda i, core: (i, 0)),
            ],
            out_specs=whole((1, PD)),
            scratch_shapes=[pltpu.VMEM((PD, 128), F32)],
        ),
        out_shape=jax.ShapeDtypeStruct((1, PD), F32),
        compiler_params=pltpu.CompilerParams(vmem_limit_bytes=VMEM_BYTES),
        cost_estimate=pl.CostEstimate(
            flops=3000000000, bytes_accessed=9000000, transcendentals=0
        ),
        name="scores",
    )(core, kept, came, norm)


def class_sum_kernel(arrived, out, last):
    labels = arrived[:, 18 * PD : 19 * PD, :].astype(F32).reshape(DOM * PD, 128)
    block = labels[:, 16:17]
    local = labels[:, 17:18]
    row = jnp.where(local < 23.5, block * 24.0 + local, block + 384.0)
    lane = lax.broadcasted_iota(jnp.int32, (DOM * PD, KPAD), 1).astype(F32)
    hits = jnp.where(lane == row, 1.0, 0.0).T[0 : OWN * KD].astype(BF16)
    last[...] = jnp.zeros_like(last)
    for pair in range(10):
        pieces = [2 * pair, 2 * pair + 1] if pair < 9 else [18]
        right = jnp.concatenate(
            [arrived[:, c * PD : c * PD + PD, :].reshape(DOM * PD, 128) for c in pieces], axis=1
        )
        total = jnp.dot(hits, right, preferred_element_type=F32)
        sums = [total[:, i * 128 : i * 128 + 128] for i in range(len(pieces))]
        for place, value in zip(pieces, sums):
            last[pl.ds(24 + place, OWN, stride=48), :] = value[OWN * 24 :]
        if pair < 9:
            both = jnp.concatenate(
                [value[0 : OWN * 24].reshape(OWN, 24, 128) for value in sums], axis=1
            )
            out[:, pair * 48 : pair * 48 + 48, :] = both.astype(BF16)
        else:
            for owner in range(OWN):
                last[owner * 48 : owner * 48 + 24, :] = sums[0][owner * 24 : owner * 24 + 24]
    out[:, 432:480, :] = last[...].reshape(OWN, 48, 128).astype(BF16)


def class_sums(arrived):
    return pl.pallas_call(
        class_sum_kernel,
        in_specs=[pl.BlockSpec(memory_space=pltpu.VMEM)],
        out_specs=pl.BlockSpec(memory_space=pltpu.VMEM),
        scratch_shapes=[pltpu.VMEM((OWN * 48, 128), F32)],
        out_shape=jax.ShapeDtypeStruct((OWN, SROWS, 128), BF16),
        compiler_params=pltpu.CompilerParams(vmem_limit_bytes=VMEM_BYTES // 2),
        cost_estimate=pl.CostEstimate(
            flops=3000000000, bytes_accessed=9000000, transcendentals=0
        ),
        name="class_sums",
    )(arrived)


def average_kernel(dom, arrived, squares, out, left, middle, right):
    total = arrived[0].astype(F32)
    for source in range(1, OWN):
        total = total + arrived[source].astype(F32)
    counts = jnp.concatenate([total[432:456], total[472:480]], axis=0)
    below = jnp.dot(counts, squares[0], precision=lax.Precision.HIGHEST, preferred_element_type=F32)
    below = below + 1.0
    for cycle in range(BAND):
        usual = below[0:24, cycle : cycle + 1]
        final = below[26:27, cycle : cycle + 1]
        for tile, target in ((0, left), (1, middle), (2, right)):
            if tile < 2:
                piece, turn = cycle * 2 + tile, 0
            else:
                piece, turn = 16 + cycle // 4, (128 - cycle % 4 * 32) % 128
            value = total[piece * 24 : piece * 24 + 24] / usual
            end = total[456 + piece : 457 + piece] / final
            if turn:
                value = pltpu.roll(value, turn, 1)
                end = pltpu.roll(end, turn, 1)
            target[pl.ds(cycle, 24, stride=BAND), :] = value
            target[24 * BAND + cycle : 24 * BAND + cycle + 1, :] = end
    out[:, 0:128] = left[...]
    out[:, 128:256] = middle[...]
    out[:, 256:288] = right[:, 0:32]


def averages(dom, arrived):
    ctf = ctf_values()
    squares = np.zeros((DOM, 128, 128), np.float32)
    for band in range(DOM):
        squares[band, :NBINS, :BAND] = (ctf * ctf)[:, band * BAND : band * BAND + BAND]
    return pl.pallas_call(
        average_kernel,
        grid_spec=pltpu.PrefetchScalarGridSpec(
            num_scalar_prefetch=1,
            grid=(1,),
            in_specs=[
                whole((OWN, SROWS, 128)),
                pl.BlockSpec((1, 128, 128), lambda i, dom: (dom[0], 0, 0)),
            ],
            out_specs=whole((KD * BAND, ROW)),
            scratch_shapes=[pltpu.VMEM((KD * BAND, 128), F32)] * 3,
        ),
        out_shape=jax.ShapeDtypeStruct((KD * BAND, ROW), F32),
        compiler_params=pltpu.CompilerParams(vmem_limit_bytes=VMEM_BYTES),
        cost_estimate=pl.CostEstimate(
            flops=2000000000, bytes_accessed=6000000, transcendentals=0
        ),
        name="averages",
    )(dom, arrived, jnp.asarray(squares))


def on_device(particles, references, class_block, class_local, rotation, shifts, defocus):
    dom = lax.axis_index("dom").astype(jnp.int32).reshape(1)
    core = dom % 2
    full_table, split_table = dft_rows()
    table = jnp.asarray(split_table)
    block = own_harmonics(core, references, table)
    scalars = jnp.stack(
        [shifts[:, 0], shifts[:, 1], defocus, rotation, class_block[:, 0], class_local], axis=0
    )
    rows = particles.reshape(PD * CYC, ROW)

    def spread_of(*blocks):
        *blocks, held = lax.optimization_barrier((*blocks, scalars))
        return *blocks, spread_bands(rows, held, full_table)

    gathered, joined, sums = gather_blocks(block, spread_of)
    late_scalars, _ = lax.optimization_barrier((scalars, joined))
    own, other = weighted_spectra(core, rows, late_scalars, table)
    swap = [(i, i ^ 1) for i in range(DOM)]
    far = lax.ppermute(other, "dom", swap)
    sums = lax.all_to_all(sums, "cls", 0, 0, tiled=True)
    class_average = averages(dom, sums).reshape(KD, BAND, ROW)
    kept, sent, norm = fold(core, gathered, own, far, defocus)
    came = lax.ppermute(sent, "dom", swap)
    best_score = scores(core, kept, came, norm).reshape(PD)
    return (best_score, class_average)


def solution(mesh):
    placed = (
        P(("dom", "cls"), None, None),
        P("cls", None, None),
        P(("dom", "cls"), None),
        P(("dom", "cls")),
        P(("dom", "cls")),
        P(("dom", "cls"), None),
        P(("dom", "cls")),
    )
    return jax.shard_map(
        on_device,
        mesh=mesh,
        in_specs=placed,
        out_specs=(P(("dom", "cls")), P("cls", "dom", None)),
        check_vma=False,
    )
```

```python
import functools
import math

import jax
import jax.numpy as jnp
import ml_dtypes
import numpy as np
from jax import lax
from jax.experimental import pallas as pl
from jax.experimental.pallas import tpu as pltpu
from jax.sharding import PartitionSpec as P

ROT = 36
BOX = 128
NBINS = 16
EPSILON = 1e-06
CYC = 64
ANG = 144
ROW = 2 * ANG
SHIFT = 5
PD = 48
KD = 25
OWN = 16
DOM = 8
BAND = CYC // DOM
UNITS = 18
HALF = UNITS // 2
MH = HALF * 8
HEAD = 192
NORM0 = 96
HROWS = HEAD + MH * 24
HH = 40
MP = 2 * HH
CHUNKS = 19
UROWS = CHUNKS * PD
SROWS = 480
KPAD = 512
STEP = 16
F32 = jnp.float32
BF16 = jnp.bfloat16
VMEM_BYTES = 58 * 1024 * 1024
NT = (((1,), (1,)), ((), ()))


def unit_harmonics():
    rows = []
    for unit in range(UNITS):
        plus, minus = (0, 18) if unit == 0 else (unit, ROT - unit)
        rows.append([plus + ROT * q for q in range(4)] + [minus + ROT * q for q in range(4)])
    return np.array(rows).reshape(2, MH)


def dft_rows():
    turn = np.arange(ANG)[:, None] * np.arange(ANG)[None, :] % ANG
    angle = turn.astype(np.float32) * np.float32(2.0 * math.pi / ANG)
    cosine = np.cos(angle.astype(np.float64))
    sine = np.sin(angle.astype(np.float64))
    upper = np.concatenate([cosine, -sine], axis=1)
    lower = np.concatenate([sine, cosine], axis=1)
    full = np.concatenate([upper, lower], axis=0).astype(np.float32).astype(ml_dtypes.bfloat16)
    halves = unit_harmonics()
    split = []
    for core in range(2):
        mine, other = halves[core], halves[1 - core]
        rows = np.zeros((4 * MP, ROW), ml_dtypes.bfloat16)
        for index, columns in enumerate((mine, ANG + mine, other, ANG + other)):
            for parity in range(2):
                start = index * MP + parity * HH
                rows[start : start + MH // 2] = full[:, columns[parity::2]].T
        split.append(rows)
    return full, np.stack(split)


def wide_columns(full):
    order = np.concatenate([np.arange(256)] + [np.arange(256, 288)] * 4)
    swapped = np.concatenate([-full[:, ANG:], full[:, :ANG]], axis=1)
    return np.concatenate([full[:, order], swapped[:, order]], axis=1), order


def turn_rows(order):
    harmonic = order % ANG
    turn = np.arange(ROT)[:, None] * 4 * harmonic[None, :] % ANG
    angle = turn * (2.0 * math.pi / ANG)
    angle = angle.reshape(ROT, 3, 128)
    rest = np.zeros((ROT, 2, 128))
    return np.concatenate([np.cos(angle), np.sin(angle), rest], axis=1).astype(np.float32)


def ctf_values():
    radius = (np.arange(CYC) + 1) / CYC
    level = np.arange(NBINS) / NBINS
    phase = math.pi * (3.0 + 9.0 * level[:, None]) * (radius * radius)[None, :]
    return 0.995 * np.sin(phase) + 0.1 * np.cos(phase)


def shift_rows():
    angle = np.arange(ANG) * (2.0 * math.pi / ANG)
    scale = 2.0 * math.pi / BOX * np.concatenate([np.arange(8), 8 * np.arange(8)])
    size = np.arange(SHIFT + 1)
    out = []
    for beam in (np.cos(angle), np.sin(angle)):
        phase = size[:, None, None] * scale[None, :, None] * beam[None, None, :]
        phase = np.concatenate([phase, phase], axis=2)
        out += [np.cos(phase), np.sin(phase)]
    return np.stack(out).astype(np.float32)


def swap_matrix():
    swap = np.zeros((ROW, ROW), np.float32)
    index = np.arange(ANG)
    swap[ANG + index, index] = -1.0
    swap[index, ANG + index] = 1.0
    return swap.astype(ml_dtypes.bfloat16)


def pair_signs():
    signs = np.zeros((2, 3, MH, 128), np.float32)
    for core in range(2):
        for row in range(MH):
            unit, place = core * HALF + row // 8, row % 8
            if unit == 0:
                signs[core, 0 if place < 4 else 1, row] = 1.0
            else:
                signs[core, 0, row] = 1.0
                flip = 1.0 if place < 4 else -1.0
                signs[core, 2, row, :64] = -flip
                signs[core, 2, row, 64:] = flip
    signs = np.pad(signs.transpose(0, 2, 1, 3), ((0, 0), (0, 0), (0, 5), (0, 0)))
    return signs


def whole(shape):
    return pl.BlockSpec(shape, lambda *_: (0,) * len(shape))


def merge_halves(real, imag, low):
    first = jnp.where(low, real, pltpu.roll(imag, 64, 1))
    second = jnp.where(low, pltpu.roll(real, 64, 1), imag)
    return first, second


def harmonics_kernel(
    core, refs_any, table_any, squares_any, out, refs, table, squares, scratch, energy, norms, sems
):
    copies = [pltpu.make_async_copy(table_any.at[core[0]], table, sems.at[0])]
    for index in range(4):
        chunk = pl.ds(index * 512, 512 if index < 3 else 64)
        copies.append(
            pltpu.make_async_copy(refs_any.at[chunk, :], refs.at[chunk, :], sems.at[index + 1])
        )
    copies.append(pltpu.make_async_copy(squares_any, squares, sems.at[5]))
    for copy in copies:
        copy.start()
    scratch[0:HEAD, :] = jnp.zeros((HEAD, 128), F32)
    energy[...] = jnp.zeros_like(energy)
    low = lax.broadcasted_iota(jnp.int32, (MP, 128), 1) < 64
    copies[0].wait()
    rows = table[...]

    def place(klass, value):
        if klass == 24:
            scratch[0:MP, :] = value
            return
        for parity in range(2):
            start = HEAD + (parity * 16 + klass if klass < 16 else 16 + parity * 8 + klass)
            piece = value[parity * HH : parity * HH + MH // 2]
            scratch[pl.ds(start, MH // 2, stride=48), :] = piece

    for group in range(7):
        start, width = (group * 256, 256) if group < 6 else (KD * CYC - 128, 128)
        if group % 2 == 0:
            copies[1 + group // 2].wait()
        full = lax.dot_general(rows, refs[start : start + width, :], NT, preferred_element_type=F32)
        kept = full.astype(BF16).astype(F32)
        total = jnp.sum(kept * kept, axis=0, keepdims=True)
        if group < 6:
            energy[group : group + 1, :] = total
        else:
            energy[group : group + 1, 0:128] = jnp.where(low[0:1], pltpu.roll(total, 64, 1), 0.0)
        for pair in range(width // 128):
            lanes = slice(pair * 128, pair * 128 + 128)
            first, second = merge_halves(full[0:MP, lanes], full[MP : 2 * MP, lanes], low)
            if group < 6:
                place(group * 4 + pair * 2, first)
                place(group * 4 + pair * 2 + 1, second)
            else:
                place(24, second)
    copies[5].wait()
    for sub in range(4):
        lanes = slice(sub // 2 * 128, sub // 2 * 128 + 128)
        power = jnp.dot(
            energy[:, lanes],
            squares[sub % 2],
            precision=lax.Precision.HIGHEST,
            preferred_element_type=F32,
        )
        norms[pl.ds(sub, 8, stride=4), :] = power
    scale = (1.0 / ANG) / jnp.sqrt(norms[...] * (1.0 / ANG) + EPSILON)
    scale = jnp.where(lax.broadcasted_iota(jnp.int32, (32, 128), 1) < NBINS, scale, 0.0)
    high = scale.astype(BF16).astype(F32)
    scratch[NORM0 : NORM0 + 32, :] = high + pltpu.roll(scale - high, NBINS, 1)
    out[...] = scratch[...].astype(BF16)


def own_harmonics(core, references, table):
    squares = np.zeros((2, 128, 128), np.float32)
    ctf = ctf_values()
    for sub in range(2):
        squares[sub, 64 * sub : 64 * sub + 64, :NBINS] = (ctf * ctf).T
    return pl.pallas_call(
        harmonics_kernel,
        in_specs=[
            pl.BlockSpec(memory_space=pltpu.SMEM),
            pl.BlockSpec(memory_space=pl.ANY),
            pl.BlockSpec(memory_space=pl.ANY),
            pl.BlockSpec(memory_space=pl.ANY),
        ],
        out_specs=pl.BlockSpec(memory_space=pltpu.VMEM),
        scratch_shapes=[
            pltpu.VMEM((KD * CYC, ROW), BF16),
            pltpu.VMEM((4 * MP, ROW), BF16),
            pltpu.VMEM((2, 128, 128), F32),
            pltpu.VMEM((HROWS, 128), F32),
            pltpu.VMEM((8, 256), F32),
            pltpu.VMEM((32, 128), F32),
            pltpu.SemaphoreType.DMA((6,)),
        ],
        out_shape=jax.ShapeDtypeStruct((HROWS, 128), BF16),
        compiler_params=pltpu.CompilerParams(vmem_limit_bytes=VMEM_BYTES),
        cost_estimate=pl.CostEstimate(
            flops=4000000000, bytes_accessed=12000000, transcendentals=0
        ),
        name="harmonics",
    )(core, references.reshape(KD * CYC, ROW), table, jnp.asarray(squares))


def shift_group(scalars, first, data, swap, phases):
    crossed = jnp.dot(data, swap, preferred_element_type=F32)
    shifted = []
    for sub in range(4):
        move_x = scalars[0, first + sub]
        move_y = scalars[1, first + sub]
        sign_x = jnp.where(move_x < 0, -1.0, 1.0)
        sign_y = jnp.where(move_y < 0, -1.0, 1.0)
        size_x = jnp.abs(move_x)
        size_y = jnp.abs(move_y)
        cos_x = phases[0, size_x]
        sin_x = phases[1, size_x] * sign_x
        cos_y = phases[2, size_y]
        sin_y = phases[3, size_y] * sign_y
        cosine = cos_x * cos_y - sin_x * sin_y
        sine = sin_x * cos_y + cos_x * sin_y
        near_cos, near_sin = cosine[0:8], sine[0:8]
        for jump in range(8):
            far_cos = cosine[8 + jump : 9 + jump]
            far_sin = sine[8 + jump : 9 + jump]
            rows = slice(sub * CYC + jump * 8, sub * CYC + jump * 8 + 8)
            value = data[rows].astype(F32) * (near_cos * far_cos - near_sin * far_sin)
            value = value + crossed[rows] * (near_sin * far_cos + near_cos * far_sin)
            shifted.append(value)
    return jnp.concatenate(shifted, axis=0).astype(BF16)


def spread_kernel(scalars, parts, wide, swap, phases, turn, ctf_columns, spread, turned, tails):
    step = pl.program_id(0)
    lane = lax.broadcasted_iota(jnp.int32, (1, 128), 1)
    group = lax.broadcasted_iota(jnp.int32, (16, 128), 1) // 32

    def one_group(quad, carry):
        first = step * STEP + quad * 4
        start = pl.multiple_of(quad * 256, 256)
        data = parts[pl.ds(start, 256), :]
        shifted = shift_group(scalars, first, data, swap[...], phases)
        natural = jnp.dot(shifted, wide[...], preferred_element_type=F32)
        for sub in range(4):
            index = first + sub
            rows = slice(sub * CYC, sub * CYC + CYC)
            angles = turn[scalars[3, index]]
            chosen = jnp.where(lane == scalars[2, index], ctf_columns[...], 0.0)
            contrast = jnp.sum(chosen, axis=1, keepdims=True)
            for tile in range(3):
                lanes = slice(tile * 128, tile * 128 + 128)
                cos_rot = angles[tile : tile + 1, :]
                sin_rot = angles[tile + 3 : tile + 4, :]
                there = slice(384 + tile * 128, 384 + tile * 128 + 128)
                value = natural[rows, lanes] * cos_rot + natural[rows, there] * sin_rot
                value = contrast * value
                if tile < 2:
                    for band in range(DOM):
                        begin = band * UROWS + tile * PD + index
                        piece = value[band * BAND : band * BAND + BAND]
                        turned[pl.ds(begin, BAND, stride=2 * PD), :] = piece
                else:
                    tails[sub] = value
                    packed = tails[sub, pl.ds(0, 16, stride=4), :]
                    for place in range(1, 4):
                        other = tails[sub, pl.ds(place, 16, stride=4), :]
                        packed = jnp.where(group == place, other, packed)
                    tails[sub, 0:16, :] = packed
                    for half in range(2):
                        piece = tails[sub, pl.ds(half, DOM, stride=2), :]
                        turned[pl.ds((16 + half) * PD + index, DOM, stride=UROWS), :] = piece
            label = jnp.where(lane == scalars[2, index], 1.0, 0.0)
            label = jnp.where(lane == 16, scalars[4, index].astype(F32), label)
            label = jnp.where(lane == 17, scalars[5, index].astype(F32), label)
            label = jnp.broadcast_to(label, (DOM, 128))
            turned[pl.ds(18 * PD + index, DOM, stride=UROWS), :] = label
        return carry

    lax.fori_loop(0, STEP // 4, one_group, 0, unroll=True)

    @pl.when(step == PD // STEP - 1)
    def _():
        spread[...] = turned[...].astype(BF16)


def spread_bands(particles, scalars, full_table):
    wide, order = wide_columns(full_table)
    ctf_columns = np.zeros((CYC, 128), np.float32)
    ctf_columns[:, :NBINS] = ctf_values().T
    return pl.pallas_call(
        spread_kernel,
        grid_spec=pltpu.PrefetchScalarGridSpec(
            num_scalar_prefetch=1,
            grid=(PD // STEP,),
            in_specs=[
                pl.BlockSpec((STEP * CYC, ROW), lambda i, sc: (i, 0)),
                whole((ROW, 768)),
                whole((ROW, ROW)),
                whole((4, SHIFT + 1, 16, ROW)),
                whole((ROT, 8, 128)),
                whole((CYC, 128)),
            ],
            out_specs=whole((DOM * UROWS, 128)),
            scratch_shapes=[
                pltpu.VMEM((DOM * UROWS, 128), F32),
                pltpu.VMEM((4, CYC, 128), F32),
            ],
        ),
        out_shape=jax.ShapeDtypeStruct((DOM * UROWS, 128), BF16),
        compiler_params=pltpu.CompilerParams(vmem_limit_bytes=VMEM_BYTES // 2),
        cost_estimate=pl.CostEstimate(
            flops=9000000000, bytes_accessed=27000000, transcendentals=0
        ),
        name="spread",
    )(
        scalars,
        particles,
        jnp.asarray(wide),
        jnp.asarray(swap_matrix()),
        jnp.asarray(shift_rows()),
        jnp.asarray(turn_rows(order)),
        jnp.asarray(ctf_columns),
    )


def weight_kernel(core, scalars, parts, table, swap, phases, ctf_rows, mine, other, weighted):
    step = pl.program_id(0)
    low = lax.broadcasted_iota(jnp.int32, (MP, 128), 1) < 64

    def one_group(quad, carry):
        first = step * STEP + quad * 4
        start = pl.multiple_of(quad * 256, 256)
        data = parts[pl.ds(start, 256), :]
        shifted = shift_group(scalars, first, data, swap[...], phases)
        full = lax.dot_general(table[0], shifted, NT, preferred_element_type=F32)
        for pair in range(2):
            lanes = slice(pair * 128, pair * 128 + 128)
            for side in range(2):
                base = side * 2 * MP
                both = merge_halves(
                    full[base : base + MP, lanes], full[base + MP : base + 2 * MP, lanes], low
                )
                for which in range(2):
                    index = first + pair * 2 + which
                    contrast = ctf_rows[pl.ds(scalars[2, index], 1), :]
                    value = both[which] * contrast
                    for parity in range(2):
                        begin = (side * MH + parity) * PD + index
                        piece = value[parity * HH : parity * HH + MH // 2]
                        weighted[pl.ds(begin, MH // 2, stride=2 * PD), :] = piece
        return carry

    lax.fori_loop(0, STEP // 4, one_group, 0, unroll=True)

    @pl.when(step == PD // STEP - 1)
    def _():
        mine[...] = weighted[0 : MH * PD, :].astype(BF16)
        other[...] = weighted[MH * PD :, :].astype(BF16)


def weighted_spectra(core, particles, scalars, table):
    ctf = ctf_values().astype(np.float32)
    half_shape = jax.ShapeDtypeStruct((MH * PD, 128), BF16)
    return pl.pallas_call(
        weight_kernel,
        grid_spec=pltpu.PrefetchScalarGridSpec(
            num_scalar_prefetch=2,
            grid=(PD // STEP,),
            in_specs=[
                pl.BlockSpec((STEP * CYC, ROW), lambda i, core, sc: (i, 0)),
                pl.BlockSpec((1, 4 * MP, ROW), lambda i, core, sc: (core[0], 0, 0)),
                whole((ROW, ROW)),
                whole((4, SHIFT + 1, 16, ROW)),
                whole((NBINS, 128)),
            ],
            out_specs=[whole((MH * PD, 128)), whole((MH * PD, 128))],
            scratch_shapes=[pltpu.VMEM((2 * MH * PD, 128), F32)],
        ),
        out_shape=[half_shape, half_shape],
        compiler_params=pltpu.CompilerParams(vmem_limit_bytes=VMEM_BYTES // 2),
        cost_estimate=pl.CostEstimate(
            flops=10000000000, bytes_accessed=30000000, transcendentals=0
        ),
        name="weights",
    )(
        core,
        scalars,
        particles,
        table,
        jnp.asarray(swap_matrix()),
        jnp.asarray(shift_rows()),
        jnp.asarray(np.concatenate([ctf, ctf], axis=1)),
    )


def fold_kernel(layout, count, core, *refs):
    pieces = refs[:count]
    own, far, signs, bins, kept_out, sent_out, norm = refs[count : count + 7]
    kept, sent, blocks, held, last, scale_rows, arrivals, leaving = refs[count + 7 :]
    copies = []
    for index, (slot, start, rows, first) in enumerate(layout):
        source = pieces[index].at[pl.ds(first, rows), :]
        target = blocks.at[slot, pl.ds(start, rows), :]
        copies.append(pltpu.make_async_copy(source, target, arrivals.at[index]))
    for copy in copies:
        copy.start()
    held[OWN * KD :, :] = jnp.zeros((KPAD - OWN * KD, 1024), BF16)
    scale_rows[...] = jnp.zeros_like(scale_rows)
    lane = lax.broadcasted_iota(jnp.int32, (PD, 128), 1)
    row = lax.broadcasted_iota(jnp.int32, (PD, 128), 0)
    level = jnp.zeros((PD, 128), jnp.int32)
    for index in range(PD):
        level = jnp.where(row == index, bins[index], level)
    hits = jnp.where((lane == level) | (lane == level + NBINS), 1.0, 0.0).astype(BF16)

    def outgoing(unit):
        both = pl.ds(2 * unit, 2)
        return (
            pltpu.make_async_copy(sent.at[both], sent_out.at[both], leaving.at[unit, 0]),
            pltpu.make_async_copy(kept.at[both], kept_out.at[both], leaving.at[unit, 1]),
        )

    def one_unit(unit, carry):
        parts_a, parts_b = [], []
        for place in range(8):
            harmonic = unit * 8 + place
            row = jnp.concatenate([own[harmonic], far[harmonic]], axis=0).astype(F32)
            factor = signs[core[0], harmonic]
            parts_a.append((row * factor[0:1]).astype(BF16))
            swapped = pltpu.roll(row, 64, 1) * factor[2:3]
            parts_b.append((row * factor[1:2] + swapped).astype(BF16))
        left = jnp.concatenate(
            [jnp.concatenate(parts_a, axis=1), jnp.concatenate(parts_b, axis=1)], axis=0
        )
        for pair in range(4):
            start = pl.multiple_of(HEAD + unit * 192 + pair * 48, 16)
            for parity in range(2):
                place = pair * 2 + parity
                lanes = slice(place * 128, place * 128 + 128)
                for slot in range(OWN):
                    held[slot * 16 : slot * 16 + 16, lanes] = blocks[
                        slot, pl.ds(start + parity * 16, 16), :
                    ]
                begin = pl.multiple_of((parity * HH + unit * 4 + pair) * OWN, OWN)
                held[OWN * 24 : OWN * KD, lanes] = last[pl.ds(begin, OWN), :].astype(BF16)
            for slot in range(0, OWN, 2):
                one = blocks[slot, pl.ds(start + 32, 16), :].astype(F32)
                two = blocks[slot + 1, pl.ds(start + 32, 16), :].astype(F32)
                for parity in range(2):
                    place = pair * 2 + parity
                    lanes = slice(place * 128, place * 128 + 128)
                    rows = slice(parity * 8, parity * 8 + 8)
                    both = jnp.concatenate([one[rows], two[rows]], axis=0).astype(BF16)
                    held[256 + slot * 8 : 256 + slot * 8 + 16, lanes] = both
        folded = lax.dot_general(left, held[...], NT, preferred_element_type=F32).astype(BF16)
        kept[2 * unit] = folded[0:PD]
        sent[2 * unit] = folded[PD : 2 * PD]
        kept[2 * unit + 1] = folded[2 * PD : 3 * PD]
        sent[2 * unit + 1] = folded[3 * PD : 4 * PD]
        for copy in outgoing(unit):
            copy.start()
        return carry

    for copy, (slot, start, rows, first) in zip(copies, layout):
        if start < HROWS // 2:
            copy.wait()
    for slot in range(OWN):
        last[pl.ds(slot, MP, stride=OWN), :] = blocks[slot, 0:MP, :].astype(F32)
        scales = blocks[slot, NORM0 : NORM0 + 32, :].astype(F32)
        scale_rows[slot * 16 : slot * 16 + 16, :] = scales[0:16]
        scale_rows[256 + slot * 8 : 256 + slot * 8 + 8, :] = scales[16:24]
        scale_rows[OWN * 24 + slot : OWN * 24 + slot + 1, :] = scales[24:25]
    table = scale_rows[...].astype(BF16)
    norm[...] = lax.dot_general(hits, table, NT, preferred_element_type=F32)
    lax.fori_loop(0, 4, one_unit, 0, unroll=True)
    for copy, (slot, start, rows, first) in zip(copies, layout):
        if start >= HROWS // 2:
            copy.wait()
    lax.fori_loop(4, HALF, one_unit, 0, unroll=True)
    for unit in range(HALF):
        for copy in outgoing(unit):
            copy.wait()


def fold(core, arrived, own, far, bins):
    layout = tuple((slot, start, rows, first) for slot, start, rows, first, _ in arrived)
    count = len(layout)
    piece = jax.ShapeDtypeStruct((UNITS, PD, KPAD), BF16)
    vmem = pl.BlockSpec(memory_space=pltpu.VMEM)
    return pl.pallas_call(
        functools.partial(fold_kernel, layout, count),
        in_specs=[pl.BlockSpec(memory_space=pltpu.SMEM)]
        + [pl.BlockSpec(memory_space=pl.ANY)] * count
        + [vmem] * 3
        + [pl.BlockSpec(memory_space=pltpu.SMEM)],
        out_specs=[pl.BlockSpec(memory_space=pl.ANY)] * 2 + [vmem],
        scratch_shapes=[
            pltpu.VMEM((UNITS, PD, KPAD), BF16),
            pltpu.VMEM((UNITS, PD, KPAD), BF16),
            pltpu.VMEM((OWN, HROWS, 128), BF16),
            pltpu.VMEM((KPAD, 1024), BF16),
            pltpu.VMEM((MP * OWN, 128), F32),
            pltpu.VMEM((KPAD, 128), F32),
            pltpu.SemaphoreType.DMA((count,)),
            pltpu.SemaphoreType.DMA((HALF, 2)),
        ],
        out_shape=[piece, piece, jax.ShapeDtypeStruct((PD, KPAD), F32)],
        compiler_params=pltpu.CompilerParams(vmem_limit_bytes=VMEM_BYTES),
        cost_estimate=pl.CostEstimate(
            flops=9000000000, bytes_accessed=27000000, transcendentals=0
        ),
        name="fold",
    )(
        core,
        *[value for *_, value in arrived],
        own.reshape(MH, PD, 128),
        far.reshape(MH, PD, 128),
        jnp.asarray(pair_signs()),
        bins,
    )


def moved_by(value, along_x, along_z):
    moves = [
        (x * 4 + z, (x + along_x) % 4 * 4 + (z + along_z) % 4) for x in range(4) for z in range(4)
    ]
    return lax.ppermute(value, "cls", moves)


def join_kernel(left, right, two_x, down, up, two_z, low, high, held, sems):
    half = HROWS // 2
    inward, outward = [], []
    for index, source in enumerate((left, right, two_x, down, up, two_z)):
        first = 0 if index < 3 else half
        target = (low if index < 3 else high).at[pl.ds(index % 3 * half, half), :]
        inward.append(
            pltpu.make_async_copy(source.at[pl.ds(first, half), :], held.at[index], sems.at[index])
        )
        outward.append(pltpu.make_async_copy(held.at[index], target, sems.at[6 + index]))
    for copy in inward:
        copy.start()
    for come, go in zip(inward, outward):
        come.wait()
        go.start()
    for copy in outward:
        copy.wait()


def join(*blocks):
    anywhere = pl.BlockSpec(memory_space=pl.ANY)
    rows = jax.ShapeDtypeStruct((3 * HROWS // 2, 128), BF16)
    return pl.pallas_call(
        join_kernel,
        in_specs=[anywhere] * 6,
        out_specs=[anywhere] * 2,
        scratch_shapes=[
            pltpu.VMEM((6, HROWS // 2, 128), BF16),
            pltpu.SemaphoreType.DMA((12,)),
        ],
        out_shape=[rows, rows],
        compiler_params=pltpu.CompilerParams(vmem_limit_bytes=VMEM_BYTES),
        cost_estimate=pl.CostEstimate(
            flops=2000000000, bytes_accessed=6000000, transcendentals=0
        ),
        name="join",
    )(*blocks)


def cut_kernel(low_before, low_after, high_before, high_after, *refs):
    outs, held, sems = refs[:4], refs[4], refs[5]
    part = 3 * HROWS // 4
    inward, outward = [], []
    for index, source in enumerate((low_before, low_after, high_before, high_after)):
        chunk = pl.ds(index % 2 * part, part)
        inward.append(pltpu.make_async_copy(source.at[chunk, :], held.at[index], sems.at[index]))
        outward.append(pltpu.make_async_copy(held.at[index], outs[index], sems.at[4 + index]))
    for copy in inward:
        copy.start()
    for come, go in zip(inward, outward):
        come.wait()
        go.start()
    for copy in outward:
        copy.wait()


def cut(*rows):
    anywhere = pl.BlockSpec(memory_space=pl.ANY)
    part = jax.ShapeDtypeStruct((3 * HROWS // 4, 128), BF16)
    return pl.pallas_call(
        cut_kernel,
        in_specs=[anywhere] * 4,
        out_specs=[anywhere] * 4,
        scratch_shapes=[
            pltpu.VMEM((4, 3 * HROWS // 4, 128), BF16),
            pltpu.SemaphoreType.DMA((8,)),
        ],
        out_shape=[part] * 4,
        compiler_params=pltpu.CompilerParams(vmem_limit_bytes=VMEM_BYTES),
        cost_estimate=pl.CostEstimate(
            flops=2000000000, bytes_accessed=6000000, transcendentals=0
        ),
        name="cut",
    )(*rows)


def gather_blocks(block, spread_of):
    half, part = HROWS // 2, 3 * HROWS // 4
    steps = (-1, 1, 2)
    by_x = [moved_by(block, -step, 0) for step in steps]
    by_z = [moved_by(block, 0, -step) for step in steps]
    by_x[2], spread = spread_of(by_x[2])
    low_rows, high_rows = join(*by_x, *by_z)
    low_far = [moved_by(low_rows, 0, 1), moved_by(low_rows, 0, -1)]
    high_far = [moved_by(high_rows, 1, 0), moved_by(high_rows, -1, 0)]
    arrived = lax.all_to_all(spread.reshape(DOM, UROWS, 128), "dom", 0, 0, tiled=True)
    sums = class_sums(arrived)
    low_far, high_far, sums = lax.optimization_barrier((low_far, high_far, sums))
    parts = cut(*low_far, *high_far)
    low_two = moved_by(parts[0], 0, 1), moved_by(parts[1], 0, -1)
    high_two = moved_by(parts[2], 1, 0), moved_by(parts[3], -1, 0)

    def slot(x, z):
        return x % 4 * 4 + z % 4

    pieces = []
    for start in (0, half):
        pieces.append((slot(0, 0), start, half, start, block))
        pieces += [(slot(step, 0), start, half, start, by_x[i]) for i, step in enumerate(steps)]
        pieces += [(slot(0, step), start, half, start, by_z[i]) for i, step in enumerate(steps)]
        near, two = (low_far, low_two) if start == 0 else (high_far, high_two)
        for j, inner in enumerate(steps):
            for i, outer in enumerate(steps[:2]):
                place = slot(inner, outer) if start == 0 else slot(outer, inner)
                pieces.append((place, start, half, j * half, near[i]))
            place = slot(inner, 2) if start == 0 else slot(2, inner)
            for i in range(2):
                first = max(j * half, i * part)
                last = min(j * half + half, i * part + part)
                if first < last:
                    begin = start + first - j * half
                    pieces.append((place, begin, last - first, first - i * part, two[i]))
    return pieces, low_rows, sums


def weigh(total, coefficient, value):
    if abs(coefficient) < 1e-12:
        return total
    if abs(coefficient - 1.0) < 1e-12:
        return value if total is None else total + value
    if abs(coefficient + 1.0) < 1e-12:
        return -value if total is None else total - value
    term = value * coefficient
    return term if total is None else total + term


def best_rotation(cosines, sines):
    best = None
    for parity in range(2):
        sign = 1.0 if parity == 0 else -1.0
        even = {0: cosines[0] + sign * cosines[18]}
        odd = {}
        for unit in range(1, 9):
            even[unit] = cosines[unit] + sign * cosines[18 - unit]
            odd[unit] = sines[unit] - sign * sines[18 - unit]
        even[9] = cosines[9]
        odd[9] = sines[9]
        for rotation in range(parity, 10, 2):
            sums = {}
            for name, values, wave in (("e", even, math.cos), ("o", odd, math.sin)):
                for rest in range(2):
                    total = None
                    for unit, value in values.items():
                        if unit % 2 == rest:
                            angle = math.pi * ((unit * rotation) % 36) / 18.0
                            total = weigh(total, wave(angle), value)
                    sums[name, rest] = total

            def joined(first, second, flip):
                if first is None and second is None:
                    return None
                if second is None:
                    return first
                if first is None:
                    return second
                return first - second if flip else first + second

            for flip in (False, True) if rotation < 9 else (False,):
                value = joined(sums["e", 0], sums["e", 1], flip)
                swing = joined(sums["o", 1], sums["o", 0], flip)
                if swing is not None:
                    value = value + jnp.abs(swing)
                best = value if best is None else jnp.maximum(best, value)
    return best


def score_kernel(core, kept, came, norm, out, found):
    step = pl.program_id(0)

    def score(low, high):
        for block in range(2):
            rows = slice(block * 8, block * 8 + 8)
            every = slice(0, 16)
            best = None
            for tile in range(KPAD // 128):
                lanes = slice(tile * 128, tile * 128 + 128)
                cosines, sines = {}, {}
                for unit in range(UNITS):
                    source = low if unit < HALF else high
                    place = unit % HALF * 2
                    cosines[unit] = source[place, every, lanes].astype(F32)[rows]
                    sines[unit] = source[place + 1, every, lanes].astype(F32)[rows]
                cosines[18] = sines[0]
                value = best_rotation(cosines, sines) * norm[rows, lanes]
                if tile == 3:
                    lane = lax.broadcasted_iota(jnp.int32, (8, 128), 1)
                    value = jnp.where(lane < OWN * KD - 384, value, -3e38)
                best = value if best is None else jnp.maximum(best, value)
            best = jnp.broadcast_to(jnp.max(best, axis=1, keepdims=True), (8, 128))
            found[pl.ds(pl.multiple_of(step * 16 + block * 8, 8), 8), :] = best

    @pl.when(core[0] == 0)
    def _():
        score(kept, came)

    @pl.when(core[0] == 1)
    def _():
        score(came, kept)

    @pl.when(step == PD // 16 - 1)
    def _():
        out[...] = found[...].T[0:1, 0:PD]


def scores(core, kept, came, norm):
    return pl.pallas_call(
        score_kernel,
        grid_spec=pltpu.PrefetchScalarGridSpec(
            num_scalar_prefetch=1,
            grid=(PD // 16,),
            in_specs=[
                pl.BlockSpec((UNITS, 16, KPAD), lambda i, core: (0, i, 0)),
                pl.BlockSpec((UNITS, 16, KPAD), lambda i, core: (0, i, 0)),
                pl.BlockSpec((16, KPAD), lambda i, core: (i, 0)),
            ],
            out_specs=whole((1, PD)),
            scratch_shapes=[pltpu.VMEM((PD, 128), F32)],
        ),
        out_shape=jax.ShapeDtypeStruct((1, PD), F32),
        compiler_params=pltpu.CompilerParams(vmem_limit_bytes=VMEM_BYTES // 2),
        cost_estimate=pl.CostEstimate(
            flops=3000000000, bytes_accessed=9000000, transcendentals=0
        ),
        name="scores",
    )(core, kept, came, norm)


def class_sum_kernel(arrived, out, last):
    labels = arrived[:, 18 * PD : 19 * PD, :].astype(F32).reshape(DOM * PD, 128)
    block = labels[:, 16:17]
    local = labels[:, 17:18]
    row = jnp.where(local < 23.5, block * 24.0 + local, block + 384.0)
    lane = lax.broadcasted_iota(jnp.int32, (DOM * PD, KPAD), 1).astype(F32)
    hits = jnp.where(lane == row, 1.0, 0.0).T[0 : OWN * KD].astype(BF16)
    last[...] = jnp.zeros_like(last)
    for pair in range(10):
        pieces = [2 * pair, 2 * pair + 1] if pair < 9 else [18]
        right = jnp.concatenate(
            [arrived[:, c * PD : c * PD + PD, :].reshape(DOM * PD, 128) for c in pieces], axis=1
        )
        total = jnp.dot(hits, right, preferred_element_type=F32)
        sums = [total[:, i * 128 : i * 128 + 128] for i in range(len(pieces))]
        for place, value in zip(pieces, sums):
            last[pl.ds(24 + place, OWN, stride=48), :] = value[OWN * 24 :]
        if pair < 9:
            both = jnp.concatenate(
                [value[0 : OWN * 24].reshape(OWN, 24, 128) for value in sums], axis=1
            )
            out[:, pair * 48 : pair * 48 + 48, :] = both.astype(BF16)
        else:
            for owner in range(OWN):
                last[owner * 48 : owner * 48 + 24, :] = sums[0][owner * 24 : owner * 24 + 24]
    out[:, 432:480, :] = last[...].reshape(OWN, 48, 128).astype(BF16)


def class_sums(arrived):
    return pl.pallas_call(
        class_sum_kernel,
        in_specs=[pl.BlockSpec(memory_space=pltpu.VMEM)],
        out_specs=pl.BlockSpec(memory_space=pltpu.VMEM),
        scratch_shapes=[pltpu.VMEM((OWN * 48, 128), F32)],
        out_shape=jax.ShapeDtypeStruct((OWN, SROWS, 128), BF16),
        compiler_params=pltpu.CompilerParams(vmem_limit_bytes=VMEM_BYTES // 2),
        cost_estimate=pl.CostEstimate(
            flops=3000000000, bytes_accessed=9000000, transcendentals=0
        ),
        name="class_sums",
    )(arrived)


def average_kernel(dom, arrived, squares, out, left, middle, right):
    total = arrived[0].astype(F32)
    for source in range(1, OWN):
        total = total + arrived[source].astype(F32)
    counts = jnp.concatenate([total[432:456], total[472:480]], axis=0)
    below = jnp.dot(counts, squares[0], precision=lax.Precision.HIGHEST, preferred_element_type=F32)
    below = below + 1.0
    for cycle in range(BAND):
        usual = below[0:24, cycle : cycle + 1]
        final = below[26:27, cycle : cycle + 1]
        for tile, target in ((0, left), (1, middle), (2, right)):
            if tile < 2:
                piece, turn = cycle * 2 + tile, 0
            else:
                piece, turn = 16 + cycle // 4, (128 - cycle % 4 * 32) % 128
            value = total[piece * 24 : piece * 24 + 24] / usual
            end = total[456 + piece : 457 + piece] / final
            if turn:
                value = pltpu.roll(value, turn, 1)
                end = pltpu.roll(end, turn, 1)
            target[pl.ds(cycle, 24, stride=BAND), :] = value
            target[24 * BAND + cycle : 24 * BAND + cycle + 1, :] = end
    out[:, 0:128] = left[...]
    out[:, 128:256] = middle[...]
    out[:, 256:288] = right[:, 0:32]


def averages(dom, arrived):
    ctf = ctf_values()
    squares = np.zeros((DOM, 128, 128), np.float32)
    for band in range(DOM):
        squares[band, :NBINS, :BAND] = (ctf * ctf)[:, band * BAND : band * BAND + BAND]
    return pl.pallas_call(
        average_kernel,
        grid_spec=pltpu.PrefetchScalarGridSpec(
            num_scalar_prefetch=1,
            grid=(1,),
            in_specs=[
                whole((OWN, SROWS, 128)),
                pl.BlockSpec((1, 128, 128), lambda i, dom: (dom[0], 0, 0)),
            ],
            out_specs=whole((KD * BAND, ROW)),
            scratch_shapes=[pltpu.VMEM((KD * BAND, 128), F32)] * 3,
        ),
        out_shape=jax.ShapeDtypeStruct((KD * BAND, ROW), F32),
        compiler_params=pltpu.CompilerParams(vmem_limit_bytes=VMEM_BYTES // 2),
        cost_estimate=pl.CostEstimate(
            flops=2000000000, bytes_accessed=6000000, transcendentals=0
        ),
        name="averages",
    )(dom, arrived, jnp.asarray(squares))


def on_device(particles, references, class_block, class_local, rotation, shifts, defocus):
    dom = lax.axis_index("dom").astype(jnp.int32).reshape(1)
    core = dom % 2
    full_table, split_table = dft_rows()
    table = jnp.asarray(split_table)
    block = own_harmonics(core, references, table)
    scalars = jnp.stack(
        [shifts[:, 0], shifts[:, 1], defocus, rotation, class_block[:, 0], class_local], axis=0
    )
    rows = particles.reshape(PD * CYC, ROW)

    def spread_of(*blocks):
        *blocks, held = lax.optimization_barrier((*blocks, scalars))
        return *blocks, spread_bands(rows, held, full_table)

    gathered, joined, sums = gather_blocks(block, spread_of)
    late_scalars, _ = lax.optimization_barrier((scalars, joined))
    own, other = weighted_spectra(core, rows, late_scalars, table)
    swap = [(i, i ^ 1) for i in range(DOM)]
    far = lax.ppermute(other, "dom", swap)
    sums = lax.all_to_all(sums, "cls", 0, 0, tiled=True)
    class_average = averages(dom, sums).reshape(KD, BAND, ROW)
    kept, sent, norm = fold(core, gathered, own, far, defocus)
    came = lax.ppermute(sent, "dom", swap)
    best_score = scores(core, kept, came, norm).reshape(PD)
    return (best_score, class_average)


def solution(mesh):
    placed = (
        P(("dom", "cls"), None, None),
        P("cls", None, None),
        P(("dom", "cls"), None),
        P(("dom", "cls")),
        P(("dom", "cls")),
        P(("dom", "cls"), None),
        P(("dom", "cls")),
    )
    return jax.shard_map(
        on_device,
        mesh=mesh,
        in_specs=placed,
        out_specs=(P(("dom", "cls")), P("cls", "dom", None)),
        check_vma=False,
    )
```

```python
import functools
import math

import jax
import jax.numpy as jnp
import ml_dtypes
import numpy as np
from jax import lax
from jax.experimental import pallas as pl
from jax.experimental.pallas import tpu as pltpu
from jax.sharding import PartitionSpec as P

ROT = 36
BOX = 128
NBINS = 16
EPSILON = 1e-06
CYC = 64
ANG = 144
ROW = 2 * ANG
SHIFT = 5
PD = 48
KD = 25
OWN = 16
DOM = 8
BAND = CYC // DOM
UNITS = 18
HALF = UNITS // 2
MH = HALF * 8
HEAD = 192
NORM0 = 96
HROWS = HEAD + MH * 24
HH = 40
MP = 2 * HH
CHUNKS = 19
UROWS = CHUNKS * PD
SROWS = 480
KPAD = 512
STEP = 16
F32 = jnp.float32
BF16 = jnp.bfloat16
VMEM_BYTES = 58 * 1024 * 1024
NT = (((1,), (1,)), ((), ()))


def unit_harmonics():
    rows = []
    for unit in range(UNITS):
        plus, minus = (0, 18) if unit == 0 else (unit, ROT - unit)
        rows.append([plus + ROT * q for q in range(4)] + [minus + ROT * q for q in range(4)])
    return np.array(rows).reshape(2, MH)


def dft_rows():
    turn = np.arange(ANG)[:, None] * np.arange(ANG)[None, :] % ANG
    angle = turn.astype(np.float32) * np.float32(2.0 * math.pi / ANG)
    cosine = np.cos(angle.astype(np.float64))
    sine = np.sin(angle.astype(np.float64))
    upper = np.concatenate([cosine, -sine], axis=1)
    lower = np.concatenate([sine, cosine], axis=1)
    full = np.concatenate([upper, lower], axis=0).astype(np.float32).astype(ml_dtypes.bfloat16)
    halves = unit_harmonics()
    split = []
    for core in range(2):
        mine, other = halves[core], halves[1 - core]
        rows = np.zeros((4 * MP, ROW), ml_dtypes.bfloat16)
        for index, columns in enumerate((mine, ANG + mine, other, ANG + other)):
            for parity in range(2):
                start = index * MP + parity * HH
                rows[start : start + MH // 2] = full[:, columns[parity::2]].T
        split.append(rows)
    return full, np.stack(split)


def wide_columns(full):
    order = np.concatenate([np.arange(256)] + [np.arange(256, 288)] * 4)
    swapped = np.concatenate([-full[:, ANG:], full[:, :ANG]], axis=1)
    return np.concatenate([full[:, order], swapped[:, order]], axis=1), order


def turn_rows(order):
    harmonic = order % ANG
    turn = np.arange(ROT)[:, None] * 4 * harmonic[None, :] % ANG
    angle = turn * (2.0 * math.pi / ANG)
    angle = angle.reshape(ROT, 3, 128)
    rest = np.zeros((ROT, 2, 128))
    return np.concatenate([np.cos(angle), np.sin(angle), rest], axis=1).astype(np.float32)


def ctf_values():
    radius = (np.arange(CYC) + 1) / CYC
    level = np.arange(NBINS) / NBINS
    phase = math.pi * (3.0 + 9.0 * level[:, None]) * (radius * radius)[None, :]
    return 0.995 * np.sin(phase) + 0.1 * np.cos(phase)


def shift_rows():
    angle = np.arange(ANG) * (2.0 * math.pi / ANG)
    scale = 2.0 * math.pi / BOX * np.concatenate([np.arange(8), 8 * np.arange(8)])
    size = np.arange(SHIFT + 1)
    out = []
    for beam in (np.cos(angle), np.sin(angle)):
        phase = size[:, None, None] * scale[None, :, None] * beam[None, None, :]
        phase = np.concatenate([phase, phase], axis=2)
        out += [np.cos(phase), np.sin(phase)]
    return np.stack(out).astype(np.float32)


def swap_matrix():
    swap = np.zeros((ROW, ROW), np.float32)
    index = np.arange(ANG)
    swap[ANG + index, index] = -1.0
    swap[index, ANG + index] = 1.0
    return swap.astype(ml_dtypes.bfloat16)


def pair_signs():
    signs = np.zeros((2, 3, MH, 128), np.float32)
    for core in range(2):
        for row in range(MH):
            unit, place = core * HALF + row // 8, row % 8
            if unit == 0:
                signs[core, 0 if place < 4 else 1, row] = 1.0
            else:
                signs[core, 0, row] = 1.0
                flip = 1.0 if place < 4 else -1.0
                signs[core, 2, row, :64] = -flip
                signs[core, 2, row, 64:] = flip
    signs = np.pad(signs.transpose(0, 2, 1, 3), ((0, 0), (0, 0), (0, 5), (0, 0)))
    return signs


def whole(shape):
    return pl.BlockSpec(shape, lambda *_: (0,) * len(shape))


def merge_halves(real, imag, low):
    first = jnp.where(low, real, pltpu.roll(imag, 64, 1))
    second = jnp.where(low, pltpu.roll(real, 64, 1), imag)
    return first, second


def harmonics_kernel(
    core, refs_any, table_any, squares_any, out, refs, table, squares, scratch, energy, norms, sems
):
    copies = [pltpu.make_async_copy(table_any.at[core[0]], table, sems.at[0])]
    for index in range(4):
        chunk = pl.ds(index * 512, 512 if index < 3 else 64)
        copies.append(
            pltpu.make_async_copy(refs_any.at[chunk, :], refs.at[chunk, :], sems.at[index + 1])
        )
    copies.append(pltpu.make_async_copy(squares_any, squares, sems.at[5]))
    for copy in copies:
        copy.start()
    scratch[0:HEAD, :] = jnp.zeros((HEAD, 128), F32)
    energy[...] = jnp.zeros_like(energy)
    low = lax.broadcasted_iota(jnp.int32, (MP, 128), 1) < 64
    copies[0].wait()
    rows = table[...]

    def place(klass, value):
        if klass == 24:
            scratch[0:MP, :] = value
            return
        for parity in range(2):
            start = HEAD + (parity * 16 + klass if klass < 16 else 16 + parity * 8 + klass)
            piece = value[parity * HH : parity * HH + MH // 2]
            scratch[pl.ds(start, MH // 2, stride=48), :] = piece

    for group in range(7):
        start, width = (group * 256, 256) if group < 6 else (KD * CYC - 128, 128)
        if group % 2 == 0:
            copies[1 + group // 2].wait()
        full = lax.dot_general(rows, refs[start : start + width, :], NT, preferred_element_type=F32)
        kept = full.astype(BF16).astype(F32)
        total = jnp.sum(kept * kept, axis=0, keepdims=True)
        if group < 6:
            energy[group : group + 1, :] = total
        else:
            energy[group : group + 1, 0:128] = jnp.where(low[0:1], pltpu.roll(total, 64, 1), 0.0)
        for pair in range(width // 128):
            lanes = slice(pair * 128, pair * 128 + 128)
            first, second = merge_halves(full[0:MP, lanes], full[MP : 2 * MP, lanes], low)
            if group < 6:
                place(group * 4 + pair * 2, first)
                place(group * 4 + pair * 2 + 1, second)
            else:
                place(24, second)
    copies[5].wait()
    for sub in range(4):
        lanes = slice(sub // 2 * 128, sub // 2 * 128 + 128)
        power = jnp.dot(
            energy[:, lanes],
            squares[sub % 2],
            precision=lax.Precision.HIGHEST,
            preferred_element_type=F32,
        )
        norms[pl.ds(sub, 8, stride=4), :] = power
    scale = (1.0 / ANG) / jnp.sqrt(norms[...] * (1.0 / ANG) + EPSILON)
    scale = jnp.where(lax.broadcasted_iota(jnp.int32, (32, 128), 1) < NBINS, scale, 0.0)
    high = scale.astype(BF16).astype(F32)
    scratch[NORM0 : NORM0 + 32, :] = high + pltpu.roll(scale - high, NBINS, 1)
    out[...] = scratch[...].astype(BF16)


def own_harmonics(core, references, table):
    squares = np.zeros((2, 128, 128), np.float32)
    ctf = ctf_values()
    for sub in range(2):
        squares[sub, 64 * sub : 64 * sub + 64, :NBINS] = (ctf * ctf).T
    return pl.pallas_call(
        harmonics_kernel,
        in_specs=[
            pl.BlockSpec(memory_space=pltpu.SMEM),
            pl.BlockSpec(memory_space=pl.ANY),
            pl.BlockSpec(memory_space=pl.ANY),
            pl.BlockSpec(memory_space=pl.ANY),
        ],
        out_specs=pl.BlockSpec(memory_space=pltpu.VMEM),
        scratch_shapes=[
            pltpu.VMEM((KD * CYC, ROW), BF16),
            pltpu.VMEM((4 * MP, ROW), BF16),
            pltpu.VMEM((2, 128, 128), F32),
            pltpu.VMEM((HROWS, 128), F32),
            pltpu.VMEM((8, 256), F32),
            pltpu.VMEM((32, 128), F32),
            pltpu.SemaphoreType.DMA((6,)),
        ],
        out_shape=jax.ShapeDtypeStruct((HROWS, 128), BF16),
        compiler_params=pltpu.CompilerParams(vmem_limit_bytes=VMEM_BYTES),
        cost_estimate=pl.CostEstimate(
            flops=4000000000, bytes_accessed=12000000, transcendentals=0
        ),
        name="harmonics",
    )(core, references.reshape(KD * CYC, ROW), table, jnp.asarray(squares))


def shift_group(scalars, first, data, swap, phases):
    crossed = jnp.dot(data, swap, preferred_element_type=F32)
    shifted = []
    for sub in range(4):
        move_x = scalars[0, first + sub]
        move_y = scalars[1, first + sub]
        sign_x = jnp.where(move_x < 0, -1.0, 1.0)
        sign_y = jnp.where(move_y < 0, -1.0, 1.0)
        size_x = jnp.abs(move_x)
        size_y = jnp.abs(move_y)
        cos_x = phases[0, size_x]
        sin_x = phases[1, size_x] * sign_x
        cos_y = phases[2, size_y]
        sin_y = phases[3, size_y] * sign_y
        cosine = cos_x * cos_y - sin_x * sin_y
        sine = sin_x * cos_y + cos_x * sin_y
        near_cos, near_sin = cosine[0:8], sine[0:8]
        for jump in range(8):
            far_cos = cosine[8 + jump : 9 + jump]
            far_sin = sine[8 + jump : 9 + jump]
            rows = slice(sub * CYC + jump * 8, sub * CYC + jump * 8 + 8)
            value = data[rows].astype(F32) * (near_cos * far_cos - near_sin * far_sin)
            value = value + crossed[rows] * (near_sin * far_cos + near_cos * far_sin)
            shifted.append(value)
    return jnp.concatenate(shifted, axis=0).astype(BF16)


def spread_kernel(scalars, parts, wide, swap, phases, turn, ctf_columns, spread, turned, tails):
    step = pl.program_id(0)
    lane = lax.broadcasted_iota(jnp.int32, (1, 128), 1)
    group = lax.broadcasted_iota(jnp.int32, (16, 128), 1) // 32

    def one_group(quad, carry):
        first = step * STEP + quad * 4
        start = pl.multiple_of(quad * 256, 256)
        data = parts[pl.ds(start, 256), :]
        shifted = shift_group(scalars, first, data, swap[...], phases)
        natural = jnp.dot(shifted, wide[...], preferred_element_type=F32)
        for sub in range(4):
            index = first + sub
            rows = slice(sub * CYC, sub * CYC + CYC)
            angles = turn[scalars[3, index]]
            chosen = jnp.where(lane == scalars[2, index], ctf_columns[...], 0.0)
            contrast = jnp.sum(chosen, axis=1, keepdims=True)
            for tile in range(3):
                lanes = slice(tile * 128, tile * 128 + 128)
                cos_rot = angles[tile : tile + 1, :]
                sin_rot = angles[tile + 3 : tile + 4, :]
                there = slice(384 + tile * 128, 384 + tile * 128 + 128)
                value = natural[rows, lanes] * cos_rot + natural[rows, there] * sin_rot
                value = contrast * value
                if tile < 2:
                    for band in range(DOM):
                        begin = band * UROWS + tile * PD + index
                        piece = value[band * BAND : band * BAND + BAND]
                        turned[pl.ds(begin, BAND, stride=2 * PD), :] = piece
                else:
                    tails[sub] = value
                    packed = tails[sub, pl.ds(0, 16, stride=4), :]
                    for place in range(1, 4):
                        other = tails[sub, pl.ds(place, 16, stride=4), :]
                        packed = jnp.where(group == place, other, packed)
                    tails[sub, 0:16, :] = packed
                    for half in range(2):
                        piece = tails[sub, pl.ds(half, DOM, stride=2), :]
                        turned[pl.ds((16 + half) * PD + index, DOM, stride=UROWS), :] = piece
            label = jnp.where(lane == scalars[2, index], 1.0, 0.0)
            label = jnp.where(lane == 16, scalars[4, index].astype(F32), label)
            label = jnp.where(lane == 17, scalars[5, index].astype(F32), label)
            label = jnp.broadcast_to(label, (DOM, 128))
            turned[pl.ds(18 * PD + index, DOM, stride=UROWS), :] = label
        return carry

    lax.fori_loop(0, STEP // 4, one_group, 0, unroll=True)

    @pl.when(step == PD // STEP - 1)
    def _():
        spread[...] = turned[...].astype(BF16)


def spread_bands(particles, scalars, full_table):
    wide, order = wide_columns(full_table)
    ctf_columns = np.zeros((CYC, 128), np.float32)
    ctf_columns[:, :NBINS] = ctf_values().T
    return pl.pallas_call(
        spread_kernel,
        grid_spec=pltpu.PrefetchScalarGridSpec(
            num_scalar_prefetch=1,
            grid=(PD // STEP,),
            in_specs=[
                pl.BlockSpec((STEP * CYC, ROW), lambda i, sc: (i, 0)),
                whole((ROW, 768)),
                whole((ROW, ROW)),
                whole((4, SHIFT + 1, 16, ROW)),
                whole((ROT, 8, 128)),
                whole((CYC, 128)),
            ],
            out_specs=whole((DOM * UROWS, 128)),
            scratch_shapes=[
                pltpu.VMEM((DOM * UROWS, 128), F32),
                pltpu.VMEM((4, CYC, 128), F32),
            ],
        ),
        out_shape=jax.ShapeDtypeStruct((DOM * UROWS, 128), BF16),
        compiler_params=pltpu.CompilerParams(vmem_limit_bytes=VMEM_BYTES // 2),
        cost_estimate=pl.CostEstimate(
            flops=9000000000, bytes_accessed=27000000, transcendentals=0
        ),
        name="spread",
    )(
        scalars,
        particles,
        jnp.asarray(wide),
        jnp.asarray(swap_matrix()),
        jnp.asarray(shift_rows()),
        jnp.asarray(turn_rows(order)),
        jnp.asarray(ctf_columns),
    )


def weight_kernel(core, scalars, parts, table, swap, phases, ctf_rows, mine, other, weighted):
    step = pl.program_id(0)
    low = lax.broadcasted_iota(jnp.int32, (MP, 128), 1) < 64

    def one_group(quad, carry):
        first = step * STEP + quad * 4
        start = pl.multiple_of(quad * 256, 256)
        data = parts[pl.ds(start, 256), :]
        shifted = shift_group(scalars, first, data, swap[...], phases)
        full = lax.dot_general(table[0], shifted, NT, preferred_element_type=F32)
        for pair in range(2):
            lanes = slice(pair * 128, pair * 128 + 128)
            for side in range(2):
                base = side * 2 * MP
                both = merge_halves(
                    full[base : base + MP, lanes], full[base + MP : base + 2 * MP, lanes], low
                )
                for which in range(2):
                    index = first + pair * 2 + which
                    contrast = ctf_rows[pl.ds(scalars[2, index], 1), :]
                    value = both[which] * contrast
                    for parity in range(2):
                        begin = (side * MH + parity) * PD + index
                        piece = value[parity * HH : parity * HH + MH // 2]
                        weighted[pl.ds(begin, MH // 2, stride=2 * PD), :] = piece
        return carry

    lax.fori_loop(0, STEP // 4, one_group, 0, unroll=True)

    @pl.when(step == PD // STEP - 1)
    def _():
        mine[...] = weighted[0 : MH * PD, :].astype(BF16)
        other[...] = weighted[MH * PD :, :].astype(BF16)


def weighted_spectra(core, particles, scalars, table):
    ctf = ctf_values().astype(np.float32)
    half_shape = jax.ShapeDtypeStruct((MH * PD, 128), BF16)
    return pl.pallas_call(
        weight_kernel,
        grid_spec=pltpu.PrefetchScalarGridSpec(
            num_scalar_prefetch=2,
            grid=(PD // STEP,),
            in_specs=[
                pl.BlockSpec((STEP * CYC, ROW), lambda i, core, sc: (i, 0)),
                pl.BlockSpec((1, 4 * MP, ROW), lambda i, core, sc: (core[0], 0, 0)),
                whole((ROW, ROW)),
                whole((4, SHIFT + 1, 16, ROW)),
                whole((NBINS, 128)),
            ],
            out_specs=[whole((MH * PD, 128)), whole((MH * PD, 128))],
            scratch_shapes=[pltpu.VMEM((2 * MH * PD, 128), F32)],
        ),
        out_shape=[half_shape, half_shape],
        compiler_params=pltpu.CompilerParams(vmem_limit_bytes=VMEM_BYTES // 2),
        cost_estimate=pl.CostEstimate(
            flops=10000000000, bytes_accessed=30000000, transcendentals=0
        ),
        name="weights",
    )(
        core,
        scalars,
        particles,
        table,
        jnp.asarray(swap_matrix()),
        jnp.asarray(shift_rows()),
        jnp.asarray(np.concatenate([ctf, ctf], axis=1)),
    )


def fold_kernel(layout, count, core, *refs):
    pieces = refs[:count]
    own, far, signs, bins, kept_out, sent_out, norm = refs[count : count + 7]
    kept, sent, blocks, held, last, scale_rows, arrivals, leaving = refs[count + 7 :]
    copies = []
    for index, (slot, start, rows, first) in enumerate(layout):
        source = pieces[index].at[pl.ds(first, rows), :]
        target = blocks.at[slot, pl.ds(start, rows), :]
        copies.append(pltpu.make_async_copy(source, target, arrivals.at[index]))
    for copy in copies:
        copy.start()
    held[OWN * KD :, :] = jnp.zeros((KPAD - OWN * KD, 1024), BF16)
    scale_rows[...] = jnp.zeros_like(scale_rows)
    lane = lax.broadcasted_iota(jnp.int32, (PD, 128), 1)
    row = lax.broadcasted_iota(jnp.int32, (PD, 128), 0)
    level = jnp.zeros((PD, 128), jnp.int32)
    for index in range(PD):
        level = jnp.where(row == index, bins[index], level)
    hits = jnp.where((lane == level) | (lane == level + NBINS), 1.0, 0.0).astype(BF16)

    def outgoing(unit):
        both = pl.ds(2 * unit, 2)
        return (
            pltpu.make_async_copy(sent.at[both], sent_out.at[both], leaving.at[unit, 0]),
            pltpu.make_async_copy(kept.at[both], kept_out.at[both], leaving.at[unit, 1]),
        )

    def one_unit(unit, carry):
        parts_a, parts_b = [], []
        for place in range(8):
            harmonic = unit * 8 + place
            row = jnp.concatenate([own[harmonic], far[harmonic]], axis=0).astype(F32)
            factor = signs[core[0], harmonic]
            parts_a.append((row * factor[0:1]).astype(BF16))
            swapped = pltpu.roll(row, 64, 1) * factor[2:3]
            parts_b.append((row * factor[1:2] + swapped).astype(BF16))
        left = jnp.concatenate(
            [jnp.concatenate(parts_a, axis=1), jnp.concatenate(parts_b, axis=1)], axis=0
        )
        for pair in range(4):
            start = pl.multiple_of(HEAD + unit * 192 + pair * 48, 16)
            for parity in range(2):
                place = pair * 2 + parity
                lanes = slice(place * 128, place * 128 + 128)
                for slot in range(OWN):
                    held[slot * 16 : slot * 16 + 16, lanes] = blocks[
                        slot, pl.ds(start + parity * 16, 16), :
                    ]
                begin = pl.multiple_of((parity * HH + unit * 4 + pair) * OWN, OWN)
                held[OWN * 24 : OWN * KD, lanes] = last[pl.ds(begin, OWN), :].astype(BF16)
            for slot in range(0, OWN, 2):
                one = blocks[slot, pl.ds(start + 32, 16), :].astype(F32)
                two = blocks[slot + 1, pl.ds(start + 32, 16), :].astype(F32)
                for parity in range(2):
                    place = pair * 2 + parity
                    lanes = slice(place * 128, place * 128 + 128)
                    rows = slice(parity * 8, parity * 8 + 8)
                    both = jnp.concatenate([one[rows], two[rows]], axis=0).astype(BF16)
                    held[256 + slot * 8 : 256 + slot * 8 + 16, lanes] = both
        folded = lax.dot_general(left, held[...], NT, preferred_element_type=F32).astype(BF16)
        kept[2 * unit] = folded[0:PD]
        sent[2 * unit] = folded[PD : 2 * PD]
        kept[2 * unit + 1] = folded[2 * PD : 3 * PD]
        sent[2 * unit + 1] = folded[3 * PD : 4 * PD]
        for copy in outgoing(unit):
            copy.start()
        return carry

    for copy, (slot, start, rows, first) in zip(copies, layout):
        if start < HROWS // 2:
            copy.wait()
    for slot in range(OWN):
        last[pl.ds(slot, MP, stride=OWN), :] = blocks[slot, 0:MP, :].astype(F32)
        scales = blocks[slot, NORM0 : NORM0 + 32, :].astype(F32)
        scale_rows[slot * 16 : slot * 16 + 16, :] = scales[0:16]
        scale_rows[256 + slot * 8 : 256 + slot * 8 + 8, :] = scales[16:24]
        scale_rows[OWN * 24 + slot : OWN * 24 + slot + 1, :] = scales[24:25]
    table = scale_rows[...].astype(BF16)
    norm[...] = lax.dot_general(hits, table, NT, preferred_element_type=F32)
    lax.fori_loop(0, 4, one_unit, 0, unroll=True)
    for copy, (slot, start, rows, first) in zip(copies, layout):
        if start >= HROWS // 2:
            copy.wait()
    lax.fori_loop(4, HALF, one_unit, 0, unroll=True)
    for unit in range(HALF):
        for copy in outgoing(unit):
            copy.wait()


def fold(core, arrived, own, far, bins):
    layout = tuple((slot, start, rows, first) for slot, start, rows, first, _ in arrived)
    count = len(layout)
    piece = jax.ShapeDtypeStruct((UNITS, PD, KPAD), BF16)
    vmem = pl.BlockSpec(memory_space=pltpu.VMEM)
    return pl.pallas_call(
        functools.partial(fold_kernel, layout, count),
        in_specs=[pl.BlockSpec(memory_space=pltpu.SMEM)]
        + [pl.BlockSpec(memory_space=pl.ANY)] * count
        + [vmem] * 3
        + [pl.BlockSpec(memory_space=pltpu.SMEM)],
        out_specs=[pl.BlockSpec(memory_space=pl.ANY)] * 2 + [vmem],
        scratch_shapes=[
            pltpu.VMEM((UNITS, PD, KPAD), BF16),
            pltpu.VMEM((UNITS, PD, KPAD), BF16),
            pltpu.VMEM((OWN, HROWS, 128), BF16),
            pltpu.VMEM((KPAD, 1024), BF16),
            pltpu.VMEM((MP * OWN, 128), F32),
            pltpu.VMEM((KPAD, 128), F32),
            pltpu.SemaphoreType.DMA((count,)),
            pltpu.SemaphoreType.DMA((HALF, 2)),
        ],
        out_shape=[piece, piece, jax.ShapeDtypeStruct((PD, KPAD), F32)],
        compiler_params=pltpu.CompilerParams(vmem_limit_bytes=VMEM_BYTES),
        cost_estimate=pl.CostEstimate(
            flops=9000000000, bytes_accessed=27000000, transcendentals=0
        ),
        name="fold",
    )(
        core,
        *[value for *_, value in arrived],
        own.reshape(MH, PD, 128),
        far.reshape(MH, PD, 128),
        jnp.asarray(pair_signs()),
        bins,
    )


def moved_by(value, along_x, along_z):
    moves = [
        (x * 4 + z, (x + along_x) % 4 * 4 + (z + along_z) % 4) for x in range(4) for z in range(4)
    ]
    return lax.ppermute(value, "cls", moves)


def join_kernel(left, right, two_x, down, up, two_z, low, high, held, sems):
    half = HROWS // 2
    inward, outward = [], []
    for index, source in enumerate((left, right, two_x, down, up, two_z)):
        first = 0 if index < 3 else half
        target = (low if index < 3 else high).at[pl.ds(index % 3 * half, half), :]
        inward.append(
            pltpu.make_async_copy(source.at[pl.ds(first, half), :], held.at[index], sems.at[index])
        )
        outward.append(pltpu.make_async_copy(held.at[index], target, sems.at[6 + index]))
    for copy in inward:
        copy.start()
    for come, go in zip(inward, outward):
        come.wait()
        go.start()
    for copy in outward:
        copy.wait()


def join(*blocks):
    anywhere = pl.BlockSpec(memory_space=pl.ANY)
    rows = jax.ShapeDtypeStruct((3 * HROWS // 2, 128), BF16)
    return pl.pallas_call(
        join_kernel,
        in_specs=[anywhere] * 6,
        out_specs=[anywhere] * 2,
        scratch_shapes=[
            pltpu.VMEM((6, HROWS // 2, 128), BF16),
            pltpu.SemaphoreType.DMA((12,)),
        ],
        out_shape=[rows, rows],
        compiler_params=pltpu.CompilerParams(vmem_limit_bytes=VMEM_BYTES),
        cost_estimate=pl.CostEstimate(
            flops=2000000000, bytes_accessed=6000000, transcendentals=0
        ),
        name="join",
    )(*blocks)


def cut_kernel(low_before, low_after, high_before, high_after, *refs):
    outs, held, sems = refs[:4], refs[4], refs[5]
    part = 3 * HROWS // 4
    inward, outward = [], []
    for index, source in enumerate((low_before, low_after, high_before, high_after)):
        chunk = pl.ds(index % 2 * part, part)
        inward.append(pltpu.make_async_copy(source.at[chunk, :], held.at[index], sems.at[index]))
        outward.append(pltpu.make_async_copy(held.at[index], outs[index], sems.at[4 + index]))
    for copy in inward:
        copy.start()
    for come, go in zip(inward, outward):
        come.wait()
        go.start()
    for copy in outward:
        copy.wait()


def cut(*rows):
    anywhere = pl.BlockSpec(memory_space=pl.ANY)
    part = jax.ShapeDtypeStruct((3 * HROWS // 4, 128), BF16)
    return pl.pallas_call(
        cut_kernel,
        in_specs=[anywhere] * 4,
        out_specs=[anywhere] * 4,
        scratch_shapes=[
            pltpu.VMEM((4, 3 * HROWS // 4, 128), BF16),
            pltpu.SemaphoreType.DMA((8,)),
        ],
        out_shape=[part] * 4,
        compiler_params=pltpu.CompilerParams(vmem_limit_bytes=VMEM_BYTES),
        cost_estimate=pl.CostEstimate(
            flops=2000000000, bytes_accessed=6000000, transcendentals=0
        ),
        name="cut",
    )(*rows)


def gather_blocks(block, spread_of):
    half, part = HROWS // 2, 3 * HROWS // 4
    steps = (-1, 1, 2)
    by_x = [moved_by(block, -step, 0) for step in steps]
    by_z = [moved_by(block, 0, -step) for step in steps]
    by_x[2], spread = spread_of(by_x[2])
    low_rows, high_rows = join(*by_x, *by_z)
    low_far = [moved_by(low_rows, 0, 1), moved_by(low_rows, 0, -1)]
    high_far = [moved_by(high_rows, 1, 0), moved_by(high_rows, -1, 0)]
    arrived = lax.all_to_all(spread.reshape(DOM, UROWS, 128), "dom", 0, 0, tiled=True)
    sums = class_sums(arrived)
    low_far, high_far, sums = lax.optimization_barrier((low_far, high_far, sums))
    parts = cut(*low_far, *high_far)
    low_two = moved_by(parts[0], 0, 1), moved_by(parts[1], 0, -1)
    high_two = moved_by(parts[2], 1, 0), moved_by(parts[3], -1, 0)

    def slot(x, z):
        return x % 4 * 4 + z % 4

    pieces = []
    for start in (0, half):
        pieces.append((slot(0, 0), start, half, start, block))
        pieces += [(slot(step, 0), start, half, start, by_x[i]) for i, step in enumerate(steps)]
        pieces += [(slot(0, step), start, half, start, by_z[i]) for i, step in enumerate(steps)]
        near, two = (low_far, low_two) if start == 0 else (high_far, high_two)
        for j, inner in enumerate(steps):
            for i, outer in enumerate(steps[:2]):
                place = slot(inner, outer) if start == 0 else slot(outer, inner)
                pieces.append((place, start, half, j * half, near[i]))
            place = slot(inner, 2) if start == 0 else slot(2, inner)
            for i in range(2):
                first = max(j * half, i * part)
                last = min(j * half + half, i * part + part)
                if first < last:
                    begin = start + first - j * half
                    pieces.append((place, begin, last - first, first - i * part, two[i]))
    return pieces, low_rows, sums


def weigh(total, coefficient, value):
    if abs(coefficient) < 1e-12:
        return total
    if abs(coefficient - 1.0) < 1e-12:
        return value if total is None else total + value
    if abs(coefficient + 1.0) < 1e-12:
        return -value if total is None else total - value
    term = value * coefficient
    return term if total is None else total + term


def best_rotation(cosines, sines):
    best = None
    for parity in range(2):
        sign = 1.0 if parity == 0 else -1.0
        even = {0: cosines[0] + sign * cosines[18]}
        odd = {}
        for unit in range(1, 9):
            even[unit] = cosines[unit] + sign * cosines[18 - unit]
            odd[unit] = sines[unit] - sign * sines[18 - unit]
        even[9] = cosines[9]
        odd[9] = sines[9]
        for rotation in range(parity, 10, 2):
            sums = {}
            for name, values, wave in (("e", even, math.cos), ("o", odd, math.sin)):
                for rest in range(2):
                    total = None
                    for unit, value in values.items():
                        if unit % 2 == rest:
                            angle = math.pi * ((unit * rotation) % 36) / 18.0
                            total = weigh(total, wave(angle), value)
                    sums[name, rest] = total

            def joined(first, second, flip):
                if first is None and second is None:
                    return None
                if second is None:
                    return first
                if first is None:
                    return second
                return first - second if flip else first + second

            for flip in (False, True) if rotation < 9 else (False,):
                value = joined(sums["e", 0], sums["e", 1], flip)
                swing = joined(sums["o", 1], sums["o", 0], flip)
                if swing is not None:
                    value = value + jnp.abs(swing)
                best = value if best is None else jnp.maximum(best, value)
    return best


def score_kernel(core, kept, came, norm, out, found):
    step = pl.program_id(0)

    def score(low, high):
        for block in range(2):
            rows = slice(block * 8, block * 8 + 8)
            every = slice(0, 16)
            best = None
            for tile in range(KPAD // 128):
                lanes = slice(tile * 128, tile * 128 + 128)
                cosines, sines = {}, {}
                for unit in range(UNITS):
                    source = low if unit < HALF else high
                    place = unit % HALF * 2
                    cosines[unit] = source[place, every, lanes].astype(F32)[rows]
                    sines[unit] = source[place + 1, every, lanes].astype(F32)[rows]
                cosines[18] = sines[0]
                value = best_rotation(cosines, sines) * norm[rows, lanes]
                if tile == 3:
                    lane = lax.broadcasted_iota(jnp.int32, (8, 128), 1)
                    value = jnp.where(lane < OWN * KD - 384, value, -3e38)
                best = value if best is None else jnp.maximum(best, value)
            best = jnp.broadcast_to(jnp.max(best, axis=1, keepdims=True), (8, 128))
            found[pl.ds(pl.multiple_of(step * 16 + block * 8, 8), 8), :] = best

    @pl.when(core[0] == 0)
    def _():
        score(kept, came)

    @pl.when(core[0] == 1)
    def _():
        score(came, kept)

    @pl.when(step == PD // 16 - 1)
    def _():
        out[...] = found[...].T[0:1, 0:PD]


def scores(core, kept, came, norm):
    return pl.pallas_call(
        score_kernel,
        grid_spec=pltpu.PrefetchScalarGridSpec(
            num_scalar_prefetch=1,
            grid=(PD // 16,),
            in_specs=[
                pl.BlockSpec((UNITS, 16, KPAD), lambda i, core: (0, i, 0)),
                pl.BlockSpec((UNITS, 16, KPAD), lambda i, core: (0, i, 0)),
                pl.BlockSpec((16, KPAD), lambda i, core: (i, 0)),
            ],
            out_specs=whole((1, PD)),
            scratch_shapes=[pltpu.VMEM((PD, 128), F32)],
        ),
        out_shape=jax.ShapeDtypeStruct((1, PD), F32),
        compiler_params=pltpu.CompilerParams(vmem_limit_bytes=VMEM_BYTES // 2),
        cost_estimate=pl.CostEstimate(
            flops=3000000000, bytes_accessed=9000000, transcendentals=0
        ),
        name="scores",
    )(core, kept, came, norm)


def class_sum_kernel(arrived, out, last):
    labels = arrived[:, 18 * PD : 19 * PD, :].astype(F32).reshape(DOM * PD, 128)
    block = labels[:, 16:17]
    local = labels[:, 17:18]
    row = jnp.where(local < 23.5, block * 24.0 + local, block + 384.0)
    lane = lax.broadcasted_iota(jnp.int32, (DOM * PD, KPAD), 1).astype(F32)
    hits = jnp.where(lane == row, 1.0, 0.0).T[0 : OWN * KD].astype(BF16)
    last[...] = jnp.zeros_like(last)
    for pair in range(10):
        pieces = [2 * pair, 2 * pair + 1] if pair < 9 else [18]
        right = jnp.concatenate(
            [arrived[:, c * PD : c * PD + PD, :].reshape(DOM * PD, 128) for c in pieces], axis=1
        )
        total = jnp.dot(hits, right, preferred_element_type=F32)
        sums = [total[:, i * 128 : i * 128 + 128] for i in range(len(pieces))]
        for place, value in zip(pieces, sums):
            last[pl.ds(24 + place, OWN, stride=48), :] = value[OWN * 24 :]
        if pair < 9:
            both = jnp.concatenate(
                [value[0 : OWN * 24].reshape(OWN, 24, 128) for value in sums], axis=1
            )
            out[:, pair * 48 : pair * 48 + 48, :] = both.astype(BF16)
        else:
            for owner in range(OWN):
                last[owner * 48 : owner * 48 + 24, :] = sums[0][owner * 24 : owner * 24 + 24]
    out[:, 432:480, :] = last[...].reshape(OWN, 48, 128).astype(BF16)


def class_sums(arrived):
    return pl.pallas_call(
        class_sum_kernel,
        in_specs=[pl.BlockSpec(memory_space=pltpu.VMEM)],
        out_specs=pl.BlockSpec(memory_space=pltpu.VMEM),
        scratch_shapes=[pltpu.VMEM((OWN * 48, 128), F32)],
        out_shape=jax.ShapeDtypeStruct((OWN, SROWS, 128), BF16),
        compiler_params=pltpu.CompilerParams(vmem_limit_bytes=VMEM_BYTES // 2),
        cost_estimate=pl.CostEstimate(
            flops=3000000000, bytes_accessed=9000000, transcendentals=0
        ),
        name="class_sums",
    )(arrived)


def average_kernel(dom, arrived, squares, out, left, middle, right):
    total = arrived[0].astype(F32)
    for source in range(1, OWN):
        total = total + arrived[source].astype(F32)
    counts = jnp.concatenate([total[432:456], total[472:480]], axis=0)
    below = jnp.dot(counts, squares[0], precision=lax.Precision.HIGHEST, preferred_element_type=F32)
    below = below + 1.0
    for cycle in range(BAND):
        usual = below[0:24, cycle : cycle + 1]
        final = below[26:27, cycle : cycle + 1]
        for tile, target in ((0, left), (1, middle), (2, right)):
            if tile < 2:
                piece, turn = cycle * 2 + tile, 0
            else:
                piece, turn = 16 + cycle // 4, (128 - cycle % 4 * 32) % 128
            value = total[piece * 24 : piece * 24 + 24] / usual
            end = total[456 + piece : 457 + piece] / final
            if turn:
                value = pltpu.roll(value, turn, 1)
                end = pltpu.roll(end, turn, 1)
            target[pl.ds(cycle, 24, stride=BAND), :] = value
            target[24 * BAND + cycle : 24 * BAND + cycle + 1, :] = end
    out[:, 0:128] = left[...]
    out[:, 128:256] = middle[...]
    out[:, 256:288] = right[:, 0:32]


def averages(dom, arrived):
    ctf = ctf_values()
    squares = np.zeros((DOM, 128, 128), np.float32)
    for band in range(DOM):
        squares[band, :NBINS, :BAND] = (ctf * ctf)[:, band * BAND : band * BAND + BAND]
    return pl.pallas_call(
        average_kernel,
        grid_spec=pltpu.PrefetchScalarGridSpec(
            num_scalar_prefetch=1,
            grid=(1,),
            in_specs=[
                whole((OWN, SROWS, 128)),
                pl.BlockSpec((1, 128, 128), lambda i, dom: (dom[0], 0, 0)),
            ],
            out_specs=whole((KD * BAND, ROW)),
            scratch_shapes=[pltpu.VMEM((KD * BAND, 128), F32)] * 3,
        ),
        out_shape=jax.ShapeDtypeStruct((KD * BAND, ROW), F32),
        compiler_params=pltpu.CompilerParams(vmem_limit_bytes=VMEM_BYTES // 2),
        cost_estimate=pl.CostEstimate(
            flops=2000000000, bytes_accessed=6000000, transcendentals=0
        ),
        name="averages",
    )(dom, arrived, jnp.asarray(squares))


def on_device(particles, references, class_block, class_local, rotation, shifts, defocus):
    dom = lax.axis_index("dom").astype(jnp.int32).reshape(1)
    core = dom % 2
    full_table, split_table = dft_rows()
    table = jnp.asarray(split_table)
    block = own_harmonics(core, references, table)
    scalars = jnp.stack(
        [shifts[:, 0], shifts[:, 1], defocus, rotation, class_block[:, 0], class_local], axis=0
    )
    rows = particles.reshape(PD * CYC, ROW)

    def spread_of(*blocks):
        *blocks, held = lax.optimization_barrier((*blocks, scalars))
        return *blocks, spread_bands(rows, held, full_table)

    gathered, joined, sums = gather_blocks(block, spread_of)
    late_scalars, _ = lax.optimization_barrier((scalars, joined))
    own, other = weighted_spectra(core, rows, late_scalars, table)
    swap = [(i, i ^ 1) for i in range(DOM)]
    far = lax.ppermute(other, "dom", swap)
    sums = lax.all_to_all(sums, "cls", 0, 0, tiled=True)
    class_average = averages(dom, sums).reshape(KD, BAND, ROW)
    kept, sent, norm = fold(core, gathered, own, far, defocus)
    came = lax.ppermute(sent, "dom", swap)
    came, class_average = lax.optimization_barrier((came, class_average))
    best_score = scores(core, kept, came, norm).reshape(PD)
    return (best_score, class_average)


def solution(mesh):
    placed = (
        P(("dom", "cls"), None, None),
        P("cls", None, None),
        P(("dom", "cls"), None),
        P(("dom", "cls")),
        P(("dom", "cls")),
        P(("dom", "cls"), None),
        P(("dom", "cls")),
    )
    return jax.shard_map(
        on_device,
        mesh=mesh,
        in_specs=placed,
        out_specs=(P(("dom", "cls")), P("cls", "dom", None)),
        check_vma=False,
    )
```
